512 devices in a mesh: gx: 16 (over y_lo, x), gy: 8 (over z), gz: 4 (over y_hi, core).
Axes of the slice: x: 4, y: 8 (y_hi: 2, y_lo: 4; y = y_hi * 4 + y_lo), z: 8, core: 2. Of those that a mesh axis runs over, the one named last changes fastest.
Arguments:
- camera: bfloat16 [6, 512, 128, 256], P(None, 'gx', ('gy', 'gz')), may hold values from 0.19921875 to 3
- initial: float32 [256, 128, 512], P('gx', 'gy', 'gz'), may hold values from 0.5 to 2
- psf_taps: float32 [6, 3, 31], replicated, may hold values from 0.05 to 1
Outputs:
- deconvolved: float32 [256, 128, 512], P('gx', 'gy', 'gz')
The draws below stay inside these ranges and needn't reach their ends.
All inputs are finite; a program needn't handle non-finite values.
Results may differ from the reference program's by a relative error of at most 0.0006.
Values may be sent and summed in bfloat16 or wider, within the bound.
A program may use at most 64 MiB of HBM per device.

```python
import math
import jax
import jax.numpy as jnp
from jax import lax

VIEWS = 6
TAPS = 31
ITERS = 2
NX = 256
NY = 128
NZ = 512


def levels(stream_key, extent, pieces, least, top_value):
    def one(position, blocks):
        steps = jax.random.uniform(jax.random.fold_in(jax.random.fold_in(stream_key, 6), position), (blocks,), jnp.float32, least / len(pieces), top_value / len(pieces))
        return jnp.repeat(jnp.exp(steps), extent[position] // blocks).reshape((-1,) + (1,) * (len(extent) - position - 1))

    loudness = one(*pieces[0])
    for cut in pieces[1:]:
        loudness = loudness * one(*cut)
    return loudness


def setup_inputs(seed: int = 0) -> dict:
    keys = jax.random.split(jax.random.key(seed), 4)
    return {
        "camera": jnp.clip(0.19921875 + 2.8007812 * jax.random.uniform(keys[0], (VIEWS, NZ, NY, NX), jnp.float32) ** levels(keys[0], (VIEWS, NZ, NY, NX), ((1, 16), (2, 32)), -0.2, 0.2), 0.19921875, 3.0).astype(jnp.bfloat16),
        "initial": jnp.clip(0.5 + 1.5 * jax.random.uniform(keys[1], (NX, NY, NZ), jnp.float32) ** levels(keys[1], (NX, NY, NZ), ((0, 16), (1, 8), (2, 4)), -0.2, 0.2), 0.5, 2.0),
        "psf_taps": jnp.clip(jnp.exp(jax.random.uniform(keys[2], (VIEWS, 3, TAPS), jnp.float32, math.log(0.05), math.log(1.0))), 0.05, 1.0),
    }


def one_pass(volume, kernel, which_axis, backward):
    half = TAPS // 2
    widths = [(0, 0), (0, 0), (0, 0)]
    widths[which_axis] = (half, half)
    padded = jnp.pad(volume, widths)
    length = volume.shape[which_axis]
    summed = jnp.zeros(volume.shape, jnp.float32)
    for tap in range(TAPS):
        offset = tap if backward else 2 * half - tap
        summed = summed + kernel[tap] * lax.slice_in_dim(padded, offset, offset + length, axis=which_axis)
    return summed


def reference(camera, initial, psf_taps):
    kernels = psf_taps / jnp.sum(psf_taps, axis=-1, keepdims=True)
    back_kernels = lax.optimization_barrier(kernels.astype(jnp.bfloat16)).astype(jnp.float32)
    estimate = initial

    for sweep in range(ITERS):
        def per_view(summed, triple):
            recorded, kernel, back_kernel = triple
            blurred = one_pass(estimate, kernel[2], 2, False)
            blurred = one_pass(blurred, kernel[1], 1, False)
            blurred = one_pass(blurred, kernel[0], 0, False)
            planes = jnp.transpose(recorded, (2, 1, 0))
            quotient = (planes.astype(jnp.float32) / blurred).astype(jnp.bfloat16)
            third = one_pass(quotient.astype(jnp.float32), back_kernel[2], 2, True).astype(jnp.bfloat16)
            second = one_pass(third.astype(jnp.float32), back_kernel[1], 1, True).astype(jnp.bfloat16)
            correction = one_pass(second.astype(jnp.float32), back_kernel[0], 0, True)
            return summed + correction, None

        summed, unused = lax.scan(per_view, jnp.zeros(estimate.shape, jnp.float32), (camera, kernels, back_kernels))
        estimate = estimate * summed / VIEWS
    return estimate
```

```python
import functools

import jax
import jax.numpy as jnp
from jax import lax
from jax.experimental import pallas as pl
from jax.experimental.pallas import tpu as pltpu
from jax.sharding import PartitionSpec as P

VIEWS = 6
TAPS = 31
HALF = TAPS // 2
ITERS = 2
F32 = jnp.float32
BF16 = jnp.bfloat16
MESH = pl.DeviceIdType.MESH


def dot(a, b):
    return jnp.dot(a, b, preferred_element_type=F32)


def iota(shape, dim):
    return lax.broadcasted_iota(jnp.int32, shape, dim)


def pick(table, index):
    index = jnp.where((index >= 0) & (index < TAPS), index, 127)
    return jnp.take_along_axis(table, index, axis=1)


def kernel(
    sizes, cam_ref, init_ref, taps_ref, out_ref,
    est, ext, quot, ubuf, kf, kb, bzf, bzb, raw, back, xf, yf, xb, yb, scale,
    picked, place, cam_out, cam_in, cam, third, part, flat, acc, code_out, code_in,
    cam_send, cam_recv, z_send, z_recv, e_send, e_recv, h_send, h_recv,
    q_send, q_recv, c_send, c_recv,
):
    nx, ny, nz = sizes
    gx, gy, gz = lax.axis_index("gx"), lax.axis_index("gy"), lax.axis_index("gz")

    def place_of(n):
        return gx + n // 3 - 1, gy + n % 3 - 1, gz

    def there(n):
        x, y, _ = place_of(n)
        return (x >= 0) & (x < nx) & (y >= 0) & (y < ny)

    def around(body):
        def step(i, carry):
            n = jnp.where(i >= 4, i + 1, i)

            @pl.when(there(n))
            def _():
                body(n)

            return carry

        lax.fori_loop(0, 8, step, 0)

    below, above = gz > 0, gz < nz - 1

    def camera_source(s):
        return 4 * gz + s // 4, gy, s % 4

    def camera_target(a):
        return a, gy, gx // 4

    def is_self(place):
        return (place[0] == gx) & (place[2] == gz)

    own_source = gx // 4 == gz
    barrier = pltpu.get_barrier_semaphore()

    def greet(place):
        pl.semaphore_signal(barrier, inc=1, device_id=place, device_id_type=MESH)

    around(lambda n: greet(place_of(n)))

    @pl.when(below)
    def _():
        greet((gx, gy, gz - 1))

    @pl.when(above)
    def _():
        greet((gx, gy, gz + 1))

    def greet_source(s, carry):
        @pl.when(jnp.logical_not(is_self(camera_source(s))))
        def _():
            greet(camera_source(s))

        return carry

    lax.fori_loop(0, 16, greet_source, 0)

    def clear(i, carry):
        n = jnp.where(i >= 4, i + 1, i)

        @pl.when(jnp.logical_not(there(n)))
        def _():
            lanes = pl.ds(pl.multiple_of(n * 256, 256), 256)
            for it in range(ITERS):
                ext[it, :, lanes] = jnp.zeros((160, 256), BF16)

        return carry

    lax.fori_loop(0, 8, clear, 0)
    for it in range(ITERS):
        @pl.when(jnp.logical_not(below))
        def _():
            ext[it, 128:144, 1024:1280] = jnp.zeros((16, 256), BF16)
            quot[it, :, 128:144, :] = jnp.zeros((VIEWS, 16, 256), BF16)

        @pl.when(jnp.logical_not(above))
        def _():
            ext[it, 144:160, 1024:1280] = jnp.zeros((16, 256), BF16)
            quot[it, :, 144:160, :] = jnp.zeros((VIEWS, 16, 256), BF16)

        quot[it, :, 160:256, :] = jnp.zeros((VIEWS, 96, 256), BF16)
    ubuf[160:256, :] = jnp.zeros((96, 256), BF16)
    ubuf[416:512, :] = jnp.zeros((96, 256), BF16)

    for y in range(16):
        flat[y * 16 : (y + 1) * 16, :] = init_ref[pl.ds(y, 16, stride=16), :]
    est[...] = flat[...].T
    ext[0, 0:128, 1024:1280] = est[...].astype(BF16)

    neighbours = jnp.int32(0)
    for n in range(9):
        if n != 4:
            neighbours += there(n).astype(jnp.int32)
    neighbours += below.astype(jnp.int32) + above.astype(jnp.int32)
    pl.semaphore_wait(barrier, neighbours + 16 - own_source.astype(jnp.int32))

    def ext_lanes(n):
        return pl.ds(pl.multiple_of(n * 256, 256), 256)

    def z_copy(it, up):
        source = 112 if up else 0
        target = 128 if up else 144
        return pltpu.make_async_remote_copy(
            src_ref=ext.at[it, pl.ds(source, 16), pl.ds(1024, 256)],
            dst_ref=ext.at[it, pl.ds(target, 16), pl.ds(1024, 256)],
            send_sem=z_send.at[it, int(up)],
            recv_sem=z_recv.at[it, int(up)],
            device_id=(gx, gy, gz + 1 if up else gz - 1),
            device_id_type=MESH,
        )

    def e_copy(it, n, slot, first, count, sends, recvs):
        return pltpu.make_async_remote_copy(
            src_ref=ext.at[it, pl.ds(first, count), pl.ds(1024, 256)],
            dst_ref=ext.at[it, pl.ds(first, count), ext_lanes(slot)],
            send_sem=sends.at[it, n],
            recv_sem=recvs.at[it, slot],
            device_id=place_of(n),
            device_id_type=MESH,
        )

    def main_copy(it, n, slot):
        return e_copy(it, n, slot, 0, 128, e_send, e_recv)

    def rim_copy(it, n, slot):
        return e_copy(it, n, slot, 128, 32, h_send, h_recv)

    def q_copy(it, up):
        source = 112 if up else 0
        target = 128 if up else 144
        return pltpu.make_async_remote_copy(
            src_ref=quot.at[it, :, pl.ds(source, 16), :],
            dst_ref=quot.at[it, :, pl.ds(target, 16), :],
            send_sem=q_send.at[it, int(up)],
            recv_sem=q_recv.at[it, int(up)],
            device_id=(gx, gy, gz + 1 if up else gz - 1),
            device_id_type=MESH,
        )

    def c_copy(it, n, slot):
        return pltpu.make_async_remote_copy(
            src_ref=code_out.at[it, n],
            dst_ref=code_in.at[it, slot],
            send_sem=c_send.at[it, n],
            recv_sem=c_recv.at[it, slot],
            device_id=place_of(n),
            device_id_type=MESH,
        )

    def both(make, act):
        @pl.when(above)
        def _():
            act(make(True))

        @pl.when(below)
        def _():
            act(make(False))

    def both_in(make):
        @pl.when(below)
        def _():
            make(True).wait_recv()

        @pl.when(above)
        def _():
            make(False).wait_recv()

    def start(copy):
        copy.start()

    def send_estimate(it):
        both(lambda up: z_copy(it, up), start)
        around(lambda n: main_copy(it, n, 8 - n).start())

    send_estimate(0)

    place[...] = jnp.zeros(place.shape, BF16)
    row, col = iota((32, 256), 0), iota((32, 256), 1)
    same_x = row == (col >> 7) * 16 + (col & 15)
    for r in range(2):
        turned = ((col >> 6) & 1) == (r + gz) % 2
        for y in range(4):
            ones = (same_x & turned & (((col >> 4) & 3) == y)).astype(F32).astype(BF16)
            for q in range(4):
                first = (r * 4 + y) * 128 + q * 32
                place[q, first : first + 32, :] = ones
    for v in range(VIEWS):
        r, w = v // 3, v % 3
        for y in range(4):
            plane = cam_ref[v, :, y, :]
            for h in range(2):
                picked[h, w * 32 : (w + 1) * 32, (r * 4 + y) * 128 : (r * 4 + y + 1) * 128] = plane[
                    :, h * 128 : (h + 1) * 128
                ]
    for p in range(8):
        block = dot(picked[p // 4], place[p % 4]).astype(BF16)
        cam_out[2 * p] = block[:, 0:128]
        cam_out[2 * p + 1] = block[:, 128:256]

    slot = (gx % 4) * 4 + gz

    def cam_copy(a, s):
        return pltpu.make_async_remote_copy(
            src_ref=cam_out.at[a],
            dst_ref=cam_in.at[s],
            send_sem=cam_send.at[a],
            recv_sem=cam_recv.at[s],
            device_id=camera_target(a),
            device_id_type=MESH,
        )

    def send_camera(a, carry):
        mine = is_self(camera_target(a))

        @pl.when(mine)
        def _():
            cam_in[slot] = cam_out[a]

        @pl.when(jnp.logical_not(mine))
        def _():
            cam_copy(a, slot).start()

        return carry

    lax.fori_loop(0, 16, send_camera, 0)

    raw[...] = jnp.zeros((24, 128), F32)
    for v in range(VIEWS):
        for a in range(3):
            raw[a * 8 + v : a * 8 + v + 1, 0:TAPS] = taps_ref[v, a : a + 1, :]
    total = jnp.sum(raw[...], axis=1, keepdims=True)
    total = jnp.where((iota((24, 1), 0) & 7) < VIEWS, total, 1.0)
    back[...] = (raw[...] / total).astype(BF16).astype(F32)
    fx, fy, fz = raw[0:8, :], raw[8:16, :], raw[16:24, :]
    bx, by = back[0:8, :], back[8:16, :]
    f_sum, b_sum = jnp.zeros((8, 128), F32), jnp.zeros((8, 128), F32)
    for t in range(TAPS):
        f_sum += (fx[:, t : t + 1] * fy).astype(BF16).astype(F32)
        b_sum += (bx[:, t : t + 1] * by).astype(BF16).astype(F32)

    def lanes_sum(a):
        return jnp.sum(a, axis=1, keepdims=True)

    f_scale = lanes_sum(f_sum) * lanes_sum(fz.astype(BF16).astype(F32))
    b_scale = lanes_sum(bx) * lanes_sum(by) / jnp.where(iota((8, 1), 0) < VIEWS, lanes_sum(b_sum), 1.0)
    scale[0:8, :] = jnp.broadcast_to(f_scale, (8, 128))
    scale[8:16, :] = jnp.broadcast_to(b_scale, (8, 128))

    def tables(j, carry):
        rows = pl.ds(pl.multiple_of(j * 8, 8), 8)
        lane = iota((8, 128), 1)
        x = lane & 15
        xf[rows, :] = pick(raw[0:8, :], x + 31 - j)
        xb[rows, :] = pick(back[0:8, :], j - 1 - x)
        for half in range(2):
            y = (lane >> 4) + 8 * half
            lanes = slice(half * 128, (half + 1) * 128)
            yf[rows, lanes] = pick(raw[8:16, :], y + 31 - j)
            yb[rows, lanes] = pick(back[8:16, :], j - 1 - y)
        return carry

    lax.fori_loop(0, 48, tables, 0)

    def products(i, carry):
        v, n = i // 9, i % 9
        dx, dy = n // 3, n % 3
        x_f = xf[pl.ds(dx * 128 + v, 16, stride=8), :]
        x_b = xb[pl.ds((2 - dx) * 128 + v, 16, stride=8), :]
        for y in range(16):
            y_f = yf[pl.ds((dy * 16 + y) * 8 + v, 1), :]
            y_b = yb[pl.ds(((2 - dy) * 16 + y) * 8 + v, 1), :]
            for half in range(2):
                lanes = slice(half * 128, (half + 1) * 128)
                kf[v, pl.ds(pl.multiple_of(n * 256 + y * 16, 16), 16), lanes] = (
                    x_f * y_f[:, lanes]
                ).astype(BF16)
                kb[n, pl.ds(pl.multiple_of(v * 256 + y * 16, 16), 16), lanes] = (
                    x_b * y_b[:, lanes]
                ).astype(BF16)
        return carry

    lax.fori_loop(0, 9 * VIEWS, products, 0)

    def band_block(i, carry):
        v, block = i // 8, i % 8
        rows = pl.ds(pl.multiple_of(block * 16, 16), 16)
        lane = iota((8, 128), 1)
        far = jnp.where(lane < 16, lane - 16, jnp.where(lane < 32, lane + 112, 1024))
        f_row = jnp.broadcast_to(raw[pl.ds(16 + v, 1), :], (8, 128))
        b_row = jnp.broadcast_to(back[pl.ds(16 + v, 1), :], (8, 128))
        for half, z_in in enumerate((lane, far)):
            lanes = slice(half * 128, (half + 1) * 128)
            forward, backward = [], []
            for k in range(2):
                apart = iota((8, 128), 0) + block * 16 + k * 8 - z_in
                forward.append(pick(f_row, apart + HALF))
                backward.append(pick(b_row, HALF - apart))
            bzf[v, rows, lanes] = jnp.concatenate(forward, axis=0).astype(BF16)
            bzb[v, rows, lanes] = jnp.concatenate(backward, axis=0).astype(BF16)
        return carry

    lax.fori_loop(0, 8 * VIEWS, band_block, 0)

    def receive_camera():
        def wait(s, carry):
            @pl.when(jnp.logical_not(is_self(camera_source(s))))
            def _():
                cam_copy(0, s).wait_recv()

            return carry

        lax.fori_loop(0, 16, wait, 0)
        low = iota((32, 128), 1) < 64
        for v in range(VIEWS):
            r, w = v // 3, v % 3
            for z in range(4):
                for t in range(2):
                    even = cam_in[z * 4 + 2 * t, w * 32 : (w + 1) * 32, :].astype(F32)
                    odd = cam_in[z * 4 + 2 * t + 1, w * 32 : (w + 1) * 32, :].astype(F32)
                    if r == 0:
                        block = jnp.where(low, even, odd)
                    else:
                        block = pltpu.roll(jnp.where(low, odd, even), 64, 1)
                    cam[v, z * 32 : (z + 1) * 32, t * 128 : (t + 1) * 128] = block.astype(BF16)

    def sweep(it, carry):
        both_in(lambda up: z_copy(it, up))
        around(lambda n: rim_copy(it, n, 8 - n).start())
        around(lambda n: main_copy(it, n, n).wait_recv())
        around(lambda n: rim_copy(it, n, n).wait_recv())

        @pl.when(it == 0)
        def _():
            receive_camera()

        def forward(v, carry):
            u = dot(ext[it], kf[v])
            high = u.astype(BF16)
            ubuf[0:160, :] = high
            ubuf[256:416, :] = (u - high.astype(F32)).astype(BF16)
            band = bzf[v]
            blurred = dot(jnp.concatenate([band, band], axis=1), ubuf[...])
            factor = scale[pl.ds(v, 1), :]
            factor = jnp.concatenate([factor, factor], axis=1)
            quot[it, v, 0:128, :] = (cam[v].astype(F32) * factor / blurred).astype(BF16)
            return carry

        lax.fori_loop(0, VIEWS, forward, 0)
        both(lambda up: q_copy(it, up), start)
        both_in(lambda up: q_copy(it, up))
        for v in range(VIEWS):
            factor = scale[8 + v : 9 + v, :]
            factor = jnp.concatenate([factor, factor], axis=1)
            third[:, v * 256 : (v + 1) * 256] = (dot(bzb[v], quot[it, v]) * factor).astype(BF16)

        def backward(i, carry):
            n = jnp.where(i >= 4, i + 1, i)

            @pl.when(there(n))
            def _():
                part[0:128, :] = dot(third[...], kb[n])
                base = jnp.concatenate(
                    [part[g * 16 + 8 : g * 16 + 9, :] for g in range(8)], axis=0
                ).astype(BF16).astype(F32)
                code_out[it, n, 128:144, :] = jnp.concatenate(
                    [base, jnp.zeros((8, 256), F32)], axis=0
                ).astype(BF16)
                for g in range(8):
                    rows = slice(g * 16, (g + 1) * 16)
                    code_out[it, n, rows, :] = (part[rows, :] - base[g : g + 1, :]).astype(BF16)
                c_copy(it, n, 8 - n).start()

            return carry

        lax.fori_loop(0, 8, backward, 0)
        acc[...] = dot(third[...], kb[4])

        def collect(n):
            c_copy(it, n, n).wait_recv()
            base = code_in[it, n, 128:144, :].astype(F32)
            for g in range(8):
                rows = slice(g * 16, (g + 1) * 16)
                acc[rows, :] += code_in[it, n, rows, :].astype(F32) + base[g : g + 1, :]

        around(collect)
        est[...] = est[...] * acc[...] / VIEWS

        @pl.when(it < ITERS - 1)
        def _():
            ext[it + 1, 0:128, 1024:1280] = est[...].astype(BF16)
            send_estimate(it + 1)

        return carry

    lax.fori_loop(0, ITERS, sweep, 0)

    flat[...] = est[...].T
    for y in range(16):
        out_ref[pl.ds(y, 16, stride=16), :] = flat[y * 16 : (y + 1) * 16, :]

    def sent(it, carry):
        both(lambda up: z_copy(it, up), lambda copy: copy.wait_send())
        both(lambda up: q_copy(it, up), lambda copy: copy.wait_send())

        def each(n):
            main_copy(it, n, 8 - n).wait_send()
            rim_copy(it, n, 8 - n).wait_send()
            c_copy(it, n, 8 - n).wait_send()

        around(each)
        return carry

    lax.fori_loop(0, ITERS, sent, 0)

    def sent_camera(a, carry):
        @pl.when(jnp.logical_not(is_self(camera_target(a))))
        def _():
            cam_copy(a, slot).wait_send()

        return carry

    lax.fori_loop(0, 16, sent_camera, 0)


def per_device(sizes, camera, initial, psf_taps):
    vmem = pl.BlockSpec(memory_space=pltpu.VMEM)
    dma = pltpu.SemaphoreType.DMA
    rows = initial.reshape(256, 128)
    result = pl.pallas_call(
        functools.partial(kernel, sizes),
        out_shape=jax.ShapeDtypeStruct((256, 128), F32),
        in_specs=[vmem, vmem, vmem],
        out_specs=vmem,
        scratch_shapes=[
            pltpu.VMEM((128, 256), F32),
            pltpu.VMEM((ITERS, 160, 9 * 256), BF16),
            pltpu.VMEM((ITERS, VIEWS, 256, 256), BF16),
            pltpu.VMEM((512, 256), BF16),
            pltpu.VMEM((VIEWS, 9 * 256, 256), BF16),
            pltpu.VMEM((9, VIEWS * 256, 256), BF16),
            pltpu.VMEM((VIEWS, 128, 256), BF16),
            pltpu.VMEM((VIEWS, 128, 256), BF16),
            pltpu.VMEM((24, 128), F32),
            pltpu.VMEM((24, 128), F32),
            pltpu.VMEM((48 * 8, 128), F32),
            pltpu.VMEM((48 * 8, 256), F32),
            pltpu.VMEM((48 * 8, 128), F32),
            pltpu.VMEM((48 * 8, 256), F32),
            pltpu.VMEM((16, 128), F32),
            pltpu.VMEM((2, 96, 1024), BF16),
            pltpu.VMEM((4, 1024, 256), BF16),
            pltpu.VMEM((16, 96, 128), BF16),
            pltpu.VMEM((16, 96, 128), BF16),
            pltpu.VMEM((VIEWS, 128, 256), BF16),
            pltpu.VMEM((128, VIEWS * 256), BF16),
            pltpu.VMEM((128, 256), F32),
            pltpu.VMEM((256, 128), F32),
            pltpu.VMEM((128, 256), F32),
            pltpu.VMEM((ITERS, 9, 144, 256), BF16),
            pltpu.VMEM((ITERS, 9, 144, 256), BF16),
            dma((16,)), dma((16,)),
            dma((ITERS, 2)), dma((ITERS, 2)),
            dma((ITERS, 9)), dma((ITERS, 9)),
            dma((ITERS, 9)), dma((ITERS, 9)),
            dma((ITERS, 2)), dma((ITERS, 2)),
            dma((ITERS, 9)), dma((ITERS, 9)),
        ],
        compiler_params=pltpu.CompilerParams(
            collective_id=0, has_side_effects=True, vmem_limit_bytes=48 * 1024 * 1024
        ),
    )(camera, rows, psf_taps)
    return result.reshape(initial.shape)


def solution(mesh):
    in_specs = (P(None, "gx", ("gy", "gz"), None), P("gx", "gy", "gz"), P())
    out_specs = P("gx", "gy", "gz")
    sizes = tuple(mesh.shape[a] for a in ("gx", "gy", "gz"))
    return jax.shard_map(
        functools.partial(per_device, sizes),
        mesh=mesh, in_specs=in_specs, out_specs=out_specs, check_vma=False,
    )
```

```python
import functools

import jax
import jax.numpy as jnp
from jax import lax
from jax.experimental import pallas as pl
from jax.experimental.pallas import tpu as pltpu
from jax.sharding import PartitionSpec as P

VIEWS = 6
TAPS = 31
HALF = TAPS // 2
ITERS = 2
F32 = jnp.float32
BF16 = jnp.bfloat16
MESH = pl.DeviceIdType.MESH
ORDER = (0, 2, 6, 8, 1, 3, 5, 7)


def dot(a, b):
    return jnp.dot(a, b, preferred_element_type=F32)


def iota(shape, dim):
    return lax.broadcasted_iota(jnp.int32, shape, dim)


def inside(index):
    return jnp.where((index >= 0) & (index < TAPS), index, 127)


def pick(table, index):
    return jnp.take_along_axis(table, index, axis=1)


def kernel(
    sizes, cam_hbm, init_hbm, taps_hbm, out_ref,
    cam_raw, init_ref, taps_ref, in_sem,
    est, ext, quot, inverse, ubuf, kf, kb, bzf, bzb, raw, back, xf, yf, xb, yb, scale,
    picked, place, cam_out, cam_in, rim_in, cam, third, part, flat, acc, code_out, code_in,
    cam_send, cam_recv, rim_send, rim_recv, e_send, e_recv, c_send, c_recv,
):
    nx, ny, nz = sizes
    gx, gy, gz = lax.axis_index("gx"), lax.axis_index("gy"), lax.axis_index("gz")
    below, above = gz > 0, gz < nz - 1

    fetch = [
        pltpu.make_async_copy(cam_hbm, cam_raw, in_sem.at[0]),
        pltpu.make_async_copy(init_hbm, init_ref, in_sem.at[1]),
        pltpu.make_async_copy(taps_hbm, taps_ref, in_sem.at[2]),
    ]
    for copy in fetch:
        copy.start()

    def place_of(m):
        n = lax.rem(m, 9)
        return gx + lax.div(n, 3) - 1, gy + lax.rem(n, 3) - 1, gz + lax.div(m, 9) - 1

    def there(m):
        x, y, z = place_of(m)
        return (x >= 0) & (x < nx) & (y >= 0) & (y < ny) & (z >= 0) & (z < nz)

    def around(first, last, body):
        def step(m, carry):
            @pl.when(there(m) & (m != 13))
            def _():
                body(m)

            return carry

        lax.fori_loop(first, last, step, 0)

    part_z, part_i = gx // 4, gx % 4

    def is_self(place):
        return (place[0] == gx) & (place[2] == gz)

    def source(s):
        return 4 * gz + s // 4, gy, s % 4

    def low_source(k):
        return 4 * gz - 1, gy, k

    def high_source(k):
        return 4 * gz + 4, gy, k

    def target(a):
        return a, gy, part_z

    gives_low = (part_i == 3) & (part_z < nz - 1)
    gives_high = (part_i == 0) & (part_z > 0)

    def low_target(a):
        return a, gy, part_z + 1

    def high_target(a):
        return a, gy, part_z - 1

    def others(count, place, body):
        def step(s, carry):
            @pl.when(jnp.logical_not(is_self(place(s))))
            def _():
                body(s)

            return carry

        lax.fori_loop(0, count, step, 0)

    barrier = pltpu.get_barrier_semaphore()

    def greet(place):
        pl.semaphore_signal(barrier, inc=1, device_id=place, device_id_type=MESH)

    others(16, source, lambda s: greet(source(s)))

    @pl.when(below)
    def _():
        others(4, low_source, lambda k: greet(low_source(k)))

    @pl.when(above)
    def _():
        others(4, high_source, lambda k: greet(high_source(k)))

    around(0, 27, lambda m: greet(place_of(m)))

    def one(flag):
        return flag.astype(jnp.int32)

    wide = 1 + one(gx > 0) + one(gx < nx - 1)
    tall = 1 + one(gy > 0) + one(gy < ny - 1)
    deep = 1 + one(below) + one(above)
    greetings = wide * tall * deep - 1 + 16 - one(part_z == gz)
    greetings += one(gives_low) * (16 - one(part_z + 1 == gz))
    greetings += one(gives_high) * (16 - one(part_z - 1 == gz))

    with jax.named_scope("zeros"):
        def clear(m, carry):
            @pl.when(jnp.logical_not(there(m)))
            def _():
                lanes = pl.ds(pl.multiple_of(lax.rem(m, 9) * 256, 256), 256)
                for it in range(ITERS):
                    @pl.when(m < 9)
                    def _():
                        ext[it, 128:160, lanes] = jnp.zeros((32, 256), BF16)

                    @pl.when((m >= 9) & (m < 18))
                    def _():
                        ext[it, 0:128, lanes] = jnp.zeros((128, 256), BF16)

                    @pl.when(m >= 18)
                    def _():
                        ext[it, 160:192, lanes] = jnp.zeros((32, 256), BF16)

            return carry

        lax.fori_loop(0, 27, clear, 0)
        quot[:, 160:256, :] = jnp.zeros((VIEWS, 96, 256), BF16)
        place[...] = jnp.zeros(place.shape, BF16)
        raw[...] = jnp.zeros((24, 128), F32)

    with jax.named_scope("sort camera"):
        row, col = iota((32, 256), 0), iota((32, 256), 1)
        same_x = row == (col >> 7) * 16 + (col & 15)
        for r in range(2):
            turned = ((col >> 6) & 1) == (r + gz) % 2
            for y in range(4):
                ones = (same_x & turned & (((col >> 4) & 3) == y)).astype(F32).astype(BF16)
                for q in range(4):
                    first = (r * 4 + y) * 128 + q * 32
                    place[q, first : first + 32, :] = ones
    fetch[0].wait()
    with jax.named_scope("sort camera 2"):
        for v in range(VIEWS):
            r, w = v // 3, v % 3
            for y in range(4):
                plane = cam_raw[v, :, y, :]
                lanes = slice((r * 4 + y) * 128, (r * 4 + y + 1) * 128)
                for h in range(2):
                    picked[h, w * 32 : (w + 1) * 32, lanes] = plane[:, h * 128 : (h + 1) * 128]
        for p in range(8):
            block = dot(picked[p // 4], place[p % 4]).astype(BF16)
            for w in range(3):
                cam_out[2 * p, w] = block[w * 32 : (w + 1) * 32, 0:128]
                cam_out[2 * p + 1, w] = block[w * 32 : (w + 1) * 32, 128:256]

    fetch[1].wait()
    with jax.named_scope("layout in"):
        for y in range(16):
            flat[y * 16 : (y + 1) * 16, :] = init_ref[pl.ds(y, 16, stride=16), :]
        est[...] = flat[...].T
        ext[0, 0:128, 1024:1280] = est[...].astype(BF16)

    with jax.named_scope("entry wait"):
        pl.semaphore_wait(barrier, greetings)

    slot = part_i * 4 + gz

    def cam_copy(a, s):
        return pltpu.make_async_remote_copy(
            src_ref=cam_out.at[a],
            dst_ref=cam_in.at[s],
            send_sem=cam_send.at[a],
            recv_sem=cam_recv.at[s],
            device_id=target(a),
            device_id_type=MESH,
        )

    def rim_copy(high, a, k):
        first = 0 if high else 16
        return pltpu.make_async_remote_copy(
            src_ref=cam_out.at[a, :, pl.ds(first, 16), :],
            dst_ref=rim_in.at[int(high), k],
            send_sem=rim_send.at[int(high), a],
            recv_sem=rim_recv.at[int(high), k],
            device_id=high_target(a) if high else low_target(a),
            device_id_type=MESH,
        )

    with jax.named_scope("send camera"):
        @pl.when(part_z == gz)
        def _():
            cam_in[slot] = cam_out[gx]

        others(16, target, lambda a: cam_copy(a, slot).start())

        @pl.when(gives_low)
        def _():
            @pl.when(part_z + 1 == gz)
            def _():
                rim_in[0, gz] = cam_out[gx, :, 16:32, :]

            others(16, low_target, lambda a: rim_copy(False, a, gz).start())

        @pl.when(gives_high)
        def _():
            @pl.when(part_z - 1 == gz)
            def _():
                rim_in[1, gz] = cam_out[gx, :, 0:16, :]

            others(16, high_target, lambda a: rim_copy(True, a, gz).start())

    def e_copy(it, step, m, at):
        first, count, to = ((0, 32, 160), (0, 128, 0), (96, 32, 128))[step + 1]
        lanes = pl.ds(pl.multiple_of(lax.rem(at, 9) * 256, 256), 256)
        return pltpu.make_async_remote_copy(
            src_ref=ext.at[it, pl.ds(first, count), pl.ds(1024, 256)],
            dst_ref=ext.at[it, pl.ds(to, count), lanes],
            send_sem=e_send.at[it, m],
            recv_sem=e_recv.at[it, at],
            device_id=place_of(m),
            device_id_type=MESH,
        )

    def each_estimate(act):
        for step in (-1, 1, 0):
            around(9 * (step + 1), 9 * (step + 2), lambda m: act(step, m))

    def send_estimate(it):
        each_estimate(lambda step, m: e_copy(it, step, m, 26 - m).start())

    with jax.named_scope("send estimate"):
        send_estimate(0)

    fetch[2].wait()
    with jax.named_scope("taps"):
        for v in range(VIEWS):
            for a in range(3):
                raw[a * 8 + v : a * 8 + v + 1, 0:TAPS] = taps_ref[v, a : a + 1, :]
        total = jnp.sum(raw[...], axis=1, keepdims=True)
        total = jnp.where((iota((24, 1), 0) & 7) < VIEWS, total, 1.0)
        back[...] = (raw[...] / total).astype(BF16).astype(F32)

    with jax.named_scope("tables"):
        def tables(i, carry):
            lane = iota((8, 128), 1)
            for k in range(6):
                j = i * 6 + k
                rows = pl.ds(pl.multiple_of(j * 8, 8), 8)
                x = lane & 15
                xf[rows, :] = pick(raw[0:8, :], inside(x + 31 - j))
                xb[rows, :] = pick(back[0:8, :], inside(j - 1 - x))
                for half in range(2):
                    y = (lane >> 4) + 8 * half
                    yf[half, rows, :] = pick(raw[8:16, :], inside(y + 31 - j))
                    yb[half, rows, :] = pick(back[8:16, :], inside(j - 1 - y))
            return carry

        lax.fori_loop(0, 8, tables, 0)

    def rows_of(table, j, v):
        return table[pl.ds(j * 128 + v, 16, stride=8), :]

    with jax.named_scope("products"):
        def products(i, carry):
            v, n = i // 9, i % 9
            dx, dy = n // 3, n % 3
            x = rows_of(xf, dx, v)
            for half in range(2):
                ys = rows_of(yf.at[half], dy, v)
                for y in range(16):
                    kf[v, pl.ds(pl.multiple_of(n * 256 + y * 16, 16), 16), half * 128 : (half + 1) * 128] = (
                        x * ys[y : y + 1, :]
                    ).astype(BF16)
            return carry

        lax.fori_loop(0, 9 * VIEWS, products, 0)

    with jax.named_scope("bands"):
        def bands(block, carry):
            r = iota((8, 128), 0) + block * 8
            z_out = jnp.where(r < 128, r, jnp.where(r < 144, r - 144, r - 16))
            rows = pl.ds(pl.multiple_of(block * 8, 8), 8)
            for t in range(3):
                lane = iota((8, 128), 1) + t * 128
                lane = jnp.where(lane < 192, lane, lane - 192)
                z_in = jnp.where(lane < 128, lane, jnp.where(lane < 160, lane - 160, lane - 32))
                index = inside(z_out - z_in + HALF)
                for v in range(VIEWS):
                    band_f = jnp.broadcast_to(raw[16 + v : 17 + v, :], (8, 128))
                    bzf[v, rows, t * 128 : (t + 1) * 128] = pick(band_f, index)
            return carry

        lax.fori_loop(0, 20, bands, 0)

        def back_bands(block, carry):
            z_out = iota((8, 128), 0) + block * 8
            rows = pl.ds(pl.multiple_of(block * 8, 8), 8)
            lane = iota((8, 128), 1)
            far = jnp.where(lane < 16, lane - 16, jnp.where(lane < 32, lane + 112, 1024))
            for half, z_in in enumerate((lane, far)):
                index = inside(z_in - z_out + HALF)
                for v in range(VIEWS):
                    band_b = jnp.broadcast_to(back[16 + v : 17 + v, :], (8, 128))
                    bzb[v, rows, half * 128 : (half + 1) * 128] = pick(band_b, index)
            return carry

        lax.fori_loop(0, 16, back_bands, 0)

    with jax.named_scope("scale"):
        fx, fy, fz = raw[0:8, :], raw[8:16, :], raw[16:24, :]
        bx, by = back[0:8, :], back[8:16, :]
        f_sum, b_sum = jnp.zeros((8, 128), F32), jnp.zeros((8, 128), F32)
        for t in range(TAPS):
            f_sum += (fx[:, t : t + 1] * fy).astype(BF16).astype(F32)
            b_sum += (bx[:, t : t + 1] * by).astype(BF16).astype(F32)

        def lanes_sum(a):
            return jnp.sum(a, axis=1, keepdims=True)

        f_scale = lanes_sum(f_sum) * lanes_sum(fz.astype(BF16).astype(F32))
        b_total = jnp.where(iota((8, 1), 0) < VIEWS, lanes_sum(b_sum), 1.0)
        b_scale = lanes_sum(bx) * lanes_sum(by) / b_total
        scale[0:8, :] = jnp.broadcast_to(f_scale, (8, 128))
        scale[8:16, :] = jnp.broadcast_to(b_scale, (8, 128))

    def factor(row):
        value = scale[row : row + 1, :]
        return jnp.concatenate([value, value], axis=1)

    def blur(it):
        for v in range(VIEWS):
            u = dot(ext[it], kf[v])
            high = u.astype(BF16)
            ubuf[v, 0:192, :] = high
            ubuf[v, 192:384, :] = (u - high.astype(F32)).astype(BF16)
        for v in range(VIEWS):
            inverse[v] = factor(v) / dot(bzf[v].astype(BF16), ubuf[v])

    def wait_estimate(it):
        each_estimate(lambda step, m: e_copy(it, step, m, m).wait_recv())

    def quotients():
        row = iota((32, 256), 0)
        seen = jnp.where(row < 16, one(below), one(above)) > 0
        for v in range(VIEWS):
            quot[v, 0:128, :] = (cam[v, 0:128, :].astype(F32) * inverse[v, 0:128, :]).astype(BF16)
            rim = jnp.where(seen, cam[v, 128:160, :].astype(F32) * inverse[v, 128:160, :], 0.0)
            quot[v, 128:160, :] = rim.astype(BF16)

    with jax.named_scope("wait estimate"):
        wait_estimate(0)
    with jax.named_scope("blur"):
        blur(0)

    with jax.named_scope("back products"):
        def back_products(i, carry):
            v, n = i // 9, i % 9
            dx, dy = n // 3, n % 3
            x = rows_of(xb, 2 - dx, v)
            for half in range(2):
                ys = rows_of(yb.at[half], 2 - dy, v)
                for y in range(16):
                    kb[n, pl.ds(pl.multiple_of(v * 256 + y * 16, 16), 16), half * 128 : (half + 1) * 128] = (
                        x * ys[y : y + 1, :]
                    ).astype(BF16)
            return carry

        lax.fori_loop(0, 9 * VIEWS, back_products, 0)

    with jax.named_scope("camera wait"):
        others(16, source, lambda s: cam_copy(0, s).wait_recv())

        @pl.when(below)
        def _():
            others(4, low_source, lambda k: rim_copy(False, 0, k).wait_recv())

        @pl.when(above)
        def _():
            others(4, high_source, lambda k: rim_copy(True, 0, k).wait_recv())

    with jax.named_scope("assemble"):
        def pair(r, even, odd):
            low = iota(even.shape, 1) < 64
            even, odd = even.astype(F32), odd.astype(F32)
            if r == 0:
                return jnp.where(low, even, odd).astype(BF16)
            return pltpu.roll(jnp.where(low, odd, even), 64, 1).astype(BF16)

        for v in range(VIEWS):
            r, w = v // 3, v % 3
            for t in range(2):
                lanes = slice(t * 128, (t + 1) * 128)
                for z in range(4):
                    cam[v, z * 32 : (z + 1) * 32, lanes] = pair(
                        r, cam_in[z * 4 + 2 * t, w], cam_in[z * 4 + 2 * t + 1, w]
                    )
                for high in range(2):
                    cam[v, 128 + high * 16 : 144 + high * 16, lanes] = pair(
                        r, rim_in[high, 2 * t, w], rim_in[high, 2 * t + 1, w]
                    )

    def c_copy(it, n, at):
        return pltpu.make_async_remote_copy(
            src_ref=code_out.at[it, n],
            dst_ref=code_in.at[it, at],
            send_sem=c_send.at[it, n],
            recv_sem=c_recv.at[it, at],
            device_id=place_of(9 + n),
            device_id_type=MESH,
        )

    for it in range(ITERS):
        if it > 0:
            with jax.named_scope("wait estimate 2"):
                wait_estimate(it)
            with jax.named_scope("blur 2"):
                blur(it)
        with jax.named_scope("quotients"):
            quotients()
        with jax.named_scope("third"):
            for v in range(VIEWS):
                value = dot(bzb[v].astype(BF16), quot[v]) * factor(8 + v)
                third[:, v * 256 : (v + 1) * 256] = value.astype(BF16)

        with jax.named_scope("partial sums"):
            for count, n in enumerate(ORDER):
                @pl.when(there(jnp.int32(9 + n)))
                def _():
                    with jax.named_scope("encode"):
                        work = part.at[count % 2]
                        work[...] = dot(third[...], kb[n])
                        base = jnp.concatenate([work[g * 16 + 8 : g * 16 + 9, :] for g in range(8)], axis=0)
                        base = base.astype(BF16).astype(F32)
                        rest = jnp.zeros((8, 256), F32)
                        code_out[it, n, 128:144, :] = jnp.concatenate([base, rest], axis=0).astype(BF16)
                        for g in range(8):
                            rows = slice(g * 16, (g + 1) * 16)
                            code_out[it, n, rows, :] = (work[rows, :] - base[g : g + 1, :]).astype(BF16)
                    c_copy(it, n, 8 - n).start()

        with jax.named_scope("own sum"):
            acc[...] = dot(third[...], kb[4])

        with jax.named_scope("collect"):
            for n in reversed(ORDER):
                @pl.when(there(jnp.int32(9 + n)))
                def _():
                    c_copy(it, n, n).wait_recv()
                    with jax.named_scope("add"):
                        base = code_in[it, n, 128:144, :].astype(F32)
                        for g in range(8):
                            rows = slice(g * 16, (g + 1) * 16)
                            acc[rows, :] += code_in[it, n, rows, :].astype(F32) + base[g : g + 1, :]

        est[...] = est[...] * acc[...] / VIEWS
        if it < ITERS - 1:
            ext[it + 1, 0:128, 1024:1280] = est[...].astype(BF16)
            with jax.named_scope("send estimate 2"):
                send_estimate(it + 1)

    with jax.named_scope("layout out"):
        flat[...] = est[...].T
        for y in range(16):
            out_ref[pl.ds(y, 16, stride=16), :] = flat[y * 16 : (y + 1) * 16, :]

    with jax.named_scope("sent"):
        def sent(it, carry):
            each_estimate(lambda step, m: e_copy(it, step, m, 26 - m).wait_send())
            around(9, 18, lambda m: c_copy(it, m - 9, 17 - m).wait_send())
            return carry

        lax.fori_loop(0, ITERS, sent, 0)
        others(16, target, lambda a: cam_copy(a, slot).wait_send())

        @pl.when(gives_low)
        def _():
            others(16, low_target, lambda a: rim_copy(False, a, gz).wait_send())

        @pl.when(gives_high)
        def _():
            others(16, high_target, lambda a: rim_copy(True, a, gz).wait_send())


def per_device(sizes, camera, initial, psf_taps):
    held = pl.BlockSpec(memory_space=pl.ANY)
    dma = pltpu.SemaphoreType.DMA
    rows = initial.reshape(256, 128)
    result = pl.pallas_call(
        functools.partial(kernel, sizes),
        out_shape=jax.ShapeDtypeStruct((256, 128), F32),
        in_specs=[held, held, held],
        out_specs=pl.BlockSpec(memory_space=pltpu.VMEM),
        scratch_shapes=[
            pltpu.VMEM((VIEWS, 32, 4, 256), BF16),
            pltpu.VMEM((256, 128), F32),
            pltpu.VMEM((VIEWS, 3, TAPS), F32),
            dma((3,)),
            pltpu.VMEM((128, 256), F32),
            pltpu.VMEM((ITERS, 192, 9 * 256), BF16),
            pltpu.VMEM((VIEWS, 256, 256), BF16),
            pltpu.VMEM((VIEWS, 160, 256), F32),
            pltpu.VMEM((VIEWS, 384, 256), BF16),
            pltpu.VMEM((VIEWS, 9 * 256, 256), BF16),
            pltpu.VMEM((9, VIEWS * 256, 256), BF16),
            pltpu.VMEM((VIEWS, 160, 384), F32),
            pltpu.VMEM((VIEWS, 128, 256), F32),
            pltpu.VMEM((24, 128), F32),
            pltpu.VMEM((24, 128), F32),
            pltpu.VMEM((48 * 8, 128), F32),
            pltpu.VMEM((2, 48 * 8, 128), F32),
            pltpu.VMEM((48 * 8, 128), F32),
            pltpu.VMEM((2, 48 * 8, 128), F32),
            pltpu.VMEM((16, 128), F32),
            pltpu.VMEM((2, 96, 1024), BF16),
            pltpu.VMEM((4, 1024, 256), BF16),
            pltpu.VMEM((16, 3, 32, 128), BF16),
            pltpu.VMEM((16, 3, 32, 128), BF16),
            pltpu.VMEM((2, 4, 3, 16, 128), BF16),
            pltpu.VMEM((VIEWS, 160, 256), BF16),
            pltpu.VMEM((128, VIEWS * 256), BF16),
            pltpu.VMEM((2, 128, 256), F32),
            pltpu.VMEM((256, 128), F32),
            pltpu.VMEM((128, 256), F32),
            pltpu.VMEM((ITERS, 9, 144, 256), BF16),
            pltpu.VMEM((ITERS, 9, 144, 256), BF16),
            dma((16,)), dma((16,)),
            dma((2, 16)), dma((2, 4)),
            dma((ITERS, 27)), dma((ITERS, 27)),
            dma((ITERS, 9)), dma((ITERS, 9)),
        ],
        compiler_params=pltpu.CompilerParams(
            collective_id=0, has_side_effects=True, vmem_limit_bytes=56 * 1024 * 1024
        ),
    )(camera, rows, psf_taps)
    return result.reshape(initial.shape)


def solution(mesh):
    in_specs = (P(None, "gx", ("gy", "gz"), None), P("gx", "gy", "gz"), P())
    out_specs = P("gx", "gy", "gz")
    sizes = tuple(mesh.shape[a] for a in ("gx", "gy", "gz"))
    return jax.shard_map(
        functools.partial(per_device, sizes),
        mesh=mesh, in_specs=in_specs, out_specs=out_specs, check_vma=False,
    )
```

```python
import functools

import jax
import jax.numpy as jnp
from jax import lax
from jax.experimental import pallas as pl
from jax.experimental.pallas import tpu as pltpu
from jax.sharding import PartitionSpec as P

VIEWS = 6
TAPS = 31
HALF = TAPS // 2
ITERS = 2
F32 = jnp.float32
BF16 = jnp.bfloat16
MESH = pl.DeviceIdType.MESH
ORDER = (0, 2, 6, 8, 1, 3, 5, 7)


def dot(a, b):
    return jnp.dot(a, b, preferred_element_type=F32)


def iota(shape, dim):
    return lax.broadcasted_iota(jnp.int32, shape, dim)


def inside(index):
    return jnp.where((index >= 0) & (index < TAPS), index, 127)


def pick(table, index):
    return jnp.take_along_axis(table, index, axis=1)


def kernel(
    sizes, cam_hbm, init_hbm, taps_hbm, out_ref,
    cam_raw, init_ref, taps_ref, in_sem,
    est, ext, quot, inverse, ubuf, kf, kb, bzf, bzb, raw, back, xf, yf, xb, yb, scale,
    picked, place, cam_out, cam_in, rim_in, cam, third, part, flat, acc, code_out, code_in,
    cam_send, cam_recv, rim_send, rim_recv, e_send, e_recv, f_send, f_recv, c_send, c_recv,
):
    nx, ny, nz = sizes
    gx, gy, gz = lax.axis_index("gx"), lax.axis_index("gy"), lax.axis_index("gz")
    below, above = gz > 0, gz < nz - 1

    fetch = [
        pltpu.make_async_copy(cam_hbm, cam_raw, in_sem.at[0]),
        pltpu.make_async_copy(init_hbm, init_ref, in_sem.at[1]),
        pltpu.make_async_copy(taps_hbm, taps_ref, in_sem.at[2]),
    ]
    for copy in fetch:
        copy.start()

    has_x = (gx > 0, True, gx < nx - 1)
    has_y = (gy > 0, True, gy < ny - 1)
    has_z = (below, True, above)

    def steps(m):
        return m % 9 // 3 - 1, m % 3 - 1, m // 9 - 1

    def place_of(m):
        dx, dy, dz = steps(m)
        return gx + dx, gy + dy, gz + dz

    def there(m):
        flags = [has[d + 1] for has, d in zip((has_x, has_y, has_z), steps(m)) if d]
        return functools.reduce(jnp.logical_and, flags)

    def around(ms, body):
        for m in ms:
            @pl.when(there(m))
            def _():
                body(m)

    everyone = sorted((m for m in range(27) if m != 13), key=lambda m: -sum(map(abs, steps(m))))
    rims = [m for m in everyone if m // 9 != 1]
    sides = [m for m in everyone if m // 9 == 1]

    part_z, part_i = gx >> 2, gx & 3

    def is_self(place):
        return (place[0] == gx) & (place[2] == gz)

    def source(s):
        return 4 * gz + s // 4, gy, s % 4

    def low_source(k):
        return 4 * gz - 1, gy, k

    def high_source(k):
        return 4 * gz + 4, gy, k

    def target(a):
        return a, gy, part_z

    gives_low = (part_i == 3) & (part_z < nz - 1)
    gives_high = (part_i == 0) & (part_z > 0)

    def low_target(a):
        return a, gy, part_z + 1

    def high_target(a):
        return a, gy, part_z - 1

    def others(count, place, body):
        for s in range(count):
            @pl.when(jnp.logical_not(is_self(place(s))))
            def _():
                body(s)

    barrier = pltpu.get_barrier_semaphore()

    def greet(place):
        pl.semaphore_signal(barrier, inc=1, device_id=place, device_id_type=MESH)

    others(16, source, lambda s: greet(source(s)))

    @pl.when(below)
    def _():
        others(4, low_source, lambda k: greet(low_source(k)))

    @pl.when(above)
    def _():
        others(4, high_source, lambda k: greet(high_source(k)))

    around(everyone, lambda m: greet(place_of(m)))

    def one(flag):
        return flag.astype(jnp.int32)

    wide = 1 + one(gx > 0) + one(gx < nx - 1)
    tall = 1 + one(gy > 0) + one(gy < ny - 1)
    deep = 1 + one(below) + one(above)
    greetings = wide * tall * deep - 1 + 16 - one(part_z == gz)
    greetings += one(gives_low) * (16 - one(part_z + 1 == gz))
    greetings += one(gives_high) * (16 - one(part_z - 1 == gz))

    with jax.named_scope("zeros"):
        for m in everyone:
            step, lanes = m // 9, slice(m % 9 * 256, m % 9 * 256 + 256)
            rows = (slice(128, 160), slice(0, 128), slice(160, 192))[step]

            for it in range(ITERS):
                sender = m if it or m in (4, 22) else 9 + m % 9

                @pl.when(jnp.logical_not(there(sender)))
                def _():
                    ext[it, rows, lanes] = jnp.zeros((rows.stop - rows.start, 256), BF16)

        quot[:, 160:256, :] = jnp.zeros((VIEWS, 96, 256), BF16)
        place[...] = jnp.zeros(place.shape, BF16)
        raw[...] = jnp.zeros((24, 128), F32)

    with jax.named_scope("sort camera"):
        row, col = iota((32, 256), 0), iota((32, 256), 1)
        same_x = row == (col >> 7) * 16 + (col & 15)
        for r in range(2):
            turned = ((col >> 6) & 1) == (r + gz) % 2
            for y in range(4):
                ones = (same_x & turned & (((col >> 4) & 3) == y)).astype(F32).astype(BF16)
                for q in range(4):
                    first = (r * 4 + y) * 128 + q * 32
                    place[q, first : first + 32, :] = ones
    fetch[0].wait()
    with jax.named_scope("sort camera 2"):
        for v in range(VIEWS):
            r, w = v // 3, v % 3
            for y in range(4):
                plane = cam_raw[v, :, y, :]
                lanes = slice((r * 4 + y) * 128, (r * 4 + y + 1) * 128)
                for h in range(2):
                    picked[h, w * 32 : (w + 1) * 32, lanes] = plane[:, h * 128 : (h + 1) * 128]
        for p in range(8):
            block = dot(picked[p // 4], place[p % 4]).astype(BF16)
            for w in range(3):
                cam_out[2 * p, w] = block[w * 32 : (w + 1) * 32, 0:128]
                cam_out[2 * p + 1, w] = block[w * 32 : (w + 1) * 32, 128:256]

    fetch[1].wait()
    with jax.named_scope("layout in"):
        for y in range(16):
            flat[y * 16 : (y + 1) * 16, :] = init_ref[pl.ds(y, 16, stride=16), :]
        est[...] = flat[...].T
        ext[0, 0:128, 1024:1280] = est[...].astype(BF16)

    with jax.named_scope("entry wait"):
        pl.semaphore_wait(barrier, greetings)

    slot = part_i * 4 + gz

    def cam_copy(a, s):
        return pltpu.make_async_remote_copy(
            src_ref=cam_out.at[a],
            dst_ref=cam_in.at[s],
            send_sem=cam_send.at[a],
            recv_sem=cam_recv.at[s],
            device_id=target(a),
            device_id_type=MESH,
        )

    def rim_copy(high, a, k):
        first = 0 if high else 16
        return pltpu.make_async_remote_copy(
            src_ref=cam_out.at[a, :, pl.ds(first, 16), :],
            dst_ref=rim_in.at[int(high), k],
            send_sem=rim_send.at[int(high), a],
            recv_sem=rim_recv.at[int(high), k],
            device_id=high_target(a) if high else low_target(a),
            device_id_type=MESH,
        )

    with jax.named_scope("send camera"):
        @pl.when(part_z == gz)
        def _():
            cam_in[slot] = cam_out[gx]

        others(16, target, lambda a: cam_copy(a, slot).start())

        @pl.when(gives_low)
        def _():
            @pl.when(part_z + 1 == gz)
            def _():
                rim_in[0, gz] = cam_out[gx, :, 16:32, :]

            others(16, low_target, lambda a: rim_copy(False, a, gz).start())

        @pl.when(gives_high)
        def _():
            @pl.when(part_z - 1 == gz)
            def _():
                rim_in[1, gz] = cam_out[gx, :, 0:16, :]

            others(16, high_target, lambda a: rim_copy(True, a, gz).start())

    def e_copy(it, m, at):
        first, count, to = ((0, 32, 160), (0, 128, 0), (96, 32, 128))[m // 9]
        return pltpu.make_async_remote_copy(
            src_ref=ext.at[it, pl.ds(first, count), pl.ds(1024, 256)],
            dst_ref=ext.at[it, pl.ds(to, count), pl.ds(at % 9 * 256, 256)],
            send_sem=e_send.at[it, m],
            recv_sem=e_recv.at[it, at],
            device_id=place_of(m),
            device_id_type=MESH,
        )

    def forward_copy(m, at):
        return pltpu.make_async_remote_copy(
            src_ref=ext.at[0, pl.ds(128, 64), pl.ds(1024, 256)],
            dst_ref=ext.at[0, pl.ds(128, 64), pl.ds(at % 9 * 256, 256)],
            send_sem=f_send.at[m - 9],
            recv_sem=f_recv.at[at - 9],
            device_id=place_of(m),
            device_id_type=MESH,
        )

    def send_estimate(it, ms):
        around(ms, lambda m: e_copy(it, m, 26 - m).start())

    def wait_estimate(it, ms):
        around(ms, lambda m: e_copy(it, m, m).wait_recv())

    vertical = (4, 22)
    with jax.named_scope("send estimate"):
        send_estimate(0, vertical)
        send_estimate(0, sides)

    fetch[2].wait()
    with jax.named_scope("taps"):
        for v in range(VIEWS):
            for a in range(3):
                raw[a * 8 + v : a * 8 + v + 1, 0:TAPS] = taps_ref[v, a : a + 1, :]
        total = jnp.sum(raw[...], axis=1, keepdims=True)
        total = jnp.where((iota((24, 1), 0) & 7) < VIEWS, total, 1.0)
        back[...] = (raw[...] / total).astype(BF16).astype(F32)

    with jax.named_scope("tables"):
        def tables(i, carry):
            lane = iota((8, 128), 1)
            for k in range(6):
                j = i * 6 + k
                rows = pl.ds(pl.multiple_of(j * 8, 8), 8)
                x = lane & 15
                xf[rows, :] = pick(raw[0:8, :], inside(x + 31 - j))
                xb[rows, :] = pick(back[0:8, :], inside(j - 1 - x))
                for half in range(2):
                    y = (lane >> 4) + 8 * half
                    yf[half, rows, :] = pick(raw[8:16, :], inside(y + 31 - j))
                    yb[half, rows, :] = pick(back[8:16, :], inside(j - 1 - y))
            return carry

        lax.fori_loop(0, 8, tables, 0)

    def rows_of(table, j, v):
        return table[pl.ds(j * 128 + v, 16, stride=8), :]

    with jax.named_scope("products"):
        def products(i, carry):
            v, n = i // 9, i % 9
            dx, dy = n // 3, n % 3
            x = rows_of(xf, dx, v)
            for half in range(2):
                ys = rows_of(yf.at[half], dy, v)
                for y in range(16):
                    kf[v, pl.ds(pl.multiple_of(n * 256 + y * 16, 16), 16), half * 128 : (half + 1) * 128] = (
                        x * ys[y : y + 1, :]
                    ).astype(BF16)
            return carry

        lax.fori_loop(0, 9 * VIEWS, products, 0)

    with jax.named_scope("forward rims"):
        wait_estimate(0, vertical)
        around(sides, lambda m: forward_copy(m, 26 - m).start())

    with jax.named_scope("bands"):
        def bands(block, carry):
            r = iota((8, 128), 0) + block * 8
            z_out = jnp.where(r < 128, r, jnp.where(r < 144, r - 144, r - 16))
            rows = pl.ds(pl.multiple_of(block * 8, 8), 8)
            for t in range(3):
                lane = iota((8, 128), 1) + t * 128
                lane = jnp.where(lane < 192, lane, lane - 192)
                z_in = jnp.where(lane < 128, lane, jnp.where(lane < 160, lane - 160, lane - 32))
                index = inside(z_out - z_in + HALF)
                for v in range(VIEWS):
                    band_f = jnp.broadcast_to(raw[16 + v : 17 + v, :], (8, 128))
                    bzf[v, rows, t * 128 : (t + 1) * 128] = pick(band_f, index)
            return carry

        lax.fori_loop(0, 20, bands, 0)

        def back_bands(block, carry):
            z_out = iota((8, 128), 0) + block * 8
            rows = pl.ds(pl.multiple_of(block * 8, 8), 8)
            lane = iota((8, 128), 1)
            far = jnp.where(lane < 16, lane - 16, jnp.where(lane < 32, lane + 112, 1024))
            for half, z_in in enumerate((lane, far)):
                index = inside(z_in - z_out + HALF)
                for v in range(VIEWS):
                    band_b = jnp.broadcast_to(back[16 + v : 17 + v, :], (8, 128))
                    bzb[v, rows, half * 128 : (half + 1) * 128] = pick(band_b, index)
            return carry

        lax.fori_loop(0, 16, back_bands, 0)

    with jax.named_scope("scale"):
        fx, fy, fz = raw[0:8, :], raw[8:16, :], raw[16:24, :]
        bx, by = back[0:8, :], back[8:16, :]
        f_sum, b_sum = jnp.zeros((8, 128), F32), jnp.zeros((8, 128), F32)
        for t in range(TAPS):
            f_sum += (fx[:, t : t + 1] * fy).astype(BF16).astype(F32)
            b_sum += (bx[:, t : t + 1] * by).astype(BF16).astype(F32)

        def lanes_sum(a):
            return jnp.sum(a, axis=1, keepdims=True)

        f_scale = lanes_sum(f_sum) * lanes_sum(fz.astype(BF16).astype(F32))
        b_total = jnp.where(iota((8, 1), 0) < VIEWS, lanes_sum(b_sum), 1.0)
        b_scale = lanes_sum(bx) * lanes_sum(by) / b_total
        scale[0:8, :] = jnp.broadcast_to(f_scale, (8, 128))
        scale[8:16, :] = jnp.broadcast_to(b_scale, (8, 128))

    with jax.named_scope("back products"):
        def back_products(i, carry):
            v, n = i // 9, i % 9
            dx, dy = n // 3, n % 3
            x = rows_of(xb, 2 - dx, v)
            for half in range(2):
                ys = rows_of(yb.at[half], 2 - dy, v)
                for y in range(16):
                    kb[n, pl.ds(pl.multiple_of(v * 256 + y * 16, 16), 16), half * 128 : (half + 1) * 128] = (
                        x * ys[y : y + 1, :]
                    ).astype(BF16)
            return carry

        lax.fori_loop(0, 9 * VIEWS, back_products, 0)

    def factor(row):
        value = scale[row : row + 1, :]
        return jnp.concatenate([value, value], axis=1)

    def blur(it):
        for v in range(VIEWS):
            u = dot(ext[it], kf[v])
            high = u.astype(BF16)
            ubuf[v, 0:192, :] = high
            ubuf[v, 192:384, :] = (u - high.astype(F32)).astype(BF16)
        for v in range(VIEWS):
            inverse[v] = factor(v) / dot(bzf[v].astype(BF16), ubuf[v])

    def quotients():
        row = iota((32, 256), 0)
        seen = jnp.where(row < 16, one(below), one(above)) > 0
        for v in range(VIEWS):
            quot[v, 0:128, :] = (cam[v, 0:128, :].astype(F32) * inverse[v, 0:128, :]).astype(BF16)
            rim = jnp.where(seen, cam[v, 128:160, :].astype(F32) * inverse[v, 128:160, :], 0.0)
            quot[v, 128:160, :] = rim.astype(BF16)

    with jax.named_scope("wait estimate"):
        wait_estimate(0, sides)
        around(sides, lambda m: forward_copy(m, m).wait_recv())
    with jax.named_scope("blur"):
        blur(0)

    with jax.named_scope("camera wait"):
        others(16, source, lambda s: cam_copy(0, s).wait_recv())

        @pl.when(below)
        def _():
            others(4, low_source, lambda k: rim_copy(False, 0, k).wait_recv())

        @pl.when(above)
        def _():
            others(4, high_source, lambda k: rim_copy(True, 0, k).wait_recv())

    with jax.named_scope("assemble"):
        def pair(r, even, odd):
            low = iota(even.shape, 1) < 64
            even, odd = even.astype(F32), odd.astype(F32)
            if r == 0:
                return jnp.where(low, even, odd).astype(BF16)
            return pltpu.roll(jnp.where(low, odd, even), 64, 1).astype(BF16)

        for v in range(VIEWS):
            r, w = v // 3, v % 3
            for t in range(2):
                lanes = slice(t * 128, (t + 1) * 128)
                for z in range(4):
                    cam[v, z * 32 : (z + 1) * 32, lanes] = pair(
                        r, cam_in[z * 4 + 2 * t, w], cam_in[z * 4 + 2 * t + 1, w]
                    )
                for high in range(2):
                    cam[v, 128 + high * 16 : 144 + high * 16, lanes] = pair(
                        r, rim_in[high, 2 * t, w], rim_in[high, 2 * t + 1, w]
                    )

    def c_copy(it, n, at):
        return pltpu.make_async_remote_copy(
            src_ref=code_out.at[it, n],
            dst_ref=code_in.at[it, at],
            send_sem=c_send.at[it, n],
            recv_sem=c_recv.at[it, at],
            device_id=place_of(9 + n),
            device_id_type=MESH,
        )

    def sent():
        around(vertical, lambda m: e_copy(0, m, 26 - m).wait_send())
        around(sides, lambda m: e_copy(0, m, 26 - m).wait_send())
        around(sides, lambda m: forward_copy(m, 26 - m).wait_send())
        for it in range(1, ITERS):
            around(everyone, lambda m: e_copy(it, m, 26 - m).wait_send())
        for it in range(ITERS - 1):
            around(sides, lambda m: c_copy(it, m - 9, 17 - m).wait_send())
        others(16, target, lambda a: cam_copy(a, slot).wait_send())

        @pl.when(gives_low)
        def _():
            others(16, low_target, lambda a: rim_copy(False, a, gz).wait_send())

        @pl.when(gives_high)
        def _():
            others(16, high_target, lambda a: rim_copy(True, a, gz).wait_send())

    for it in range(ITERS):
        if it > 0:
            with jax.named_scope("wait estimate 2"):
                wait_estimate(it, everyone)
            with jax.named_scope("blur 2"):
                blur(it)
        with jax.named_scope("quotients"):
            quotients()
        with jax.named_scope("third"):
            for v in range(VIEWS):
                value = dot(bzb[v].astype(BF16), quot[v]) * factor(8 + v)
                third[:, v * 256 : (v + 1) * 256] = value.astype(BF16)

        with jax.named_scope("partial sums"):
            for count, n in enumerate(ORDER):
                @pl.when(there(9 + n))
                def _():
                    with jax.named_scope("encode"):
                        work = part.at[count % 2]
                        work[...] = dot(third[...], kb[n])
                        base = jnp.concatenate([work[g * 16 + 8 : g * 16 + 9, :] for g in range(8)], axis=0)
                        base = base.astype(BF16).astype(F32)
                        rest = jnp.zeros((8, 256), F32)
                        code_out[it, n, 128:144, :] = jnp.concatenate([base, rest], axis=0).astype(BF16)
                        for g in range(8):
                            rows = slice(g * 16, (g + 1) * 16)
                            code_out[it, n, rows, :] = (work[rows, :] - base[g : g + 1, :]).astype(BF16)
                    c_copy(it, n, 8 - n).start()

        with jax.named_scope("own sum"):
            acc[...] = dot(third[...], kb[4])

        if it == ITERS - 1:
            with jax.named_scope("sent"):
                sent()

        with jax.named_scope("collect"):
            for n in reversed(ORDER):
                @pl.when(there(9 + n))
                def _():
                    c_copy(it, n, n).wait_recv()
                    with jax.named_scope("add"):
                        base = code_in[it, n, 128:144, :].astype(F32)
                        for g in range(8):
                            rows = slice(g * 16, (g + 1) * 16)
                            acc[rows, :] += code_in[it, n, rows, :].astype(F32) + base[g : g + 1, :]

        est[...] = est[...] * acc[...] / VIEWS
        if it < ITERS - 1:
            ext[it + 1, 0:128, 1024:1280] = est[...].astype(BF16)
            with jax.named_scope("send estimate 2"):
                send_estimate(it + 1, everyone)

    with jax.named_scope("layout out"):
        flat[...] = est[...].T
        for y in range(16):
            out_ref[pl.ds(y, 16, stride=16), :] = flat[y * 16 : (y + 1) * 16, :]

    for n in ORDER:
        @pl.when(there(9 + n))
        def _():
            c_copy(ITERS - 1, n, 8 - n).wait_send()


def per_device(sizes, camera, initial, psf_taps):
    held = pl.BlockSpec(memory_space=pl.ANY)
    dma = pltpu.SemaphoreType.DMA
    rows = initial.reshape(256, 128)
    result = pl.pallas_call(
        functools.partial(kernel, sizes),
        out_shape=jax.ShapeDtypeStruct((256, 128), F32),
        in_specs=[held, held, held],
        out_specs=pl.BlockSpec(memory_space=pltpu.VMEM),
        scratch_shapes=[
            pltpu.VMEM((VIEWS, 32, 4, 256), BF16),
            pltpu.VMEM((256, 128), F32),
            pltpu.VMEM((VIEWS, 3, TAPS), F32),
            dma((3,)),
            pltpu.VMEM((128, 256), F32),
            pltpu.VMEM((ITERS, 192, 9 * 256), BF16),
            pltpu.VMEM((VIEWS, 256, 256), BF16),
            pltpu.VMEM((VIEWS, 160, 256), F32),
            pltpu.VMEM((VIEWS, 384, 256), BF16),
            pltpu.VMEM((VIEWS, 9 * 256, 256), BF16),
            pltpu.VMEM((9, VIEWS * 256, 256), BF16),
            pltpu.VMEM((VIEWS, 160, 384), F32),
            pltpu.VMEM((VIEWS, 128, 256), F32),
            pltpu.VMEM((24, 128), F32),
            pltpu.VMEM((24, 128), F32),
            pltpu.VMEM((48 * 8, 128), F32),
            pltpu.VMEM((2, 48 * 8, 128), F32),
            pltpu.VMEM((48 * 8, 128), F32),
            pltpu.VMEM((2, 48 * 8, 128), F32),
            pltpu.VMEM((16, 128), F32),
            pltpu.VMEM((2, 96, 1024), BF16),
            pltpu.VMEM((4, 1024, 256), BF16),
            pltpu.VMEM((16, 3, 32, 128), BF16),
            pltpu.VMEM((16, 3, 32, 128), BF16),
            pltpu.VMEM((2, 4, 3, 16, 128), BF16),
            pltpu.VMEM((VIEWS, 160, 256), BF16),
            pltpu.VMEM((128, VIEWS * 256), BF16),
            pltpu.VMEM((2, 128, 256), F32),
            pltpu.VMEM((256, 128), F32),
            pltpu.VMEM((128, 256), F32),
            pltpu.VMEM((ITERS, 9, 144, 256), BF16),
            pltpu.VMEM((ITERS, 9, 144, 256), BF16),
            dma((16,)), dma((16,)),
            dma((2, 16)), dma((2, 4)),
            dma((ITERS, 27)), dma((ITERS, 27)),
            dma((9,)), dma((9,)),
            dma((ITERS, 9)), dma((ITERS, 9)),
        ],
        compiler_params=pltpu.CompilerParams(
            collective_id=0, has_side_effects=True, vmem_limit_bytes=56 * 1024 * 1024
        ),
    )(camera, rows, psf_taps)
    return result.reshape(initial.shape)


def solution(mesh):
    in_specs = (P(None, "gx", ("gy", "gz"), None), P("gx", "gy", "gz"), P())
    out_specs = P("gx", "gy", "gz")
    sizes = tuple(mesh.shape[a] for a in ("gx", "gy", "gz"))
    return jax.shard_map(
        functools.partial(per_device, sizes),
        mesh=mesh, in_specs=in_specs, out_specs=out_specs, check_vma=False,
    )
```

```python
import functools

import jax
import jax.numpy as jnp
from jax import lax
from jax.experimental import pallas as pl
from jax.experimental.pallas import tpu as pltpu
from jax.sharding import PartitionSpec as P

VIEWS = 6
TAPS = 31
HALF = TAPS // 2
ITERS = 2
F32 = jnp.float32
BF16 = jnp.bfloat16
MESH = pl.DeviceIdType.MESH
ORDER = (0, 2, 6, 8, 1, 3, 5, 7)


def dot(a, b):
    return jnp.dot(a, b, preferred_element_type=F32)


def iota(shape, dim):
    return lax.broadcasted_iota(jnp.int32, shape, dim)


def inside(index):
    return jnp.where((index >= 0) & (index < TAPS), index, 127)


def pick(table, index):
    return jnp.take_along_axis(table, index, axis=1)


def kernel(
    sizes, cam_hbm, init_hbm, taps_hbm, out_ref,
    cam_raw, init_ref, taps_ref, in_sem,
    est, ext, quot, inverse, ubuf, kf, kb, bzf, bzb, raw, back, xf, yf, xb, yb, scale,
    picked, place, cam_out, cam_in, rim_in, cam, third, part, flat, acc, code_out0, code_out1, code_out2, code_in0, code_in1, code_in2,
    cam_send, cam_recv, rim_send, rim_recv, e_send, e_recv, f_send, f_recv, c_send, c_recv, m_send, m_recv,
):
    code_out, code_in = (code_out0, code_out1, code_out2), (code_in0, code_in1, code_in2)
    nx, ny, nz = sizes
    gx, gy, gz = lax.axis_index("gx"), lax.axis_index("gy"), lax.axis_index("gz")
    below, above = gz > 0, gz < nz - 1

    fetch = [
        pltpu.make_async_copy(cam_hbm, cam_raw, in_sem.at[0]),
        pltpu.make_async_copy(init_hbm, init_ref, in_sem.at[1]),
        pltpu.make_async_copy(taps_hbm, taps_ref, in_sem.at[2]),
    ]
    for copy in fetch:
        copy.start()

    has_x = (gx > 0, True, gx < nx - 1)
    has_y = (gy > 0, True, gy < ny - 1)
    has_z = (below, True, above)

    def steps(m):
        return m % 9 // 3 - 1, m % 3 - 1, m // 9 - 1

    def place_of(m):
        dx, dy, dz = steps(m)
        return gx + dx, gy + dy, gz + dz

    def there(m):
        flags = [has[d + 1] for has, d in zip((has_x, has_y, has_z), steps(m)) if d]
        return functools.reduce(jnp.logical_and, flags)

    def around(ms, body):
        for m in ms:
            @pl.when(there(m))
            def _():
                body(m)

    everyone = sorted((m for m in range(27) if m != 13), key=lambda m: -sum(map(abs, steps(m))))
    rims = [m for m in everyone if m // 9 != 1]
    sides = [m for m in everyone if m // 9 == 1]

    part_z, part_i = gx >> 2, gx & 3

    def is_self(place):
        return (place[0] == gx) & (place[2] == gz)

    def source(s):
        return 4 * gz + s // 4, gy, s % 4

    def low_source(k):
        return 4 * gz - 1, gy, k

    def high_source(k):
        return 4 * gz + 4, gy, k

    def target(a):
        return a, gy, part_z

    gives_low = (part_i == 3) & (part_z == 1)
    gives_high = (part_i == 0) & (part_z == 2)
    takes_low, takes_high = gz == 2, gz == 1

    def low_target(a):
        return a, gy, part_z + 1

    def high_target(a):
        return a, gy, part_z - 1

    def others(count, place, body):
        for s in range(count):
            @pl.when(jnp.logical_not(is_self(place(s))))
            def _():
                body(s)

    barrier = pltpu.get_barrier_semaphore()

    def greet(place):
        pl.semaphore_signal(barrier, inc=1, device_id=place, device_id_type=MESH)

    others(16, source, lambda s: greet(source(s)))

    @pl.when(takes_low)
    def _():
        others(4, low_source, lambda k: greet(low_source(k)))

    @pl.when(takes_high)
    def _():
        others(4, high_source, lambda k: greet(high_source(k)))

    around(everyone, lambda m: greet(place_of(m)))

    def one(flag):
        return flag.astype(jnp.int32)

    wide = 1 + one(gx > 0) + one(gx < nx - 1)
    tall = 1 + one(gy > 0) + one(gy < ny - 1)
    deep = 1 + one(below) + one(above)
    greetings = wide * tall * deep - 1 + 16 - one(part_z == gz)
    greetings += one(gives_low) * (16 - one(part_z + 1 == gz))
    greetings += one(gives_high) * (16 - one(part_z - 1 == gz))

    with jax.named_scope("zeros"):
        for m in everyone:
            step, lanes = m // 9, slice(m % 9 * 256, m % 9 * 256 + 256)
            rows = (slice(128, 160), slice(0, 128), slice(160, 192))[step]

            for it in range(ITERS):
                sender = m if it or m in (4, 22) else 9 + m % 9

                @pl.when(jnp.logical_not(there(sender)))
                def _():
                    ext[it, rows, lanes] = jnp.zeros((rows.stop - rows.start, 256), BF16)

        quot[:, 160:256, :] = jnp.zeros((VIEWS, 96, 256), BF16)
        place[...] = jnp.zeros(place.shape, BF16)
        raw[...] = jnp.zeros((24, 128), F32)

    with jax.named_scope("sort camera"):
        row, col = iota((32, 256), 0), iota((32, 256), 1)
        same_x = row == (col >> 7) * 16 + (col & 15)
        for r in range(2):
            turned = ((col >> 6) & 1) == (r + gz) % 2
            for y in range(4):
                ones = (same_x & turned & (((col >> 4) & 3) == y)).astype(F32).astype(BF16)
                for q in range(4):
                    first = (r * 4 + y) * 128 + q * 32
                    place[q, first : first + 32, :] = ones
    fetch[0].wait()
    with jax.named_scope("sort camera 2"):
        for v in range(VIEWS):
            r, w = v // 3, v % 3
            for y in range(4):
                plane = cam_raw[v, :, y, :]
                lanes = slice((r * 4 + y) * 128, (r * 4 + y + 1) * 128)
                for h in range(2):
                    picked[h, w * 32 : (w + 1) * 32, lanes] = plane[:, h * 128 : (h + 1) * 128]
        for p in range(8):
            block = dot(picked[p // 4], place[p % 4]).astype(BF16)
            for w in range(3):
                cam_out[2 * p, w] = block[w * 32 : (w + 1) * 32, 0:128]
                cam_out[2 * p + 1, w] = block[w * 32 : (w + 1) * 32, 128:256]

    fetch[1].wait()
    with jax.named_scope("layout in"):
        for y in range(16):
            flat[y * 16 : (y + 1) * 16, :] = init_ref[pl.ds(y, 16, stride=16), :]
        est[...] = flat[...].T
        ext[0, 0:128, 1024:1280] = est[...].astype(BF16)

    with jax.named_scope("entry wait"):
        pl.semaphore_wait(barrier, greetings)

    slot = part_i * 4 + gz

    def cam_copy(a, s):
        return pltpu.make_async_remote_copy(
            src_ref=cam_out.at[a],
            dst_ref=cam_in.at[s],
            send_sem=cam_send.at[a],
            recv_sem=cam_recv.at[s],
            device_id=target(a),
            device_id_type=MESH,
        )

    def rim_copy(high, a, k):
        first = 0 if high else 16
        return pltpu.make_async_remote_copy(
            src_ref=cam_out.at[a, :, pl.ds(first, 16), :],
            dst_ref=rim_in.at[int(high), k],
            send_sem=rim_send.at[int(high), a],
            recv_sem=rim_recv.at[int(high), k],
            device_id=high_target(a) if high else low_target(a),
            device_id_type=MESH,
        )

    def e_copy(it, m, at):
        first, count, to = ((0, 32, 160), (0, 128, 0), (96, 32, 128))[m // 9]
        return pltpu.make_async_remote_copy(
            src_ref=ext.at[it, pl.ds(first, count), pl.ds(1024, 256)],
            dst_ref=ext.at[it, pl.ds(to, count), pl.ds(at % 9 * 256, 256)],
            send_sem=e_send.at[it, m],
            recv_sem=e_recv.at[it, at],
            device_id=place_of(m),
            device_id_type=MESH,
        )

    def forward_copy(m, at):
        return pltpu.make_async_remote_copy(
            src_ref=ext.at[0, pl.ds(128, 64), pl.ds(1024, 256)],
            dst_ref=ext.at[0, pl.ds(128, 64), pl.ds(at % 9 * 256, 256)],
            send_sem=f_send.at[m - 9],
            recv_sem=f_recv.at[at - 9],
            device_id=place_of(m),
            device_id_type=MESH,
        )

    def send_estimate(it, ms):
        around(ms, lambda m: e_copy(it, m, 26 - m).start())

    def wait_estimate(it, ms):
        around(ms, lambda m: e_copy(it, m, m).wait_recv())

    vertical = (4, 22)
    with jax.named_scope("send rims"):
        send_estimate(0, vertical)

    with jax.named_scope("send camera"):
        @pl.when(part_z == gz)
        def _():
            cam_in[slot] = cam_out[gx]

        others(16, target, lambda a: cam_copy(a, slot).start())

        @pl.when(gives_low)
        def _():
            @pl.when(part_z + 1 == gz)
            def _():
                rim_in[0, gz] = cam_out[gx, :, 16:32, :]

            others(16, low_target, lambda a: rim_copy(False, a, gz).start())

        @pl.when(gives_high)
        def _():
            @pl.when(part_z - 1 == gz)
            def _():
                rim_in[1, gz] = cam_out[gx, :, 0:16, :]

            others(16, high_target, lambda a: rim_copy(True, a, gz).start())

    with jax.named_scope("send estimate"):
        send_estimate(0, sides)

    fetch[2].wait()
    with jax.named_scope("taps"):
        for v in range(VIEWS):
            for a in range(3):
                raw[a * 8 + v : a * 8 + v + 1, 0:TAPS] = taps_ref[v, a : a + 1, :]
        total = jnp.sum(raw[...], axis=1, keepdims=True)
        total = jnp.where((iota((24, 1), 0) & 7) < VIEWS, total, 1.0)
        back[...] = (raw[...] / total).astype(BF16).astype(F32)

    with jax.named_scope("tables"):
        def tables(i, carry):
            lane = iota((8, 128), 1)
            for k in range(6):
                j = i * 6 + k
                rows = pl.ds(pl.multiple_of(j * 8, 8), 8)
                x = lane & 15
                xf[rows, :] = pick(raw[0:8, :], inside(x + 31 - j))
                xb[rows, :] = pick(back[0:8, :], inside(j - 1 - x))
                for half in range(2):
                    y = (lane >> 4) + 8 * half
                    yf[half, rows, :] = pick(raw[8:16, :], inside(y + 31 - j))
                    yb[half, rows, :] = pick(back[8:16, :], inside(j - 1 - y))
            return carry

        lax.fori_loop(0, 8, tables, 0)

    def rows_of(table, j, v):
        return table[pl.ds(j * 128 + v, 16, stride=8), :]

    with jax.named_scope("products"):
        def products(i, carry):
            v, n = i // 9, i % 9
            dx, dy = n // 3, n % 3
            x = rows_of(xf, dx, v)
            for half in range(2):
                ys = rows_of(yf.at[half], dy, v)
                for y in range(16):
                    kf[v, pl.ds(pl.multiple_of(n * 256 + y * 16, 16), 16), half * 128 : (half + 1) * 128] = (
                        x * ys[y : y + 1, :]
                    ).astype(BF16)
            return carry

        lax.fori_loop(0, 9 * VIEWS, products, 0)

    with jax.named_scope("forward rims"):
        wait_estimate(0, vertical)
        around(sides, lambda m: forward_copy(m, 26 - m).start())

    with jax.named_scope("bands"):
        def bands(block, carry):
            r = iota((8, 128), 0) + block * 8
            z_out = jnp.where(r < 128, r, jnp.where(r < 144, r - 144, r - 16))
            rows = pl.ds(pl.multiple_of(block * 8, 8), 8)
            for t in range(3):
                lane = iota((8, 128), 1) + t * 128
                lane = jnp.where(lane < 192, lane, lane - 192)
                z_in = jnp.where(lane < 128, lane, jnp.where(lane < 160, lane - 160, lane - 32))
                index = inside(z_out - z_in + HALF)
                for v in range(VIEWS):
                    band_f = jnp.broadcast_to(raw[16 + v : 17 + v, :], (8, 128))
                    bzf[v, rows, t * 128 : (t + 1) * 128] = pick(band_f, index)
            return carry

        lax.fori_loop(0, 20, bands, 0)

        def back_bands(block, carry):
            z_out = iota((8, 128), 0) + block * 8
            rows = pl.ds(pl.multiple_of(block * 8, 8), 8)
            lane = iota((8, 128), 1)
            far = jnp.where(lane < 16, lane - 16, jnp.where(lane < 32, lane + 112, 1024))
            for half, z_in in enumerate((lane, far)):
                index = inside(z_in - z_out + HALF)
                for v in range(VIEWS):
                    band_b = jnp.broadcast_to(back[16 + v : 17 + v, :], (8, 128))
                    bzb[v, rows, half * 128 : (half + 1) * 128] = pick(band_b, index)
            return carry

        lax.fori_loop(0, 16, back_bands, 0)

    with jax.named_scope("scale"):
        fx, fy, fz = raw[0:8, :], raw[8:16, :], raw[16:24, :]
        bx, by = back[0:8, :], back[8:16, :]
        f_sum, b_sum = jnp.zeros((8, 128), F32), jnp.zeros((8, 128), F32)
        for t in range(TAPS):
            f_sum += (fx[:, t : t + 1] * fy).astype(BF16).astype(F32)
            b_sum += (bx[:, t : t + 1] * by).astype(BF16).astype(F32)

        def lanes_sum(a):
            return jnp.sum(a, axis=1, keepdims=True)

        f_scale = lanes_sum(f_sum) * lanes_sum(fz.astype(BF16).astype(F32))
        b_total = jnp.where(iota((8, 1), 0) < VIEWS, lanes_sum(b_sum), 1.0)
        b_scale = lanes_sum(bx) * lanes_sum(by) / b_total
        scale[0:8, :] = jnp.broadcast_to(f_scale, (8, 128))
        scale[8:16, :] = jnp.broadcast_to(b_scale, (8, 128))

    with jax.named_scope("back products"):
        def back_products(i, carry):
            v, n = i // 9, i % 9
            dx, dy = n // 3, n % 3
            x = rows_of(xb, 2 - dx, v)
            for half in range(2):
                ys = rows_of(yb.at[half], 2 - dy, v)
                for y in range(16):
                    kb[n, pl.ds(pl.multiple_of(v * 256 + y * 16, 16), 16), half * 128 : (half + 1) * 128] = (
                        x * ys[y : y + 1, :]
                    ).astype(BF16)
            return carry

        lax.fori_loop(0, 9 * VIEWS, back_products, 0)

    def factor(row):
        value = scale[row : row + 1, :]
        return jnp.concatenate([value, value], axis=1)

    def blur(it):
        for v in range(VIEWS):
            u = dot(ext[it], kf[v])
            high = u.astype(BF16)
            ubuf[v, 0:192, :] = high
            ubuf[v, 192:384, :] = (u - high.astype(F32)).astype(BF16)
        for v in range(VIEWS):
            inverse[v] = factor(v) / dot(bzf[v].astype(BF16), ubuf[v])

    def quotients():
        row = iota((32, 256), 0)
        seen = jnp.where(row < 16, one(below), one(above)) > 0
        for v in range(VIEWS):
            quot[v, 0:128, :] = (cam[v, 0:128, :].astype(F32) * inverse[v, 0:128, :]).astype(BF16)
            rim = jnp.where(seen, cam[v, 128:160, :].astype(F32) * inverse[v, 128:160, :], 0.0)
            quot[v, 128:160, :] = rim.astype(BF16)

    with jax.named_scope("wait estimate"):
        wait_estimate(0, sides)
        around(sides, lambda m: forward_copy(m, m).wait_recv())
    with jax.named_scope("blur"):
        blur(0)

    def mate_copy(first, to):
        return pltpu.make_async_remote_copy(
            src_ref=cam.at[:, pl.ds(first, 16), :],
            dst_ref=cam.at[:, pl.ds(to, 16), :],
            send_sem=m_send,
            recv_sem=m_recv,
            device_id=(gx, gy, gz ^ 1),
            device_id_type=MESH,
        )

    def pair(r, even, odd):
        low = iota(even.shape, 1) < 64
        even, odd = even.astype(F32), odd.astype(F32)
        if r == 0:
            return jnp.where(low, even, odd).astype(BF16)
        return pltpu.roll(jnp.where(low, odd, even), 64, 1).astype(BF16)

    def assemble(z):
        for k in range(4):
            @pl.when(jnp.logical_not(is_self(source(4 * z + k))))
            def _():
                cam_copy(0, 4 * z + k).wait_recv()
        for v in range(VIEWS):
            r, w = v // 3, v % 3
            for t in range(2):
                cam[v, z * 32 : (z + 1) * 32, t * 128 : (t + 1) * 128] = pair(
                    r, cam_in[z * 4 + 2 * t, w], cam_in[z * 4 + 2 * t + 1, w]
                )

    def assemble_rim(high):
        place = high_source if high else low_source
        others(4, place, lambda k: rim_copy(high, 0, k).wait_recv())
        for v in range(VIEWS):
            r, w = v // 3, v % 3
            for t in range(2):
                cam[v, 128 + high * 16 : 144 + high * 16, t * 128 : (t + 1) * 128] = pair(
                    r, rim_in[high, 2 * t, w], rim_in[high, 2 * t + 1, w]
                )

    even = (gz & 1) == 0
    with jax.named_scope("camera in"):
        @pl.when(even)
        def _():
            assemble(3)
            mate_copy(112, 128).start()
            assemble(0)

        @pl.when(jnp.logical_not(even))
        def _():
            assemble(0)
            mate_copy(0, 144).start()
            assemble(3)

        assemble(1)
        assemble(2)

        @pl.when(takes_low)
        def _():
            assemble_rim(0)

        @pl.when(takes_high)
        def _():
            assemble_rim(1)

        @pl.when(even)
        def _():
            mate_copy(0, 144).wait_recv()

        @pl.when(jnp.logical_not(even))
        def _():
            mate_copy(112, 128).wait_recv()

    parts = ((0, 1, 6, 7), (2, 3, 4, 5), tuple(range(8)))

    def c_copy(part_of, n, at):
        return pltpu.make_async_remote_copy(
            src_ref=code_out[part_of].at[n],
            dst_ref=code_in[part_of].at[at],
            send_sem=c_send.at[part_of, n],
            recv_sem=c_recv.at[part_of, at],
            device_id=place_of(9 + n),
            device_id_type=MESH,
        )

    def encode(work, part_of, n):
        groups, out = parts[part_of], code_out[part_of]
        base = [work[g * 16 + 8 : g * 16 + 9, :] for g in groups]
        base = jnp.concatenate(base + [jnp.zeros((16 - len(groups), 256), F32)], axis=0).astype(BF16)
        out[n, len(groups) * 16 : len(groups) * 16 + 16, :] = base
        base = base.astype(F32)
        for i, g in enumerate(groups):
            out[n, i * 16 : (i + 1) * 16, :] = (work[g * 16 : (g + 1) * 16, :] - base[i : i + 1, :]).astype(BF16)

    def collect(part_of):
        groups, code = parts[part_of], code_in[part_of]
        for n in reversed(ORDER):
            @pl.when(there(9 + n))
            def _():
                c_copy(part_of, n, n).wait_recv()
                with jax.named_scope("add"):
                    base = code[n, len(groups) * 16 : len(groups) * 16 + 16, :].astype(F32)
                    for i, g in enumerate(groups):
                        rows = slice(g * 16, (g + 1) * 16)
                        acc[rows, :] += code[n, i * 16 : (i + 1) * 16, :].astype(F32) + base[i : i + 1, :]

    def update(part_of, it):
        for g in parts[part_of]:
            rows = slice(g * 16, (g + 1) * 16)
            value = est[rows, :] * acc[rows, :] / VIEWS
            est[rows, :] = value
            if it < ITERS - 1:
                ext[it + 1, rows, 1024:1280] = value.astype(BF16)

    def sent():
        around(vertical, lambda m: e_copy(0, m, 26 - m).wait_send())
        around(sides, lambda m: e_copy(0, m, 26 - m).wait_send())
        around(sides, lambda m: forward_copy(m, 26 - m).wait_send())
        for it in range(1, ITERS):
            around(everyone, lambda m: e_copy(it, m, 26 - m).wait_send())
        for part_of in range(2):
            around(sides, lambda m: c_copy(part_of, m - 9, 17 - m).wait_send())

        @pl.when(even)
        def _():
            mate_copy(112, 128).wait_send()

        @pl.when(jnp.logical_not(even))
        def _():
            mate_copy(0, 144).wait_send()
        others(16, target, lambda a: cam_copy(a, slot).wait_send())

        @pl.when(gives_low)
        def _():
            others(16, low_target, lambda a: rim_copy(False, a, gz).wait_send())

        @pl.when(gives_high)
        def _():
            others(16, high_target, lambda a: rim_copy(True, a, gz).wait_send())

    for it in range(ITERS):
        if it > 0:
            with jax.named_scope("wait estimate 2"):
                wait_estimate(it, everyone)
            with jax.named_scope("blur 2"):
                blur(it)
        with jax.named_scope("quotients"):
            quotients()
        with jax.named_scope("third"):
            for v in range(VIEWS):
                value = dot(bzb[v].astype(BF16), quot[v]) * factor(8 + v)
                third[:, v * 256 : (v + 1) * 256] = value.astype(BF16)

        last = it == ITERS - 1
        with jax.named_scope("partial sums"):
            for count, n in enumerate(ORDER):
                @pl.when(there(9 + n))
                def _():
                    work = part.at[count % 2]
                    work[...] = dot(third[...], kb[n])
                    if last:
                        encode(work, 2, n)
                        c_copy(2, n, 8 - n).start()
                    else:
                        encode(work, 0, n)
                        c_copy(0, n, 8 - n).start()
                        encode(work, 1, n)
            if not last:
                for n in ORDER:
                    @pl.when(there(9 + n))
                    def _():
                        c_copy(1, n, 8 - n).start()

        with jax.named_scope("own sum"):
            acc[...] = dot(third[...], kb[4])
        if last:
            with jax.named_scope("sent"):
                sent()
            collect(2)
            update(2, it)
        else:
            collect(0)
            update(0, it)
            send_estimate(it + 1, rims)
            collect(1)
            update(1, it)
            send_estimate(it + 1, sides)

    with jax.named_scope("layout out"):
        flat[...] = est[...].T
        for y in range(16):
            out_ref[pl.ds(y, 16, stride=16), :] = flat[y * 16 : (y + 1) * 16, :]

    for n in ORDER:
        @pl.when(there(9 + n))
        def _():
            c_copy(2, n, 8 - n).wait_send()


def per_device(sizes, camera, initial, psf_taps):
    held = pl.BlockSpec(memory_space=pl.ANY)
    dma = pltpu.SemaphoreType.DMA
    rows = initial.reshape(256, 128)
    result = pl.pallas_call(
        functools.partial(kernel, sizes),
        out_shape=jax.ShapeDtypeStruct((256, 128), F32),
        in_specs=[held, held, held],
        out_specs=pl.BlockSpec(memory_space=pltpu.VMEM),
        scratch_shapes=[
            pltpu.VMEM((VIEWS, 32, 4, 256), BF16),
            pltpu.VMEM((256, 128), F32),
            pltpu.VMEM((VIEWS, 3, TAPS), F32),
            dma((3,)),
            pltpu.VMEM((128, 256), F32),
            pltpu.VMEM((ITERS, 192, 9 * 256), BF16),
            pltpu.VMEM((VIEWS, 256, 256), BF16),
            pltpu.VMEM((VIEWS, 160, 256), F32),
            pltpu.VMEM((VIEWS, 384, 256), BF16),
            pltpu.VMEM((VIEWS, 9 * 256, 256), BF16),
            pltpu.VMEM((9, VIEWS * 256, 256), BF16),
            pltpu.VMEM((VIEWS, 160, 384), F32),
            pltpu.VMEM((VIEWS, 128, 256), F32),
            pltpu.VMEM((24, 128), F32),
            pltpu.VMEM((24, 128), F32),
            pltpu.VMEM((48 * 8, 128), F32),
            pltpu.VMEM((2, 48 * 8, 128), F32),
            pltpu.VMEM((48 * 8, 128), F32),
            pltpu.VMEM((2, 48 * 8, 128), F32),
            pltpu.VMEM((16, 128), F32),
            pltpu.VMEM((2, 96, 1024), BF16),
            pltpu.VMEM((4, 1024, 256), BF16),
            pltpu.VMEM((16, 3, 32, 128), BF16),
            pltpu.VMEM((16, 3, 32, 128), BF16),
            pltpu.VMEM((2, 4, 3, 16, 128), BF16),
            pltpu.VMEM((VIEWS, 160, 256), BF16),
            pltpu.VMEM((128, VIEWS * 256), BF16),
            pltpu.VMEM((2, 128, 256), F32),
            pltpu.VMEM((256, 128), F32),
            pltpu.VMEM((128, 256), F32),
            *[pltpu.VMEM((9, rows, 256), BF16) for rows in (80, 80, 144) * 2],
            dma((16,)), dma((16,)),
            dma((2, 16)), dma((2, 4)),
            dma((ITERS, 27)), dma((ITERS, 27)),
            dma((9,)), dma((9,)),
            dma((3, 9)), dma((3, 9)),
            dma(()), dma(()),
        ],
        compiler_params=pltpu.CompilerParams(
            collective_id=0, has_side_effects=True, vmem_limit_bytes=56 * 1024 * 1024
        ),
    )(camera, rows, psf_taps)
    return result.reshape(initial.shape)


def solution(mesh):
    in_specs = (P(None, "gx", ("gy", "gz"), None), P("gx", "gy", "gz"), P())
    out_specs = P("gx", "gy", "gz")
    sizes = tuple(mesh.shape[a] for a in ("gx", "gy", "gz"))
    return jax.shard_map(
        functools.partial(per_device, sizes),
        mesh=mesh, in_specs=in_specs, out_specs=out_specs, check_vma=False,
    )
```

```python
import functools

import jax
import jax.numpy as jnp
from jax import lax
from jax.experimental import pallas as pl
from jax.experimental.pallas import tpu as pltpu
from jax.sharding import PartitionSpec as P

VIEWS = 6
TAPS = 31
HALF = TAPS // 2
ITERS = 2
F32 = jnp.float32
BF16 = jnp.bfloat16
MESH = pl.DeviceIdType.MESH
ORDER = (0, 2, 6, 8, 1, 3, 5, 7)


def dot(a, b):
    return jnp.dot(a, b, preferred_element_type=F32)


def iota(shape, dim):
    return lax.broadcasted_iota(jnp.int32, shape, dim)


def inside(index):
    return jnp.where((index >= 0) & (index < TAPS), index, 127)


def pick(table, index):
    return jnp.take_along_axis(table, index, axis=1)


def kernel(
    sizes, cam_hbm, init_hbm, taps_hbm, out_ref,
    cam_raw, init_ref, taps_ref, in_sem,
    est, ext, quot, inverse, ubuf, kf, kb, bzf, bzb, raw, back, xf, yf, xb, yb, scale,
    picked, place, cam_out, cam_in, rim_in, cam, third, part, flat, acc, code_out0, code_out1, code_out2, code_in0, code_in1, code_in2,
    cam_send, cam_recv, rim_send, rim_recv, e_send, e_recv, g_send, g_recv, c_send, c_recv, m_send, m_recv,
):
    code_out, code_in = (code_out0, code_out1, code_out2), (code_in0, code_in1, code_in2)
    nx, ny, nz = sizes
    gx, gy, gz = lax.axis_index("gx"), lax.axis_index("gy"), lax.axis_index("gz")
    below, above = gz > 0, gz < nz - 1

    fetch = [
        pltpu.make_async_copy(cam_hbm, cam_raw, in_sem.at[0]),
        pltpu.make_async_copy(init_hbm, init_ref, in_sem.at[1]),
        pltpu.make_async_copy(taps_hbm, taps_ref, in_sem.at[2]),
    ]
    for copy in fetch:
        copy.start()

    has_x = (gx > 0, True, gx < nx - 1)
    has_y = (gy > 0, True, gy < ny - 1)
    has_z = (below, True, above)

    def steps(m):
        return m % 9 // 3 - 1, m % 3 - 1, m // 9 - 1

    def place_of(m):
        dx, dy, dz = steps(m)
        return gx + dx, gy + dy, gz + dz

    def there(m):
        flags = [has[d + 1] for has, d in zip((has_x, has_y, has_z), steps(m)) if d]
        return functools.reduce(jnp.logical_and, flags)

    def around(ms, body):
        for m in ms:
            @pl.when(there(m))
            def _():
                body(m)

    everyone = sorted((m for m in range(27) if m != 13), key=lambda m: -sum(map(abs, steps(m))))
    rims = [m for m in everyone if m // 9 != 1]
    sides = [m for m in everyone if m // 9 == 1]

    part_z, part_i = gx >> 2, gx & 3

    def is_self(place):
        return (place[0] == gx) & (place[2] == gz)

    def source(s):
        return 4 * gz + s // 4, gy, s % 4

    def low_source(k):
        return 4 * gz - 1, gy, k

    def high_source(k):
        return 4 * gz + 4, gy, k

    def target(a):
        return a, gy, part_z

    gives_low = (part_i == 3) & (part_z == 1)
    gives_high = (part_i == 0) & (part_z == 2)
    takes_low, takes_high = gz == 2, gz == 1

    def low_target(a):
        return a, gy, part_z + 1

    def high_target(a):
        return a, gy, part_z - 1

    def others(count, place, body):
        for s in range(count):
            @pl.when(jnp.logical_not(is_self(place(s))))
            def _():
                body(s)

    barrier = pltpu.get_barrier_semaphore()

    def greet(place):
        pl.semaphore_signal(barrier, inc=1, device_id=place, device_id_type=MESH)

    others(16, source, lambda s: greet(source(s)))

    @pl.when(takes_low)
    def _():
        others(4, low_source, lambda k: greet(low_source(k)))

    @pl.when(takes_high)
    def _():
        others(4, high_source, lambda k: greet(high_source(k)))

    around(everyone, lambda m: greet(place_of(m)))

    def one(flag):
        return flag.astype(jnp.int32)

    wide = 1 + one(gx > 0) + one(gx < nx - 1)
    tall = 1 + one(gy > 0) + one(gy < ny - 1)
    deep = 1 + one(below) + one(above)
    greetings = wide * tall * deep - 1 + 16 - one(part_z == gz)
    greetings += one(gives_low) * (16 - one(part_z + 1 == gz))
    greetings += one(gives_high) * (16 - one(part_z - 1 == gz))

    with jax.named_scope("zeros"):
        for m in everyone:
            step, lanes = m // 9, slice(m % 9 * 256, m % 9 * 256 + 256)
            rows = (slice(128, 160), slice(0, 128), slice(160, 192))[step]

            for it in range(ITERS):
                @pl.when(jnp.logical_not(there(m)))
                def _():
                    ext[it, rows, lanes] = jnp.zeros((rows.stop - rows.start, 256), BF16)

        quot[:, 160:256, :] = jnp.zeros((VIEWS, 96, 256), BF16)
        place[...] = jnp.zeros(place.shape, BF16)
        raw[...] = jnp.zeros((24, 128), F32)
        ubuf[:, 192:256, :] = jnp.zeros((VIEWS, 64, 512), BF16)

    with jax.named_scope("sort camera"):
        row, col = iota((32, 256), 0), iota((32, 256), 1)
        same_x = row == (col >> 7) * 16 + (col & 15)
        for r in range(2):
            turned = ((col >> 6) & 1) == (r + gz) % 2
            for y in range(4):
                ones = (same_x & turned & (((col >> 4) & 3) == y)).astype(F32).astype(BF16)
                for q in range(4):
                    first = (r * 4 + y) * 128 + q * 32
                    place[q, first : first + 32, :] = ones
    fetch[0].wait()
    with jax.named_scope("sort camera 2"):
        for v in range(VIEWS):
            r, w = v // 3, v % 3
            for y in range(4):
                plane = cam_raw[v, :, y, :]
                lanes = slice((r * 4 + y) * 128, (r * 4 + y + 1) * 128)
                for h in range(2):
                    picked[h, w * 32 : (w + 1) * 32, lanes] = plane[:, h * 128 : (h + 1) * 128]
        for p in range(8):
            block = dot(picked[p // 4], place[p % 4]).astype(BF16)
            for w in range(3):
                cam_out[2 * p, w] = block[w * 32 : (w + 1) * 32, 0:128]
                cam_out[2 * p + 1, w] = block[w * 32 : (w + 1) * 32, 128:256]

    parts = ((0, 1, 6, 7), (2, 3, 4, 5), tuple(range(8)))

    def keep(it, part_of):
        for i, g in enumerate(parts[part_of]):
            first = part_of * 64 + i * 16
            ext[it, first : first + 16, 1024:1280] = est[g * 16 : (g + 1) * 16, :].astype(BF16)

    fetch[1].wait()
    with jax.named_scope("layout in"):
        for y in range(16):
            flat[y * 16 : (y + 1) * 16, :] = init_ref[pl.ds(y, 16, stride=16), :]
        est[...] = flat[...].T
        for part_of in range(2):
            keep(0, part_of)

    with jax.named_scope("entry wait"):
        pl.semaphore_wait(barrier, greetings)

    slot = part_i * 4 + gz

    def cam_copy(a, s):
        return pltpu.make_async_remote_copy(
            src_ref=cam_out.at[a],
            dst_ref=cam_in.at[s],
            send_sem=cam_send.at[a],
            recv_sem=cam_recv.at[s],
            device_id=target(a),
            device_id_type=MESH,
        )

    def rim_copy(high, a, k):
        first = 0 if high else 16
        return pltpu.make_async_remote_copy(
            src_ref=cam_out.at[a, :, pl.ds(first, 16), :],
            dst_ref=rim_in.at[int(high), k],
            send_sem=rim_send.at[int(high), a],
            recv_sem=rim_recv.at[int(high), k],
            device_id=high_target(a) if high else low_target(a),
            device_id_type=MESH,
        )

    def e_copy(it, m, at):
        first, count, to = ((0, 32, 160), (0, 64 if it else 128, 0), (32, 32, 128))[m // 9]
        return pltpu.make_async_remote_copy(
            src_ref=ext.at[it, pl.ds(first, count), pl.ds(1024, 256)],
            dst_ref=ext.at[it, pl.ds(to, count), pl.ds(at % 9 * 256, 256)],
            send_sem=e_send.at[it, m],
            recv_sem=e_recv.at[it, at],
            device_id=place_of(m),
            device_id_type=MESH,
        )

    def middle_copy(m, at):
        return pltpu.make_async_remote_copy(
            src_ref=ext.at[1, pl.ds(64, 64), pl.ds(1024, 256)],
            dst_ref=ext.at[1, pl.ds(64, 64), pl.ds(at % 9 * 256, 256)],
            send_sem=g_send.at[m - 9],
            recv_sem=g_recv.at[at - 9],
            device_id=place_of(m),
            device_id_type=MESH,
        )

    def send_estimate(it, ms):
        around(ms, lambda m: e_copy(it, m, 26 - m).start())

    def wait_estimate(it, ms):
        around(ms, lambda m: e_copy(it, m, m).wait_recv())

    with jax.named_scope("send estimate"):
        send_estimate(0, everyone)

    with jax.named_scope("send camera"):
        @pl.when(part_z == gz)
        def _():
            cam_in[slot] = cam_out[gx]

        others(16, target, lambda a: cam_copy(a, slot).start())

        @pl.when(gives_low)
        def _():
            @pl.when(part_z + 1 == gz)
            def _():
                rim_in[0, gz] = cam_out[gx, :, 16:32, :]

            others(16, low_target, lambda a: rim_copy(False, a, gz).start())

        @pl.when(gives_high)
        def _():
            @pl.when(part_z - 1 == gz)
            def _():
                rim_in[1, gz] = cam_out[gx, :, 0:16, :]

            others(16, high_target, lambda a: rim_copy(True, a, gz).start())

    fetch[2].wait()
    with jax.named_scope("taps"):
        for v in range(VIEWS):
            for a in range(3):
                raw[a * 8 + v : a * 8 + v + 1, 0:TAPS] = taps_ref[v, a : a + 1, :]
        total = jnp.sum(raw[...], axis=1, keepdims=True)
        total = jnp.where((iota((24, 1), 0) & 7) < VIEWS, total, 1.0)
        back[...] = (raw[...] / total).astype(BF16).astype(F32)

    with jax.named_scope("tables"):
        def tables(i, carry):
            lane = iota((8, 128), 1)
            for k in range(6):
                j = i * 6 + k
                rows = pl.ds(pl.multiple_of(j * 8, 8), 8)
                x = lane & 15
                xf[rows, :] = pick(raw[0:8, :], inside(x + 31 - j))
                xb[rows, :] = pick(back[0:8, :], inside(j - 1 - x))
                for half in range(2):
                    y = (lane >> 4) + 8 * half
                    yf[half, rows, :] = pick(raw[8:16, :], inside(y + 31 - j))
                    yb[half, rows, :] = pick(back[8:16, :], inside(j - 1 - y))
            return carry

        lax.fori_loop(0, 8, tables, 0)

    def rows_of(table, j, v):
        return table[pl.ds(j * 128 + v, 16, stride=8), :]

    with jax.named_scope("products"):
        def products(i, carry):
            v, n = i // 9, i % 9
            dx, dy = n // 3, n % 3
            x = rows_of(xf, dx, v)
            for half in range(2):
                ys = rows_of(yf.at[half], dy, v)
                for y in range(16):
                    kf[v, pl.ds(pl.multiple_of(n * 256 + y * 16, 16), 16), half * 128 : (half + 1) * 128] = (
                        x * ys[y : y + 1, :]
                    ).astype(BF16)
            return carry

        lax.fori_loop(0, 9 * VIEWS, products, 0)

    with jax.named_scope("bands"):
        def bands(block, carry):
            r = iota((8, 128), 0) + block * 8
            z_out = jnp.where(r < 128, r, jnp.where(r < 144, r - 144, r - 16))
            rows = pl.ds(pl.multiple_of(block * 8, 8), 8)
            lane = iota((8, 128), 1)
            near = jnp.where(lane < 32, lane, jnp.where(lane < 64, lane + 64, lane - 32))
            far = jnp.where(lane < 32, lane - 32, jnp.where(lane < 64, lane + 96, 4096))
            for half, z_in in enumerate((near, far)):
                index = inside(z_out - z_in + HALF)
                for v in range(VIEWS):
                    band_f = jnp.broadcast_to(raw[16 + v : 17 + v, :], (8, 128))
                    bzf[v, rows, half * 128 : (half + 1) * 128] = pick(band_f, index)
            return carry

        lax.fori_loop(0, 20, bands, 0)

        def back_bands(block, carry):
            z_out = iota((8, 128), 0) + block * 8
            rows = pl.ds(pl.multiple_of(block * 8, 8), 8)
            lane = iota((8, 128), 1)
            far = jnp.where(lane < 16, lane - 16, jnp.where(lane < 32, lane + 112, 1024))
            for half, z_in in enumerate((lane, far)):
                index = inside(z_in - z_out + HALF)
                for v in range(VIEWS):
                    band_b = jnp.broadcast_to(back[16 + v : 17 + v, :], (8, 128))
                    bzb[v, rows, half * 128 : (half + 1) * 128] = pick(band_b, index)
            return carry

        lax.fori_loop(0, 16, back_bands, 0)

    with jax.named_scope("scale"):
        fx, fy, fz = raw[0:8, :], raw[8:16, :], raw[16:24, :]
        bx, by = back[0:8, :], back[8:16, :]
        f_sum, b_sum = jnp.zeros((8, 128), F32), jnp.zeros((8, 128), F32)
        for t in range(TAPS):
            f_sum += (fx[:, t : t + 1] * fy).astype(BF16).astype(F32)
            b_sum += (bx[:, t : t + 1] * by).astype(BF16).astype(F32)

        def lanes_sum(a):
            return jnp.sum(a, axis=1, keepdims=True)

        f_scale = lanes_sum(f_sum) * lanes_sum(fz.astype(BF16).astype(F32))
        b_total = jnp.where(iota((8, 1), 0) < VIEWS, lanes_sum(b_sum), 1.0)
        b_scale = lanes_sum(bx) * lanes_sum(by) / b_total
        scale[0:8, :] = jnp.broadcast_to(f_scale, (8, 128))
        scale[8:16, :] = jnp.broadcast_to(b_scale, (8, 128))

    with jax.named_scope("back products"):
        def back_products(i, carry):
            v, n = i // 9, i % 9
            dx, dy = n // 3, n % 3
            x = rows_of(xb, 2 - dx, v)
            for half in range(2):
                ys = rows_of(yb.at[half], 2 - dy, v)
                for y in range(16):
                    kb[n, pl.ds(pl.multiple_of(v * 256 + y * 16, 16), 16), half * 128 : (half + 1) * 128] = (
                        x * ys[y : y + 1, :]
                    ).astype(BF16)
            return carry

        lax.fori_loop(0, 9 * VIEWS, back_products, 0)

    def factor(row):
        value = scale[row : row + 1, :]
        return jnp.concatenate([value, value], axis=1)

    def blur(it):
        for v in range(VIEWS):
            u = dot(ext[it], kf[v])
            high = u.astype(BF16)
            ubuf[v, 0:192, 0:256] = high
            ubuf[v, 0:192, 256:512] = (u - high.astype(F32)).astype(BF16)
        for v in range(VIEWS):
            halves = dot(bzf[v].astype(BF16), ubuf[v])
            inverse[v] = factor(v) / (halves[:, 0:256] + halves[:, 256:512])

    def quotients():
        row = iota((32, 256), 0)
        seen = jnp.where(row < 16, one(below), one(above)) > 0
        for v in range(VIEWS):
            quot[v, 0:128, :] = (cam[v, 0:128, :].astype(F32) * inverse[v, 0:128, :]).astype(BF16)
            rim = jnp.where(seen, cam[v, 128:160, :].astype(F32) * inverse[v, 128:160, :], 0.0)
            quot[v, 128:160, :] = rim.astype(BF16)

    with jax.named_scope("wait estimate"):
        wait_estimate(0, everyone)
    with jax.named_scope("blur"):
        blur(0)

    def mate_copy(first, to):
        return pltpu.make_async_remote_copy(
            src_ref=cam.at[:, pl.ds(first, 16), :],
            dst_ref=cam.at[:, pl.ds(to, 16), :],
            send_sem=m_send,
            recv_sem=m_recv,
            device_id=(gx, gy, gz ^ 1),
            device_id_type=MESH,
        )

    def pair(r, even, odd):
        low = iota(even.shape, 1) < 64
        even, odd = even.astype(F32), odd.astype(F32)
        if r == 0:
            return jnp.where(low, even, odd).astype(BF16)
        return pltpu.roll(jnp.where(low, odd, even), 64, 1).astype(BF16)

    def assemble(z):
        for k in range(4):
            @pl.when(jnp.logical_not(is_self(source(4 * z + k))))
            def _():
                cam_copy(0, 4 * z + k).wait_recv()
        for v in range(VIEWS):
            r, w = v // 3, v % 3
            for t in range(2):
                cam[v, z * 32 : (z + 1) * 32, t * 128 : (t + 1) * 128] = pair(
                    r, cam_in[z * 4 + 2 * t, w], cam_in[z * 4 + 2 * t + 1, w]
                )

    def assemble_rim(high):
        place = high_source if high else low_source
        others(4, place, lambda k: rim_copy(high, 0, k).wait_recv())
        for v in range(VIEWS):
            r, w = v // 3, v % 3
            for t in range(2):
                cam[v, 128 + high * 16 : 144 + high * 16, t * 128 : (t + 1) * 128] = pair(
                    r, rim_in[high, 2 * t, w], rim_in[high, 2 * t + 1, w]
                )

    even = (gz & 1) == 0
    with jax.named_scope("camera in"):
        @pl.when(even)
        def _():
            assemble(3)
            mate_copy(112, 128).start()
            assemble(0)

        @pl.when(jnp.logical_not(even))
        def _():
            assemble(0)
            mate_copy(0, 144).start()
            assemble(3)

        assemble(1)
        assemble(2)

        @pl.when(takes_low)
        def _():
            assemble_rim(0)

        @pl.when(takes_high)
        def _():
            assemble_rim(1)

        @pl.when(even)
        def _():
            mate_copy(0, 144).wait_recv()

        @pl.when(jnp.logical_not(even))
        def _():
            mate_copy(112, 128).wait_recv()

    def c_copy(part_of, n, at):
        return pltpu.make_async_remote_copy(
            src_ref=code_out[part_of].at[n],
            dst_ref=code_in[part_of].at[at],
            send_sem=c_send.at[part_of, n],
            recv_sem=c_recv.at[part_of, at],
            device_id=place_of(9 + n),
            device_id_type=MESH,
        )

    def encode(work, part_of, n):
        groups, out = parts[part_of], code_out[part_of]
        base = [work[g * 16 + 8 : g * 16 + 9, :] for g in groups]
        base = jnp.concatenate(base + [jnp.zeros((16 - len(groups), 256), F32)], axis=0).astype(BF16)
        out[n, len(groups) * 16 : len(groups) * 16 + 16, :] = base
        base = base.astype(F32)
        for i, g in enumerate(groups):
            out[n, i * 16 : (i + 1) * 16, :] = (work[g * 16 : (g + 1) * 16, :] - base[i : i + 1, :]).astype(BF16)

    def collect(part_of):
        groups, code = parts[part_of], code_in[part_of]
        for n in reversed(ORDER):
            @pl.when(there(9 + n))
            def _():
                c_copy(part_of, n, n).wait_recv()
                with jax.named_scope("add"):
                    base = code[n, len(groups) * 16 : len(groups) * 16 + 16, :].astype(F32)
                    for i, g in enumerate(groups):
                        rows = slice(g * 16, (g + 1) * 16)
                        acc[rows, :] += code[n, i * 16 : (i + 1) * 16, :].astype(F32) + base[i : i + 1, :]

    def update(part_of):
        for g in parts[part_of]:
            rows = slice(g * 16, (g + 1) * 16)
            est[rows, :] = est[rows, :] * acc[rows, :] / VIEWS

    def sent():
        around(everyone, lambda m: e_copy(0, m, 26 - m).wait_send())
        for it in range(1, ITERS):
            around(everyone, lambda m: e_copy(it, m, 26 - m).wait_send())
            around(sides, lambda m: middle_copy(m, 26 - m).wait_send())
        for part_of in range(2):
            around(sides, lambda m: c_copy(part_of, m - 9, 17 - m).wait_send())

        @pl.when(even)
        def _():
            mate_copy(112, 128).wait_send()

        @pl.when(jnp.logical_not(even))
        def _():
            mate_copy(0, 144).wait_send()
        others(16, target, lambda a: cam_copy(a, slot).wait_send())

        @pl.when(gives_low)
        def _():
            others(16, low_target, lambda a: rim_copy(False, a, gz).wait_send())

        @pl.when(gives_high)
        def _():
            others(16, high_target, lambda a: rim_copy(True, a, gz).wait_send())

    for it in range(ITERS):
        if it > 0:
            with jax.named_scope("wait estimate 2"):
                wait_estimate(it, everyone)
                around(sides, lambda m: middle_copy(m, m).wait_recv())
            with jax.named_scope("blur 2"):
                blur(it)
        with jax.named_scope("quotients"):
            quotients()
        with jax.named_scope("third"):
            for v in range(VIEWS):
                value = dot(bzb[v].astype(BF16), quot[v]) * factor(8 + v)
                third[:, v * 256 : (v + 1) * 256] = value.astype(BF16)

        last = it == ITERS - 1
        with jax.named_scope("partial sums"):
            for count, n in enumerate(ORDER):
                @pl.when(there(9 + n))
                def _():
                    work = part.at[count % 2]
                    work[...] = dot(third[...], kb[n])
                    if last:
                        encode(work, 2, n)
                        c_copy(2, n, 8 - n).start()
                    else:
                        encode(work, 0, n)
                        c_copy(0, n, 8 - n).start()
                        encode(work, 1, n)
            if not last:
                for n in ORDER:
                    @pl.when(there(9 + n))
                    def _():
                        c_copy(1, n, 8 - n).start()

        with jax.named_scope("own sum"):
            acc[...] = dot(third[...], kb[4])
        if last:
            with jax.named_scope("sent"):
                sent()
            collect(2)
            update(2)
        else:
            collect(0)
            update(0)
            keep(it + 1, 0)
            send_estimate(it + 1, everyone)
            collect(1)
            update(1)
            keep(it + 1, 1)
            around(sides, lambda m: middle_copy(m, 26 - m).start())

    with jax.named_scope("layout out"):
        flat[...] = est[...].T
        for y in range(16):
            out_ref[pl.ds(y, 16, stride=16), :] = flat[y * 16 : (y + 1) * 16, :]

    for n in ORDER:
        @pl.when(there(9 + n))
        def _():
            c_copy(2, n, 8 - n).wait_send()


def per_device(sizes, camera, initial, psf_taps):
    held = pl.BlockSpec(memory_space=pl.ANY)
    dma = pltpu.SemaphoreType.DMA
    rows = initial.reshape(256, 128)
    result = pl.pallas_call(
        functools.partial(kernel, sizes),
        out_shape=jax.ShapeDtypeStruct((256, 128), F32),
        in_specs=[held, held, held],
        out_specs=pl.BlockSpec(memory_space=pltpu.VMEM),
        scratch_shapes=[
            pltpu.VMEM((VIEWS, 32, 4, 256), BF16),
            pltpu.VMEM((256, 128), F32),
            pltpu.VMEM((VIEWS, 3, TAPS), F32),
            dma((3,)),
            pltpu.VMEM((128, 256), F32),
            pltpu.VMEM((ITERS, 192, 9 * 256), BF16),
            pltpu.VMEM((VIEWS, 256, 256), BF16),
            pltpu.VMEM((VIEWS, 160, 256), F32),
            pltpu.VMEM((VIEWS, 256, 512), BF16),
            pltpu.VMEM((VIEWS, 9 * 256, 256), BF16),
            pltpu.VMEM((9, VIEWS * 256, 256), BF16),
            pltpu.VMEM((VIEWS, 160, 256), F32),
            pltpu.VMEM((VIEWS, 128, 256), F32),
            pltpu.VMEM((24, 128), F32),
            pltpu.VMEM((24, 128), F32),
            pltpu.VMEM((48 * 8, 128), F32),
            pltpu.VMEM((2, 48 * 8, 128), F32),
            pltpu.VMEM((48 * 8, 128), F32),
            pltpu.VMEM((2, 48 * 8, 128), F32),
            pltpu.VMEM((16, 128), F32),
            pltpu.VMEM((2, 96, 1024), BF16),
            pltpu.VMEM((4, 1024, 256), BF16),
            pltpu.VMEM((16, 3, 32, 128), BF16),
            pltpu.VMEM((16, 3, 32, 128), BF16),
            pltpu.VMEM((2, 4, 3, 16, 128), BF16),
            pltpu.VMEM((VIEWS, 160, 256), BF16),
            pltpu.VMEM((128, VIEWS * 256), BF16),
            pltpu.VMEM((2, 128, 256), F32),
            pltpu.VMEM((256, 128), F32),
            pltpu.VMEM((128, 256), F32),
            *[pltpu.VMEM((9, rows, 256), BF16) for rows in (80, 80, 144) * 2],
            dma((16,)), dma((16,)),
            dma((2, 16)), dma((2, 4)),
            dma((ITERS, 27)), dma((ITERS, 27)),
            dma((9,)), dma((9,)),
            dma((3, 9)), dma((3, 9)),
            dma(()), dma(()),
        ],
        compiler_params=pltpu.CompilerParams(
            collective_id=0, has_side_effects=True, vmem_limit_bytes=55040 * 1024
        ),
    )(camera, rows, psf_taps)
    return result.reshape(initial.shape)


def solution(mesh):
    in_specs = (P(None, "gx", ("gy", "gz"), None), P("gx", "gy", "gz"), P())
    out_specs = P("gx", "gy", "gz")
    sizes = tuple(mesh.shape[a] for a in ("gx", "gy", "gz"))
    return jax.shard_map(
        functools.partial(per_device, sizes),
        mesh=mesh, in_specs=in_specs, out_specs=out_specs, check_vma=False,
    )
```

```python
import functools

import jax
import jax.numpy as jnp
from jax import lax
from jax.experimental import pallas as pl
from jax.experimental.pallas import tpu as pltpu
from jax.sharding import PartitionSpec as P

VIEWS = 6
TAPS = 31
HALF = TAPS // 2
ITERS = 2
F32 = jnp.float32
BF16 = jnp.bfloat16
MESH = pl.DeviceIdType.MESH
ORDER = (0, 2, 6, 8, 1, 3, 5, 7)


def dot(a, b):
    return jnp.dot(a, b, preferred_element_type=F32)


def iota(shape, dim):
    return lax.broadcasted_iota(jnp.int32, shape, dim)


def inside(index):
    return jnp.where((index >= 0) & (index < TAPS), index, 127)


def pick(table, index):
    return jnp.take_along_axis(table, index, axis=1)


def kernel(
    sizes, cam_hbm, init_hbm, taps_hbm, out_ref,
    cam_raw, init_ref, taps_ref, in_sem,
    est, ext, quot, inverse, ubuf, kf, kb, bzf, bzb, raw, back, xf, yf, xb, yb, scale,
    picked, place, cam_out, cam_in, rim_in, cam, third, part, flat, acc, code_out0, code_out1, code_out2, code_in0, code_in1, code_in2,
    cam_send, cam_recv, rim_send, rim_recv, e_send, e_recv, f_send, f_recv, g_send, g_recv, c_send, c_recv, m_send, m_recv,
):
    code_out, code_in = (code_out0, code_out1, code_out2), (code_in0, code_in1, code_in2)
    nx, ny, nz = sizes
    gx, gy, gz = lax.axis_index("gx"), lax.axis_index("gy"), lax.axis_index("gz")
    below, above = gz > 0, gz < nz - 1

    fetch = [
        pltpu.make_async_copy(cam_hbm, cam_raw, in_sem.at[0]),
        pltpu.make_async_copy(init_hbm, init_ref, in_sem.at[1]),
        pltpu.make_async_copy(taps_hbm, taps_ref, in_sem.at[2]),
    ]
    for copy in fetch:
        copy.start()

    has_x = (gx > 0, True, gx < nx - 1)
    has_y = (gy > 0, True, gy < ny - 1)
    has_z = (below, True, above)

    def steps(m):
        return m % 9 // 3 - 1, m % 3 - 1, m // 9 - 1

    def place_of(m):
        dx, dy, dz = steps(m)
        return gx + dx, gy + dy, gz + dz

    def there(m):
        flags = [has[d + 1] for has, d in zip((has_x, has_y, has_z), steps(m)) if d]
        return functools.reduce(jnp.logical_and, flags)

    def around(ms, body):
        for m in ms:
            @pl.when(there(m))
            def _():
                body(m)

    everyone = sorted((m for m in range(27) if m != 13), key=lambda m: -sum(map(abs, steps(m))))
    rims = [m for m in everyone if m // 9 != 1]
    sides = [m for m in everyone if m // 9 == 1]

    part_z, part_i = gx >> 2, gx & 3

    def is_self(place):
        return (place[0] == gx) & (place[2] == gz)

    def source(s):
        return 4 * gz + s // 4, gy, s % 4

    def low_source(k):
        return 4 * gz - 1, gy, k

    def high_source(k):
        return 4 * gz + 4, gy, k

    def target(a):
        return a, gy, part_z

    gives_low = (part_i == 3) & (part_z == 1)
    gives_high = (part_i == 0) & (part_z == 2)
    takes_low, takes_high = gz == 2, gz == 1

    def low_target(a):
        return a, gy, part_z + 1

    def high_target(a):
        return a, gy, part_z - 1

    def others(count, place, body):
        for s in range(count):
            @pl.when(jnp.logical_not(is_self(place(s))))
            def _():
                body(s)

    barrier = pltpu.get_barrier_semaphore()

    def greet(place):
        pl.semaphore_signal(barrier, inc=1, device_id=place, device_id_type=MESH)

    others(16, source, lambda s: greet(source(s)))

    @pl.when(takes_low)
    def _():
        others(4, low_source, lambda k: greet(low_source(k)))

    @pl.when(takes_high)
    def _():
        others(4, high_source, lambda k: greet(high_source(k)))

    around(everyone, lambda m: greet(place_of(m)))

    def one(flag):
        return flag.astype(jnp.int32)

    wide = 1 + one(gx > 0) + one(gx < nx - 1)
    tall = 1 + one(gy > 0) + one(gy < ny - 1)
    deep = 1 + one(below) + one(above)
    greetings = wide * tall * deep - 1 + 16 - one(part_z == gz)
    greetings += one(gives_low) * (16 - one(part_z + 1 == gz))
    greetings += one(gives_high) * (16 - one(part_z - 1 == gz))

    with jax.named_scope("zeros"):
        for m in everyone:
            step, lanes = m // 9, slice(m % 9 * 256, m % 9 * 256 + 256)
            rows = (slice(128, 160), slice(0, 128), slice(160, 192))[step]

            for it in range(ITERS):
                sender = m if it or m in (4, 22) else 9 + m % 9

                @pl.when(jnp.logical_not(there(sender)))
                def _():
                    ext[it, rows, lanes] = jnp.zeros((rows.stop - rows.start, 256), BF16)

        quot[:, 160:256, :] = jnp.zeros((VIEWS, 96, 256), BF16)
        place[...] = jnp.zeros(place.shape, BF16)
        raw[...] = jnp.zeros((24, 128), F32)
        ubuf[:, 192:256, :] = jnp.zeros((VIEWS, 64, 512), BF16)

    with jax.named_scope("sort camera"):
        row, col = iota((32, 256), 0), iota((32, 256), 1)
        same_x = row == (col >> 7) * 16 + (col & 15)
        for r in range(2):
            turned = ((col >> 6) & 1) == (r + gz) % 2
            for y in range(4):
                ones = (same_x & turned & (((col >> 4) & 3) == y)).astype(F32).astype(BF16)
                for q in range(4):
                    first = (r * 4 + y) * 128 + q * 32
                    place[q, first : first + 32, :] = ones
    fetch[0].wait()
    with jax.named_scope("sort camera 2"):
        for v in range(VIEWS):
            r, w = v // 3, v % 3
            for y in range(4):
                plane = cam_raw[v, :, y, :]
                lanes = slice((r * 4 + y) * 128, (r * 4 + y + 1) * 128)
                for h in range(2):
                    picked[h, w * 32 : (w + 1) * 32, lanes] = plane[:, h * 128 : (h + 1) * 128]
        for p in range(8):
            block = dot(picked[p // 4], place[p % 4]).astype(BF16)
            for w in range(3):
                cam_out[2 * p, w] = block[w * 32 : (w + 1) * 32, 0:128]
                cam_out[2 * p + 1, w] = block[w * 32 : (w + 1) * 32, 128:256]

    parts = ((0, 1, 6, 7), (2, 3, 4, 5), tuple(range(8)))

    def keep(it, part_of):
        for i, g in enumerate(parts[part_of]):
            first = part_of * 64 + i * 16
            ext[it, first : first + 16, 1024:1280] = est[g * 16 : (g + 1) * 16, :].astype(BF16)

    fetch[1].wait()
    with jax.named_scope("layout in"):
        for y in range(16):
            flat[y * 16 : (y + 1) * 16, :] = init_ref[pl.ds(y, 16, stride=16), :]
        est[...] = flat[...].T
        for part_of in range(2):
            keep(0, part_of)

    with jax.named_scope("entry wait"):
        pl.semaphore_wait(barrier, greetings)

    slot = part_i * 4 + gz

    def cam_copy(a, s):
        return pltpu.make_async_remote_copy(
            src_ref=cam_out.at[a],
            dst_ref=cam_in.at[s],
            send_sem=cam_send.at[a],
            recv_sem=cam_recv.at[s],
            device_id=target(a),
            device_id_type=MESH,
        )

    def rim_copy(high, a, k):
        first = 0 if high else 16
        return pltpu.make_async_remote_copy(
            src_ref=cam_out.at[a, :, pl.ds(first, 16), :],
            dst_ref=rim_in.at[int(high), k],
            send_sem=rim_send.at[int(high), a],
            recv_sem=rim_recv.at[int(high), k],
            device_id=high_target(a) if high else low_target(a),
            device_id_type=MESH,
        )

    def e_copy(it, m, at):
        first, count, to = ((0, 32, 160), (0, 64 if it else 128, 0), (32, 32, 128))[m // 9]
        return pltpu.make_async_remote_copy(
            src_ref=ext.at[it, pl.ds(first, count), pl.ds(1024, 256)],
            dst_ref=ext.at[it, pl.ds(to, count), pl.ds(at % 9 * 256, 256)],
            send_sem=e_send.at[it, m],
            recv_sem=e_recv.at[it, at],
            device_id=place_of(m),
            device_id_type=MESH,
        )

    def middle_copy(m, at):
        return pltpu.make_async_remote_copy(
            src_ref=ext.at[1, pl.ds(64, 64), pl.ds(1024, 256)],
            dst_ref=ext.at[1, pl.ds(64, 64), pl.ds(at % 9 * 256, 256)],
            send_sem=g_send.at[m - 9],
            recv_sem=g_recv.at[at - 9],
            device_id=place_of(m),
            device_id_type=MESH,
        )

    def forward_copy(m, at):
        return pltpu.make_async_remote_copy(
            src_ref=ext.at[0, pl.ds(128, 64), pl.ds(1024, 256)],
            dst_ref=ext.at[0, pl.ds(128, 64), pl.ds(at % 9 * 256, 256)],
            send_sem=f_send.at[m - 9],
            recv_sem=f_recv.at[at - 9],
            device_id=place_of(m),
            device_id_type=MESH,
        )

    def send_estimate(it, ms):
        around(ms, lambda m: e_copy(it, m, 26 - m).start())

    def wait_estimate(it, ms):
        around(ms, lambda m: e_copy(it, m, m).wait_recv())

    vertical = (4, 22)
    with jax.named_scope("send rims"):
        send_estimate(0, vertical)

    with jax.named_scope("send camera"):
        @pl.when(part_z == gz)
        def _():
            cam_in[slot] = cam_out[gx]

        others(16, target, lambda a: cam_copy(a, slot).start())

        @pl.when(gives_low)
        def _():
            @pl.when(part_z + 1 == gz)
            def _():
                rim_in[0, gz] = cam_out[gx, :, 16:32, :]

            others(16, low_target, lambda a: rim_copy(False, a, gz).start())

        @pl.when(gives_high)
        def _():
            @pl.when(part_z - 1 == gz)
            def _():
                rim_in[1, gz] = cam_out[gx, :, 0:16, :]

            others(16, high_target, lambda a: rim_copy(True, a, gz).start())

    with jax.named_scope("send estimate"):
        send_estimate(0, sides)

    fetch[2].wait()
    with jax.named_scope("taps"):
        for v in range(VIEWS):
            for a in range(3):
                raw[a * 8 + v : a * 8 + v + 1, 0:TAPS] = taps_ref[v, a : a + 1, :]
        total = jnp.sum(raw[...], axis=1, keepdims=True)
        total = jnp.where((iota((24, 1), 0) & 7) < VIEWS, total, 1.0)
        back[...] = (raw[...] / total).astype(BF16).astype(F32)

    with jax.named_scope("tables"):
        def tables(i, carry):
            lane = iota((8, 128), 1)
            for k in range(6):
                j = i * 6 + k
                rows = pl.ds(pl.multiple_of(j * 8, 8), 8)
                x = lane & 15
                xf[rows, :] = pick(raw[0:8, :], inside(x + 31 - j))
                xb[rows, :] = pick(back[0:8, :], inside(j - 1 - x))
                for half in range(2):
                    y = (lane >> 4) + 8 * half
                    yf[half, rows, :] = pick(raw[8:16, :], inside(y + 31 - j))
                    yb[half, rows, :] = pick(back[8:16, :], inside(j - 1 - y))
            return carry

        lax.fori_loop(0, 8, tables, 0)

    def rows_of(table, j, v):
        return table[pl.ds(j * 128 + v, 16, stride=8), :]

    with jax.named_scope("products"):
        def products(i, carry):
            v, n = i // 9, i % 9
            dx, dy = n // 3, n % 3
            x = rows_of(xf, dx, v)
            for half in range(2):
                ys = rows_of(yf.at[half], dy, v)
                for y in range(16):
                    kf[v, pl.ds(pl.multiple_of(n * 256 + y * 16, 16), 16), half * 128 : (half + 1) * 128] = (
                        x * ys[y : y + 1, :]
                    ).astype(BF16)
            return carry

        lax.fori_loop(0, 9 * VIEWS, products, 0)

    with jax.named_scope("forward rims"):
        wait_estimate(0, vertical)
        around(sides, lambda m: forward_copy(m, 26 - m).start())

    with jax.named_scope("bands"):
        def bands(block, carry):
            r = iota((8, 128), 0) + block * 8
            z_out = jnp.where(r < 128, r, jnp.where(r < 144, r - 144, r - 16))
            rows = pl.ds(pl.multiple_of(block * 8, 8), 8)
            lane = iota((8, 128), 1)
            near = jnp.where(lane < 32, lane, jnp.where(lane < 64, lane + 64, lane - 32))
            far = jnp.where(lane < 32, lane - 32, jnp.where(lane < 64, lane + 96, 4096))
            for half, z_in in enumerate((near, far)):
                index = inside(z_out - z_in + HALF)
                for v in range(VIEWS):
                    band_f = jnp.broadcast_to(raw[16 + v : 17 + v, :], (8, 128))
                    bzf[v, rows, half * 128 : (half + 1) * 128] = pick(band_f, index)
            return carry

        lax.fori_loop(0, 20, bands, 0)

        def back_bands(block, carry):
            z_out = iota((8, 128), 0) + block * 8
            rows = pl.ds(pl.multiple_of(block * 8, 8), 8)
            lane = iota((8, 128), 1)
            far = jnp.where(lane < 16, lane - 16, jnp.where(lane < 32, lane + 112, 1024))
            for half, z_in in enumerate((lane, far)):
                index = inside(z_in - z_out + HALF)
                for v in range(VIEWS):
                    band_b = jnp.broadcast_to(back[16 + v : 17 + v, :], (8, 128))
                    bzb[v, rows, half * 128 : (half + 1) * 128] = pick(band_b, index)
            return carry

        lax.fori_loop(0, 16, back_bands, 0)

    with jax.named_scope("scale"):
        fx, fy, fz = raw[0:8, :], raw[8:16, :], raw[16:24, :]
        bx, by = back[0:8, :], back[8:16, :]
        f_sum, b_sum = jnp.zeros((8, 128), F32), jnp.zeros((8, 128), F32)
        for t in range(TAPS):
            f_sum += (fx[:, t : t + 1] * fy).astype(BF16).astype(F32)
            b_sum += (bx[:, t : t + 1] * by).astype(BF16).astype(F32)

        def lanes_sum(a):
            return jnp.sum(a, axis=1, keepdims=True)

        f_scale = lanes_sum(f_sum) * lanes_sum(fz.astype(BF16).astype(F32))
        b_total = jnp.where(iota((8, 1), 0) < VIEWS, lanes_sum(b_sum), 1.0)
        b_scale = lanes_sum(bx) * lanes_sum(by) / b_total
        scale[0:8, :] = jnp.broadcast_to(f_scale, (8, 128))
        scale[8:16, :] = jnp.broadcast_to(b_scale, (8, 128))

    with jax.named_scope("back products"):
        def back_products(i, carry):
            v, n = i // 9, i % 9
            dx, dy = n // 3, n % 3
            x = rows_of(xb, 2 - dx, v)
            for half in range(2):
                ys = rows_of(yb.at[half], 2 - dy, v)
                for y in range(16):
                    kb[n, pl.ds(pl.multiple_of(v * 256 + y * 16, 16), 16), half * 128 : (half + 1) * 128] = (
                        x * ys[y : y + 1, :]
                    ).astype(BF16)
            return carry

        lax.fori_loop(0, 9 * VIEWS, back_products, 0)

    def factor(row):
        value = scale[row : row + 1, :]
        return jnp.concatenate([value, value], axis=1)

    def blur(it):
        for v in range(VIEWS):
            u = dot(ext[it], kf[v])
            high = u.astype(BF16)
            ubuf[v, 0:192, 0:256] = high
            ubuf[v, 0:192, 256:512] = (u - high.astype(F32)).astype(BF16)
        for v in range(VIEWS):
            halves = dot(bzf[v].astype(BF16), ubuf[v])
            inverse[v] = factor(v) / (halves[:, 0:256] + halves[:, 256:512])

    def quotients():
        row = iota((32, 256), 0)
        seen = jnp.where(row < 16, one(below), one(above)) > 0
        for v in range(VIEWS):
            quot[v, 0:128, :] = (cam[v, 0:128, :].astype(F32) * inverse[v, 0:128, :]).astype(BF16)
            rim = jnp.where(seen, cam[v, 128:160, :].astype(F32) * inverse[v, 128:160, :], 0.0)
            quot[v, 128:160, :] = rim.astype(BF16)

    with jax.named_scope("wait estimate"):
        wait_estimate(0, sides)
        around(sides, lambda m: forward_copy(m, m).wait_recv())
    with jax.named_scope("blur"):
        blur(0)

    def mate_copy(first, to):
        return pltpu.make_async_remote_copy(
            src_ref=cam.at[:, pl.ds(first, 16), :],
            dst_ref=cam.at[:, pl.ds(to, 16), :],
            send_sem=m_send,
            recv_sem=m_recv,
            device_id=(gx, gy, gz ^ 1),
            device_id_type=MESH,
        )

    def pair(r, even, odd):
        low = iota(even.shape, 1) < 64
        even, odd = even.astype(F32), odd.astype(F32)
        if r == 0:
            return jnp.where(low, even, odd).astype(BF16)
        return pltpu.roll(jnp.where(low, odd, even), 64, 1).astype(BF16)

    def assemble(z):
        for k in range(4):
            @pl.when(jnp.logical_not(is_self(source(4 * z + k))))
            def _():
                cam_copy(0, 4 * z + k).wait_recv()
        for v in range(VIEWS):
            r, w = v // 3, v % 3
            for t in range(2):
                cam[v, z * 32 : (z + 1) * 32, t * 128 : (t + 1) * 128] = pair(
                    r, cam_in[z * 4 + 2 * t, w], cam_in[z * 4 + 2 * t + 1, w]
                )

    def assemble_rim(high):
        place = high_source if high else low_source
        others(4, place, lambda k: rim_copy(high, 0, k).wait_recv())
        for v in range(VIEWS):
            r, w = v // 3, v % 3
            for t in range(2):
                cam[v, 128 + high * 16 : 144 + high * 16, t * 128 : (t + 1) * 128] = pair(
                    r, rim_in[high, 2 * t, w], rim_in[high, 2 * t + 1, w]
                )

    even = (gz & 1) == 0
    with jax.named_scope("camera in"):
        @pl.when(even)
        def _():
            assemble(3)
            mate_copy(112, 128).start()
            assemble(0)

        @pl.when(jnp.logical_not(even))
        def _():
            assemble(0)
            mate_copy(0, 144).start()
            assemble(3)

        assemble(1)
        assemble(2)

        @pl.when(takes_low)
        def _():
            assemble_rim(0)

        @pl.when(takes_high)
        def _():
            assemble_rim(1)

        @pl.when(even)
        def _():
            mate_copy(0, 144).wait_recv()

        @pl.when(jnp.logical_not(even))
        def _():
            mate_copy(112, 128).wait_recv()

    def c_copy(part_of, n, at):
        return pltpu.make_async_remote_copy(
            src_ref=code_out[part_of].at[n],
            dst_ref=code_in[part_of].at[at],
            send_sem=c_send.at[part_of, n],
            recv_sem=c_recv.at[part_of, at],
            device_id=place_of(9 + n),
            device_id_type=MESH,
        )

    def encode(work, part_of, n):
        groups, out = parts[part_of], code_out[part_of]
        base = [work[g * 16 + 8 : g * 16 + 9, :] for g in groups]
        base = jnp.concatenate(base + [jnp.zeros((16 - len(groups), 256), F32)], axis=0).astype(BF16)
        out[n, len(groups) * 16 : len(groups) * 16 + 16, :] = base
        base = base.astype(F32)
        for i, g in enumerate(groups):
            out[n, i * 16 : (i + 1) * 16, :] = (work[g * 16 : (g + 1) * 16, :] - base[i : i + 1, :]).astype(BF16)

    def collect(part_of):
        groups, code = parts[part_of], code_in[part_of]
        for n in reversed(ORDER):
            @pl.when(there(9 + n))
            def _():
                c_copy(part_of, n, n).wait_recv()
                with jax.named_scope("add"):
                    base = code[n, len(groups) * 16 : len(groups) * 16 + 16, :].astype(F32)
                    for i, g in enumerate(groups):
                        rows = slice(g * 16, (g + 1) * 16)
                        acc[rows, :] += code[n, i * 16 : (i + 1) * 16, :].astype(F32) + base[i : i + 1, :]

    def update(part_of):
        for g in parts[part_of]:
            rows = slice(g * 16, (g + 1) * 16)
            est[rows, :] = est[rows, :] * acc[rows, :] / VIEWS

    def sent():
        around(vertical, lambda m: e_copy(0, m, 26 - m).wait_send())
        around(sides, lambda m: e_copy(0, m, 26 - m).wait_send())
        around(sides, lambda m: forward_copy(m, 26 - m).wait_send())
        for it in range(1, ITERS):
            around(everyone, lambda m: e_copy(it, m, 26 - m).wait_send())
            around(sides, lambda m: middle_copy(m, 26 - m).wait_send())
        for part_of in range(2):
            around(sides, lambda m: c_copy(part_of, m - 9, 17 - m).wait_send())

        @pl.when(even)
        def _():
            mate_copy(112, 128).wait_send()

        @pl.when(jnp.logical_not(even))
        def _():
            mate_copy(0, 144).wait_send()
        others(16, target, lambda a: cam_copy(a, slot).wait_send())

        @pl.when(gives_low)
        def _():
            others(16, low_target, lambda a: rim_copy(False, a, gz).wait_send())

        @pl.when(gives_high)
        def _():
            others(16, high_target, lambda a: rim_copy(True, a, gz).wait_send())

    for it in range(ITERS):
        if it > 0:
            with jax.named_scope("wait estimate 2"):
                wait_estimate(it, everyone)
                around(sides, lambda m: middle_copy(m, m).wait_recv())
            with jax.named_scope("blur 2"):
                blur(it)
        with jax.named_scope("quotients"):
            quotients()
        with jax.named_scope("third"):
            for v in range(VIEWS):
                value = dot(bzb[v].astype(BF16), quot[v]) * factor(8 + v)
                third[:, v * 256 : (v + 1) * 256] = value.astype(BF16)

        last = it == ITERS - 1
        with jax.named_scope("partial sums"):
            for count, n in enumerate(ORDER):
                @pl.when(there(9 + n))
                def _():
                    work = part.at[count % 2]
                    work[...] = dot(third[...], kb[n])
                    if last:
                        encode(work, 2, n)
                        c_copy(2, n, 8 - n).start()
                    else:
                        encode(work, 0, n)
                        c_copy(0, n, 8 - n).start()
                        encode(work, 1, n)
            if not last:
                for n in ORDER:
                    @pl.when(there(9 + n))
                    def _():
                        c_copy(1, n, 8 - n).start()

        with jax.named_scope("own sum"):
            acc[...] = dot(third[...], kb[4])
        if last:
            with jax.named_scope("sent"):
                sent()
            collect(2)
            update(2)
        else:
            collect(0)
            update(0)
            keep(it + 1, 0)
            send_estimate(it + 1, everyone)
            collect(1)
            update(1)
            keep(it + 1, 1)
            around(sides, lambda m: middle_copy(m, 26 - m).start())

    with jax.named_scope("layout out"):
        flat[...] = est[...].T
        for y in range(16):
            out_ref[pl.ds(y, 16, stride=16), :] = flat[y * 16 : (y + 1) * 16, :]

    for n in ORDER:
        @pl.when(there(9 + n))
        def _():
            c_copy(2, n, 8 - n).wait_send()


def per_device(sizes, camera, initial, psf_taps):
    held = pl.BlockSpec(memory_space=pl.ANY)
    dma = pltpu.SemaphoreType.DMA
    rows = initial.reshape(256, 128)
    result = pl.pallas_call(
        functools.partial(kernel, sizes),
        out_shape=jax.ShapeDtypeStruct((256, 128), F32),
        in_specs=[held, held, held],
        out_specs=pl.BlockSpec(memory_space=pltpu.VMEM),
        scratch_shapes=[
            pltpu.VMEM((VIEWS, 32, 4, 256), BF16),
            pltpu.VMEM((256, 128), F32),
            pltpu.VMEM((VIEWS, 3, TAPS), F32),
            dma((3,)),
            pltpu.VMEM((128, 256), F32),
            pltpu.VMEM((ITERS, 192, 9 * 256), BF16),
            pltpu.VMEM((VIEWS, 256, 256), BF16),
            pltpu.VMEM((VIEWS, 160, 256), F32),
            pltpu.VMEM((VIEWS, 256, 512), BF16),
            pltpu.VMEM((VIEWS, 9 * 256, 256), BF16),
            pltpu.VMEM((9, VIEWS * 256, 256), BF16),
            pltpu.VMEM((VIEWS, 160, 256), F32),
            pltpu.VMEM((VIEWS, 128, 256), F32),
            pltpu.VMEM((24, 128), F32),
            pltpu.VMEM((24, 128), F32),
            pltpu.VMEM((48 * 8, 128), F32),
            pltpu.VMEM((2, 48 * 8, 128), F32),
            pltpu.VMEM((48 * 8, 128), F32),
            pltpu.VMEM((2, 48 * 8, 128), F32),
            pltpu.VMEM((16, 128), F32),
            pltpu.VMEM((2, 96, 1024), BF16),
            pltpu.VMEM((4, 1024, 256), BF16),
            pltpu.VMEM((16, 3, 32, 128), BF16),
            pltpu.VMEM((16, 3, 32, 128), BF16),
            pltpu.VMEM((2, 4, 3, 16, 128), BF16),
            pltpu.VMEM((VIEWS, 160, 256), BF16),
            pltpu.VMEM((128, VIEWS * 256), BF16),
            pltpu.VMEM((2, 128, 256), F32),
            pltpu.VMEM((256, 128), F32),
            pltpu.VMEM((128, 256), F32),
            *[pltpu.VMEM((9, rows, 256), BF16) for rows in (80, 80, 144) * 2],
            dma((16,)), dma((16,)),
            dma((2, 16)), dma((2, 4)),
            dma((ITERS, 27)), dma((ITERS, 27)),
            dma((9,)), dma((9,)),
            dma((9,)), dma((9,)),
            dma((3, 9)), dma((3, 9)),
            dma(()), dma(()),
        ],
        compiler_params=pltpu.CompilerParams(
            collective_id=0, has_side_effects=True, vmem_limit_bytes=55040 * 1024
        ),
    )(camera, rows, psf_taps)
    return result.reshape(initial.shape)


def solution(mesh):
    in_specs = (P(None, "gx", ("gy", "gz"), None), P("gx", "gy", "gz"), P())
    out_specs = P("gx", "gy", "gz")
    sizes = tuple(mesh.shape[a] for a in ("gx", "gy", "gz"))
    return jax.shard_map(
        functools.partial(per_device, sizes),
        mesh=mesh, in_specs=in_specs, out_specs=out_specs, check_vma=False,
    )
```

```python
import functools

import jax
import jax.numpy as jnp
from jax import lax
from jax.experimental import pallas as pl
from jax.experimental.pallas import tpu as pltpu
from jax.sharding import PartitionSpec as P

VIEWS = 6
TAPS = 31
HALF = TAPS // 2
ITERS = 2
F32 = jnp.float32
BF16 = jnp.bfloat16
MESH = pl.DeviceIdType.MESH
ORDER = (0, 2, 6, 8, 1, 3, 5, 7)


def dot(a, b):
    return jnp.dot(a, b, preferred_element_type=F32)


def iota(shape, dim):
    return lax.broadcasted_iota(jnp.int32, shape, dim)


def inside(index):
    return jnp.where((index >= 0) & (index < TAPS), index, 127)


def pick(table, index):
    return jnp.take_along_axis(table, index, axis=1)


def kernel(
    sizes, cam_hbm, init_hbm, taps_hbm, out_ref,
    cam_raw, init_ref, taps_ref, in_sem,
    est, ext, quot, inverse, ubuf, kf, kb, bzf, bzb, raw, back, xf, yf, xb, yb, scale,
    picked, place, cam_out, cam_in, rim_in, cam, third, part, flat, acc, early, bases, code_out0, code_out1, code_out2, code_in0, code_in1, code_in2,
    cam_send, cam_recv, rim_send, rim_recv, e_send, e_recv, g_send, g_recv, c_send, c_recv, m_send, m_recv,
):
    code_out, code_in = (code_out0, code_out1, code_out2), (code_in0, code_in1, code_in2)
    nx, ny, nz = sizes
    gx, gy, gz = lax.axis_index("gx"), lax.axis_index("gy"), lax.axis_index("gz")
    below, above = gz > 0, gz < nz - 1

    fetch = [
        pltpu.make_async_copy(cam_hbm, cam_raw, in_sem.at[0]),
        pltpu.make_async_copy(init_hbm, init_ref, in_sem.at[1]),
        pltpu.make_async_copy(taps_hbm, taps_ref, in_sem.at[2]),
    ]
    for copy in fetch:
        copy.start()

    has_x = (gx > 0, True, gx < nx - 1)
    has_y = (gy > 0, True, gy < ny - 1)
    has_z = (below, True, above)

    def steps(m):
        return m % 9 // 3 - 1, m % 3 - 1, m // 9 - 1

    def place_of(m):
        dx, dy, dz = steps(m)
        return gx + dx, gy + dy, gz + dz

    def there(m):
        flags = [has[d + 1] for has, d in zip((has_x, has_y, has_z), steps(m)) if d]
        return functools.reduce(jnp.logical_and, flags)

    def around(ms, body):
        for m in ms:
            @pl.when(there(m))
            def _():
                body(m)

    everyone = sorted((m for m in range(27) if m != 13), key=lambda m: -sum(map(abs, steps(m))))
    rims = [m for m in everyone if m // 9 != 1]
    sides = [m for m in everyone if m // 9 == 1]

    part_z, part_i = gx >> 2, gx & 3

    def is_self(place):
        return (place[0] == gx) & (place[2] == gz)

    def source(s):
        return 4 * gz + s // 4, gy, s % 4

    def low_source(k):
        return 4 * gz - 1, gy, k

    def high_source(k):
        return 4 * gz + 4, gy, k

    def target(a):
        return a, gy, part_z

    gives_low = (part_i == 3) & (part_z == 1)
    gives_high = (part_i == 0) & (part_z == 2)
    takes_low, takes_high = gz == 2, gz == 1

    def low_target(a):
        return a, gy, part_z + 1

    def high_target(a):
        return a, gy, part_z - 1

    def others(count, place, body):
        for s in range(count):
            @pl.when(jnp.logical_not(is_self(place(s))))
            def _():
                body(s)

    barrier = pltpu.get_barrier_semaphore()

    def greet(place):
        pl.semaphore_signal(barrier, inc=1, device_id=place, device_id_type=MESH)

    others(16, source, lambda s: greet(source(s)))

    @pl.when(takes_low)
    def _():
        others(4, low_source, lambda k: greet(low_source(k)))

    @pl.when(takes_high)
    def _():
        others(4, high_source, lambda k: greet(high_source(k)))

    around(everyone, lambda m: greet(place_of(m)))

    def one(flag):
        return flag.astype(jnp.int32)

    wide = 1 + one(gx > 0) + one(gx < nx - 1)
    tall = 1 + one(gy > 0) + one(gy < ny - 1)
    deep = 1 + one(below) + one(above)
    greetings = wide * tall * deep - 1 + 16 - one(part_z == gz)
    greetings += one(gives_low) * (16 - one(part_z + 1 == gz))
    greetings += one(gives_high) * (16 - one(part_z - 1 == gz))

    with jax.named_scope("zeros"):
        for m in everyone:
            step, lanes = m // 9, slice(m % 9 * 256, m % 9 * 256 + 256)
            rows = (slice(128, 160), slice(0, 128), slice(160, 192))[step]

            for it in range(ITERS):
                @pl.when(jnp.logical_not(there(m)))
                def _():
                    ext[it, rows, lanes] = jnp.zeros((rows.stop - rows.start, 256), BF16)

        quot[:, 160:256, :] = jnp.zeros((VIEWS, 96, 256), BF16)
        place[...] = jnp.zeros(place.shape, BF16)
        raw[...] = jnp.zeros((24, 128), F32)
        ubuf[:, 192:256, :] = jnp.zeros((VIEWS, 64, 512), BF16)

    with jax.named_scope("sort camera"):
        row, col = iota((32, 256), 0), iota((32, 256), 1)
        same_x = row == (col >> 7) * 16 + (col & 15)
        for r in range(2):
            turned = ((col >> 6) & 1) == (r + gz) % 2
            for y in range(4):
                ones = (same_x & turned & (((col >> 4) & 3) == y)).astype(F32).astype(BF16)
                for q in range(4):
                    first = (r * 4 + y) * 128 + q * 32
                    place[q, first : first + 32, :] = ones
    fetch[0].wait()
    with jax.named_scope("sort camera 2"):
        for v in range(VIEWS):
            r, w = v % 2, v // 2
            for y in range(4):
                plane = cam_raw[v, :, y, :]
                lanes = slice((r * 4 + y) * 128, (r * 4 + y + 1) * 128)
                for h in range(2):
                    picked[h, w * 32 : (w + 1) * 32, lanes] = plane[:, h * 128 : (h + 1) * 128]
        for p in range(8):
            block = dot(picked[p // 4], place[p % 4]).astype(BF16)
            for w in range(3):
                cam_out[2 * p, w] = block[w * 32 : (w + 1) * 32, 0:128]
                cam_out[2 * p + 1, w] = block[w * 32 : (w + 1) * 32, 128:256]

    parts = ((0, 1, 6, 7), (2, 3, 4, 5), tuple(range(8)))

    def keep(it, part_of):
        for i, g in enumerate(parts[part_of]):
            first = part_of * 64 + i * 16
            ext[it, first : first + 16, 1024:1280] = est[g * 16 : (g + 1) * 16, :].astype(BF16)

    fetch[1].wait()
    with jax.named_scope("layout in"):
        for y in range(16):
            flat[y * 16 : (y + 1) * 16, :] = init_ref[pl.ds(y, 16, stride=16), :]
        est[...] = flat[...].T
        for part_of in range(2):
            keep(0, part_of)

    with jax.named_scope("entry wait"):
        pl.semaphore_wait(barrier, greetings)

    slot = part_i * 4 + gz

    pieces, views = (pl.ds(0, 2), pl.ds(2, 1)), (range(0, 4), range(4, 6))

    def cam_copy(piece, a, s):
        return pltpu.make_async_remote_copy(
            src_ref=cam_out.at[a, pieces[piece]],
            dst_ref=cam_in.at[s, pieces[piece]],
            send_sem=cam_send.at[piece, a],
            recv_sem=cam_recv.at[piece, s],
            device_id=target(a),
            device_id_type=MESH,
        )

    def rim_copy(piece, high, a, k):
        first = 0 if high else 16
        return pltpu.make_async_remote_copy(
            src_ref=cam_out.at[a, pieces[piece], pl.ds(first, 16), :],
            dst_ref=rim_in.at[int(high), k, pieces[piece]],
            send_sem=rim_send.at[piece, int(high), a],
            recv_sem=rim_recv.at[piece, int(high), k],
            device_id=high_target(a) if high else low_target(a),
            device_id_type=MESH,
        )

    def e_copy(it, m, at):
        first, count, to = ((0, 32, 160), (0, 64 if it else 128, 0), (32, 32, 128))[m // 9]
        return pltpu.make_async_remote_copy(
            src_ref=ext.at[it, pl.ds(first, count), pl.ds(1024, 256)],
            dst_ref=ext.at[it, pl.ds(to, count), pl.ds(at % 9 * 256, 256)],
            send_sem=e_send.at[it, m],
            recv_sem=e_recv.at[it, at],
            device_id=place_of(m),
            device_id_type=MESH,
        )

    def middle_copy(m, at):
        return pltpu.make_async_remote_copy(
            src_ref=ext.at[1, pl.ds(64, 64), pl.ds(1024, 256)],
            dst_ref=ext.at[1, pl.ds(64, 64), pl.ds(at % 9 * 256, 256)],
            send_sem=g_send.at[m - 9],
            recv_sem=g_recv.at[at - 9],
            device_id=place_of(m),
            device_id_type=MESH,
        )

    def send_estimate(it, ms):
        around(ms, lambda m: e_copy(it, m, 26 - m).start())

    def wait_estimate(it, ms):
        around(ms, lambda m: e_copy(it, m, m).wait_recv())

    with jax.named_scope("send estimate"):
        send_estimate(0, everyone)

    with jax.named_scope("send camera"):
        @pl.when(part_z == gz)
        def _():
            cam_in[slot] = cam_out[gx]

        for piece in range(2):
            others(16, target, lambda a: cam_copy(piece, a, slot).start())

            @pl.when(gives_low)
            def _():
                others(16, low_target, lambda a: rim_copy(piece, False, a, gz).start())

            @pl.when(gives_high)
            def _():
                others(16, high_target, lambda a: rim_copy(piece, True, a, gz).start())

        @pl.when(gives_low & (part_z + 1 == gz))
        def _():
            rim_in[0, gz] = cam_out[gx, :, 16:32, :]

        @pl.when(gives_high & (part_z - 1 == gz))
        def _():
            rim_in[1, gz] = cam_out[gx, :, 0:16, :]

    fetch[2].wait()
    with jax.named_scope("taps"):
        for v in range(VIEWS):
            for a in range(3):
                raw[a * 8 + v : a * 8 + v + 1, 0:TAPS] = taps_ref[v, a : a + 1, :]
        total = jnp.sum(raw[...], axis=1, keepdims=True)
        total = jnp.where((iota((24, 1), 0) & 7) < VIEWS, total, 1.0)
        back[...] = (raw[...] / total).astype(BF16).astype(F32)

    with jax.named_scope("tables"):
        def tables(i, carry):
            lane = iota((8, 128), 1)
            for k in range(6):
                j = i * 6 + k
                rows = pl.ds(pl.multiple_of(j * 8, 8), 8)
                x = lane & 15
                xf[rows, :] = pick(raw[0:8, :], inside(x + 31 - j))
                xb[rows, :] = pick(back[0:8, :], inside(j - 1 - x))
                for half in range(2):
                    y = (lane >> 4) + 8 * half
                    yf[half, rows, :] = pick(raw[8:16, :], inside(y + 31 - j))
                    yb[half, rows, :] = pick(back[8:16, :], inside(j - 1 - y))
            return carry

        lax.fori_loop(0, 8, tables, 0)

    def rows_of(table, j, v):
        return table[pl.ds(j * 128 + v, 16, stride=8), :]

    with jax.named_scope("products"):
        def products(i, carry):
            v, n = i // 9, i % 9
            dx, dy = n // 3, n % 3
            x = rows_of(xf, dx, v)
            for half in range(2):
                ys = rows_of(yf.at[half], dy, v)
                for y in range(16):
                    kf[v, pl.ds(pl.multiple_of(n * 256 + y * 16, 16), 16), half * 128 : (half + 1) * 128] = (
                        x * ys[y : y + 1, :]
                    ).astype(BF16)
            return carry

        lax.fori_loop(0, 9 * VIEWS, products, 0)

    with jax.named_scope("bands"):
        def bands(block, carry):
            r = iota((8, 128), 0) + block * 8
            z_out = jnp.where(r < 128, r, jnp.where(r < 144, r - 144, r - 16))
            rows = pl.ds(pl.multiple_of(block * 8, 8), 8)
            lane = iota((8, 128), 1)
            near = jnp.where(lane < 32, lane, jnp.where(lane < 64, lane + 64, lane - 32))
            far = jnp.where(lane < 32, lane - 32, jnp.where(lane < 64, lane + 96, 4096))
            for half, z_in in enumerate((near, far)):
                index = inside(z_out - z_in + HALF)
                for v in range(VIEWS):
                    band_f = jnp.broadcast_to(raw[16 + v : 17 + v, :], (8, 128))
                    bzf[v, rows, half * 128 : (half + 1) * 128] = pick(band_f, index)
            return carry

        lax.fori_loop(0, 20, bands, 0)

        def back_bands(block, carry):
            z_out = iota((8, 128), 0) + block * 8
            rows = pl.ds(pl.multiple_of(block * 8, 8), 8)
            lane = iota((8, 128), 1)
            far = jnp.where(lane < 16, lane - 16, jnp.where(lane < 32, lane + 112, 1024))
            for half, z_in in enumerate((lane, far)):
                index = inside(z_in - z_out + HALF)
                for v in range(VIEWS):
                    band_b = jnp.broadcast_to(back[16 + v : 17 + v, :], (8, 128))
                    bzb[v, rows, half * 128 : (half + 1) * 128] = pick(band_b, index)
            return carry

        lax.fori_loop(0, 16, back_bands, 0)

    with jax.named_scope("scale"):
        fx, fy, fz = raw[0:8, :], raw[8:16, :], raw[16:24, :]
        bx, by = back[0:8, :], back[8:16, :]
        f_sum, b_sum = jnp.zeros((8, 128), F32), jnp.zeros((8, 128), F32)
        for t in range(TAPS):
            f_sum += (fx[:, t : t + 1] * fy).astype(BF16).astype(F32)
            b_sum += (bx[:, t : t + 1] * by).astype(BF16).astype(F32)

        def lanes_sum(a):
            return jnp.sum(a, axis=1, keepdims=True)

        f_scale = lanes_sum(f_sum) * lanes_sum(fz.astype(BF16).astype(F32))
        b_total = jnp.where(iota((8, 1), 0) < VIEWS, lanes_sum(b_sum), 1.0)
        b_scale = lanes_sum(bx) * lanes_sum(by) / b_total
        scale[0:8, :] = jnp.broadcast_to(f_scale, (8, 128))
        scale[8:16, :] = jnp.broadcast_to(b_scale, (8, 128))

    with jax.named_scope("back products"):
        def back_products(i, carry):
            v, n = i // 9, i % 9
            dx, dy = n // 3, n % 3
            x = rows_of(xb, 2 - dx, v)
            for half in range(2):
                ys = rows_of(yb.at[half], 2 - dy, v)
                for y in range(16):
                    kb[n, pl.ds(pl.multiple_of(v * 256 + y * 16, 16), 16), half * 128 : (half + 1) * 128] = (
                        x * ys[y : y + 1, :]
                    ).astype(BF16)
            return carry

        lax.fori_loop(0, 9 * VIEWS, back_products, 0)

    def factor(row):
        value = scale[row : row + 1, :]
        return jnp.concatenate([value, value], axis=1)

    def blur(it):
        for v in range(VIEWS):
            u = dot(ext[it], kf[v])
            high = u.astype(BF16)
            ubuf[v, 0:192, 0:256] = high
            ubuf[v, 0:192, 256:512] = (u - high.astype(F32)).astype(BF16)
        for v in range(VIEWS):
            halves = dot(bzf[v].astype(BF16), ubuf[v])
            inverse[v] = factor(v) / (halves[:, 0:256] + halves[:, 256:512])

    def quotients(some):
        row = iota((32, 256), 0)
        seen = jnp.where(row < 16, one(below), one(above)) > 0
        for v in some:
            quot[v, 0:128, :] = (cam[v, 0:128, :].astype(F32) * inverse[v, 0:128, :]).astype(BF16)
            rim = jnp.where(seen, cam[v, 128:160, :].astype(F32) * inverse[v, 128:160, :], 0.0)
            quot[v, 128:160, :] = rim.astype(BF16)

    with jax.named_scope("wait estimate"):
        wait_estimate(0, everyone)
    with jax.named_scope("blur"):
        blur(0)

    def mate_copy(piece, first, to):
        some = pl.ds(views[piece].start, len(views[piece]))
        return pltpu.make_async_remote_copy(
            src_ref=cam.at[some, pl.ds(first, 16), :],
            dst_ref=cam.at[some, pl.ds(to, 16), :],
            send_sem=m_send.at[piece],
            recv_sem=m_recv.at[piece],
            device_id=(gx, gy, gz ^ 1),
            device_id_type=MESH,
        )

    def pair(r, even, odd):
        low = iota(even.shape, 1) < 64
        even, odd = even.astype(F32), odd.astype(F32)
        if r == 0:
            return jnp.where(low, even, odd).astype(BF16)
        return pltpu.roll(jnp.where(low, odd, even), 64, 1).astype(BF16)

    def assemble(piece, z):
        for k in range(4):
            @pl.when(jnp.logical_not(is_self(source(4 * z + k))))
            def _():
                cam_copy(piece, 0, 4 * z + k).wait_recv()
        for v in views[piece]:
            r, w = v % 2, v // 2
            for t in range(2):
                cam[v, z * 32 : (z + 1) * 32, t * 128 : (t + 1) * 128] = pair(
                    r, cam_in[z * 4 + 2 * t, w], cam_in[z * 4 + 2 * t + 1, w]
                )

    def assemble_rim(piece, high):
        place = high_source if high else low_source
        others(4, place, lambda k: rim_copy(piece, high, 0, k).wait_recv())
        for v in views[piece]:
            r, w = v % 2, v // 2
            for t in range(2):
                cam[v, 128 + high * 16 : 144 + high * 16, t * 128 : (t + 1) * 128] = pair(
                    r, rim_in[high, 2 * t, w], rim_in[high, 2 * t + 1, w]
                )

    even = (gz & 1) == 0

    def receive_camera(piece):
        @pl.when(even)
        def _():
            assemble(piece, 3)
            mate_copy(piece, 112, 128).start()
            assemble(piece, 0)

        @pl.when(jnp.logical_not(even))
        def _():
            assemble(piece, 0)
            mate_copy(piece, 0, 144).start()
            assemble(piece, 3)

        assemble(piece, 1)
        assemble(piece, 2)

        @pl.when(takes_low)
        def _():
            assemble_rim(piece, 0)

        @pl.when(takes_high)
        def _():
            assemble_rim(piece, 1)

        @pl.when(even)
        def _():
            mate_copy(piece, 0, 144).wait_recv()

        @pl.when(jnp.logical_not(even))
        def _():
            mate_copy(piece, 112, 128).wait_recv()

    def c_copy(part_of, n, at):
        return pltpu.make_async_remote_copy(
            src_ref=code_out[part_of].at[n],
            dst_ref=code_in[part_of].at[at],
            send_sem=c_send.at[part_of, n],
            recv_sem=c_recv.at[part_of, at],
            device_id=place_of(9 + n),
            device_id_type=MESH,
        )

    def encode(work, part_of, n):
        groups, out = parts[part_of], code_out[part_of]
        if part_of != 1:
            base = jnp.concatenate(
                [work[g * 16 + 8 : g * 16 + 9, :] for g in range(8)] + [jnp.zeros((8, 256), F32)], axis=0
            ).astype(BF16)
            out[n, len(groups) * 16 : len(groups) * 16 + 16, :] = base
            bases[...] = base.astype(F32)
        for i, g in enumerate(groups):
            out[n, i * 16 : (i + 1) * 16, :] = (work[g * 16 : (g + 1) * 16, :] - bases[g : g + 1, :]).astype(BF16)

    def collect(part_of):
        groups, code = parts[part_of], code_in[part_of]
        for n in reversed(ORDER):
            @pl.when(there(9 + n))
            def _():
                c_copy(part_of, n, n).wait_recv()
                with jax.named_scope("add"):
                    if part_of == 2:
                        base = code[n, 128:144, :].astype(F32)
                    else:
                        base = code_in[0][n, 64:80, :].astype(F32)
                    for i, g in enumerate(groups):
                        rows = slice(g * 16, (g + 1) * 16)
                        acc[rows, :] += code[n, i * 16 : (i + 1) * 16, :].astype(F32) + base[g : g + 1, :]

    def update(part_of):
        for g in parts[part_of]:
            rows = slice(g * 16, (g + 1) * 16)
            est[rows, :] = est[rows, :] * acc[rows, :] / VIEWS

    def sent():
        around(everyone, lambda m: e_copy(0, m, 26 - m).wait_send())
        for it in range(1, ITERS):
            around(everyone, lambda m: e_copy(it, m, 26 - m).wait_send())
            around(sides, lambda m: middle_copy(m, 26 - m).wait_send())
        for part_of in range(2):
            around(sides, lambda m: c_copy(part_of, m - 9, 17 - m).wait_send())

        for piece in range(2):
            @pl.when(even)
            def _():
                mate_copy(piece, 112, 128).wait_send()

            @pl.when(jnp.logical_not(even))
            def _():
                mate_copy(piece, 0, 144).wait_send()

            others(16, target, lambda a: cam_copy(piece, a, slot).wait_send())

            @pl.when(gives_low)
            def _():
                others(16, low_target, lambda a: rim_copy(piece, False, a, gz).wait_send())

            @pl.when(gives_high)
            def _():
                others(16, high_target, lambda a: rim_copy(piece, True, a, gz).wait_send())

    for it in range(ITERS):
        if it > 0:
            with jax.named_scope("wait estimate 2"):
                wait_estimate(it, everyone)
                around(sides, lambda m: middle_copy(m, m).wait_recv())
            with jax.named_scope("blur 2"):
                blur(it)
        for piece in range(2):
            if it == 0:
                receive_camera(piece)
            with jax.named_scope("quotients"):
                quotients(views[piece])
            with jax.named_scope("third"):
                for v in views[piece]:
                    value = dot(bzb[v].astype(BF16), quot[v]) * factor(8 + v)
                    third[:, v * 256 : (v + 1) * 256] = value.astype(BF16)
            if it == 0 and piece == 0:
                for n in range(9):
                    early[n] = dot(third[:, 0:1024], kb[n, 0:1024, :])

        def sums(n):
            if it == 0:
                return early[n] + dot(third[:, 1024:1536], kb[n, 1024:1536, :])
            return dot(third[...], kb[n])

        last = it == ITERS - 1
        with jax.named_scope("partial sums"):
            for count, n in enumerate(ORDER):
                @pl.when(there(9 + n))
                def _():
                    work = part.at[count % 2]
                    work[...] = sums(n)
                    if last:
                        encode(work, 2, n)
                        c_copy(2, n, 8 - n).start()
                    else:
                        encode(work, 0, n)
                        c_copy(0, n, 8 - n).start()
                        encode(work, 1, n)
            if not last:
                for n in ORDER:
                    @pl.when(there(9 + n))
                    def _():
                        c_copy(1, n, 8 - n).start()

        with jax.named_scope("own sum"):
            acc[...] = sums(4)
        if last:
            with jax.named_scope("sent"):
                sent()
            collect(2)
            update(2)
        else:
            collect(0)
            update(0)
            keep(it + 1, 0)
            send_estimate(it + 1, everyone)
            collect(1)
            update(1)
            keep(it + 1, 1)
            around(sides, lambda m: middle_copy(m, 26 - m).start())

    with jax.named_scope("layout out"):
        flat[...] = est[...].T
        for y in range(16):
            out_ref[pl.ds(y, 16, stride=16), :] = flat[y * 16 : (y + 1) * 16, :]

    for n in ORDER:
        @pl.when(there(9 + n))
        def _():
            c_copy(2, n, 8 - n).wait_send()


def per_device(sizes, camera, initial, psf_taps):
    held = pl.BlockSpec(memory_space=pl.ANY)
    dma = pltpu.SemaphoreType.DMA
    rows = initial.reshape(256, 128)
    result = pl.pallas_call(
        functools.partial(kernel, sizes),
        out_shape=jax.ShapeDtypeStruct((256, 128), F32),
        in_specs=[held, held, held],
        out_specs=pl.BlockSpec(memory_space=pltpu.VMEM),
        scratch_shapes=[
            pltpu.VMEM((VIEWS, 32, 4, 256), BF16),
            pltpu.VMEM((256, 128), F32),
            pltpu.VMEM((VIEWS, 3, TAPS), F32),
            dma((3,)),
            pltpu.VMEM((128, 256), F32),
            pltpu.VMEM((ITERS, 192, 9 * 256), BF16),
            pltpu.VMEM((VIEWS, 256, 256), BF16),
            pltpu.VMEM((VIEWS, 160, 256), F32),
            pltpu.VMEM((VIEWS, 256, 512), BF16),
            pltpu.VMEM((VIEWS, 9 * 256, 256), BF16),
            pltpu.VMEM((9, VIEWS * 256, 256), BF16),
            pltpu.VMEM((VIEWS, 160, 256), F32),
            pltpu.VMEM((VIEWS, 128, 256), F32),
            pltpu.VMEM((24, 128), F32),
            pltpu.VMEM((24, 128), F32),
            pltpu.VMEM((48 * 8, 128), F32),
            pltpu.VMEM((2, 48 * 8, 128), F32),
            pltpu.VMEM((48 * 8, 128), F32),
            pltpu.VMEM((2, 48 * 8, 128), F32),
            pltpu.VMEM((16, 128), F32),
            pltpu.VMEM((2, 96, 1024), BF16),
            pltpu.VMEM((4, 1024, 256), BF16),
            pltpu.VMEM((16, 3, 32, 128), BF16),
            pltpu.VMEM((16, 3, 32, 128), BF16),
            pltpu.VMEM((2, 4, 3, 16, 128), BF16),
            pltpu.VMEM((VIEWS, 160, 256), BF16),
            pltpu.VMEM((128, VIEWS * 256), BF16),
            pltpu.VMEM((2, 128, 256), F32),
            pltpu.VMEM((256, 128), F32),
            pltpu.VMEM((128, 256), F32),
            pltpu.VMEM((9, 128, 256), F32),
            pltpu.VMEM((16, 256), F32),
            *[pltpu.VMEM((9, rows, 256), BF16) for rows in (80, 64, 144) * 2],
            dma((2, 16)), dma((2, 16)),
            dma((2, 2, 16)), dma((2, 2, 4)),
            dma((ITERS, 27)), dma((ITERS, 27)),
            dma((9,)), dma((9,)),
            dma((3, 9)), dma((3, 9)),
            dma((2,)), dma((2,)),
        ],
        compiler_params=pltpu.CompilerParams(
            collective_id=0, has_side_effects=True, vmem_limit_bytes=55040 * 1024
        ),
    )(camera, rows, psf_taps)
    return result.reshape(initial.shape)


def solution(mesh):
    in_specs = (P(None, "gx", ("gy", "gz"), None), P("gx", "gy", "gz"), P())
    out_specs = P("gx", "gy", "gz")
    sizes = tuple(mesh.shape[a] for a in ("gx", "gy", "gz"))
    return jax.shard_map(
        functools.partial(per_device, sizes),
        mesh=mesh, in_specs=in_specs, out_specs=out_specs, check_vma=False,
    )
```

```python
import functools

import jax
import jax.numpy as jnp
from jax import lax
from jax.experimental import pallas as pl
from jax.experimental.pallas import tpu as pltpu
from jax.sharding import PartitionSpec as P

VIEWS = 6
TAPS = 31
HALF = TAPS // 2
ITERS = 2
F32 = jnp.float32
BF16 = jnp.bfloat16
MESH = pl.DeviceIdType.MESH
ORDER = (0, 2, 6, 8, 1, 3, 5, 7)


def dot(a, b):
    return jnp.dot(a, b, preferred_element_type=F32)


def iota(shape, dim):
    return lax.broadcasted_iota(jnp.int32, shape, dim)


def inside(index):
    return jnp.where((index >= 0) & (index < TAPS), index, 127)


def pick(table, index):
    return jnp.take_along_axis(table, index, axis=1)


def kernel(
    sizes, cam_hbm, init_hbm, taps_hbm, out_ref,
    cam_raw, init_ref, taps_ref, in_sem,
    est, ext, quot, inverse, ubuf, kf, kb, bzf, bzb, raw, back, xf, yf, xb, yb, scale,
    picked, place, cam_out, cam_in, rim_in, cam, third, part, flat, acc, bases, code_out0, code_out1, code_out2, code_in0, code_in1, code_in2,
    cam_send, cam_recv, rim_send, rim_recv, e_send, e_recv, g_send, g_recv, c_send, c_recv, m_send, m_recv, r_send, r_recv,
):
    code_out, code_in = (code_out0, code_out1, code_out2), (code_in0, code_in1, code_in2)
    nx, ny, nz = sizes
    gx, gy, gz = lax.axis_index("gx"), lax.axis_index("gy"), lax.axis_index("gz")
    below, above = gz > 0, gz < nz - 1

    fetch = [
        pltpu.make_async_copy(cam_hbm, cam_raw, in_sem.at[0]),
        pltpu.make_async_copy(init_hbm, init_ref, in_sem.at[1]),
        pltpu.make_async_copy(taps_hbm, taps_ref, in_sem.at[2]),
    ]
    for copy in fetch:
        copy.start()

    has_x = (gx > 0, True, gx < nx - 1)
    has_y = (gy > 0, True, gy < ny - 1)
    has_z = (gz == 2, True, gz == 1)
    even = (gz & 1) == 0
    mate = (gx, gy, gz ^ 1)

    def steps(m):
        return m % 9 // 3 - 1, m % 3 - 1, m // 9 - 1

    def place_of(m):
        dx, dy, dz = steps(m)
        return gx + dx, gy + dy, gz + dz

    def there(m):
        flags = [has[d + 1] for has, d in zip((has_x, has_y, has_z), steps(m)) if d]
        return functools.reduce(jnp.logical_and, flags)

    def around(ms, body):
        for m in ms:
            @pl.when(there(m))
            def _():
                body(m)

    everyone = sorted((m for m in range(27) if m != 13), key=lambda m: -sum(map(abs, steps(m))))
    rims = [m for m in everyone if m // 9 != 1]
    sides = [m for m in everyone if m // 9 == 1]

    part_z, part_i = gx >> 2, gx & 3

    def is_self(place):
        return (place[0] == gx) & (place[2] == gz)

    def source(s):
        return 4 * gz + s // 4, gy, s % 4

    def low_source(k):
        return 4 * gz - 1, gy, k

    def high_source(k):
        return 4 * gz + 4, gy, k

    def target(a):
        return a, gy, part_z

    gives_low = (part_i == 3) & (part_z == 1)
    gives_high = (part_i == 0) & (part_z == 2)
    takes_low, takes_high = gz == 2, gz == 1

    def low_target(a):
        return a, gy, part_z + 1

    def high_target(a):
        return a, gy, part_z - 1

    def others(count, place, body):
        for s in range(count):
            @pl.when(jnp.logical_not(is_self(place(s))))
            def _():
                body(s)

    barrier = pltpu.get_barrier_semaphore()

    def greet(place):
        pl.semaphore_signal(barrier, inc=1, device_id=place, device_id_type=MESH)

    others(16, source, lambda s: greet(source(s)))

    @pl.when(takes_low)
    def _():
        others(4, low_source, lambda k: greet(low_source(k)))

    @pl.when(takes_high)
    def _():
        others(4, high_source, lambda k: greet(high_source(k)))

    around(everyone, lambda m: greet(place_of(m)))
    greet(mate)

    def one(flag):
        return flag.astype(jnp.int32)

    wide = 1 + one(gx > 0) + one(gx < nx - 1)
    tall = 1 + one(gy > 0) + one(gy < ny - 1)
    deep = 1 + one(gz == 1) + one(gz == 2)
    greetings = wide * tall * deep + 16 - one(part_z == gz)
    greetings += one(gives_low) * (16 - one(part_z + 1 == gz))
    greetings += one(gives_high) * (16 - one(part_z - 1 == gz))

    with jax.named_scope("zeros"):
        for m in everyone:
            step, lanes = m // 9, slice(m % 9 * 256, m % 9 * 256 + 256)
            rows = (slice(128, 160), slice(0, 128), slice(160, 192))[step]

            none = jnp.logical_not(there(m))
            if step == 0:
                none = none & even
            elif step == 2:
                none = none & jnp.logical_not(even)
            for it in range(ITERS):
                @pl.when(none)
                def _():
                    ext[it, rows, lanes] = jnp.zeros((rows.stop - rows.start, 256), BF16)

        quot[:, 160:256, :] = jnp.zeros((VIEWS, 96, 256), BF16)
        place[...] = jnp.zeros(place.shape, BF16)
        raw[...] = jnp.zeros((24, 128), F32)
        ubuf[:, 192:256, :] = jnp.zeros((VIEWS, 64, 512), BF16)

    with jax.named_scope("sort camera"):
        row, col = iota((32, 256), 0), iota((32, 256), 1)
        same_x = row == (col >> 7) * 16 + (col & 15)
        for r in range(2):
            turned = ((col >> 6) & 1) == (r + gz) % 2
            for y in range(4):
                ones = (same_x & turned & (((col >> 4) & 3) == y)).astype(F32).astype(BF16)
                for q in range(4):
                    first = (r * 4 + y) * 128 + q * 32
                    place[q, first : first + 32, :] = ones
    fetch[0].wait()
    with jax.named_scope("sort camera 2"):
        for v in range(VIEWS):
            r, w = v // 3, v % 3
            for y in range(4):
                plane = cam_raw[v, :, y, :]
                lanes = slice((r * 4 + y) * 128, (r * 4 + y + 1) * 128)
                for h in range(2):
                    picked[h, w * 32 : (w + 1) * 32, lanes] = plane[:, h * 128 : (h + 1) * 128]
        for p in range(8):
            block = dot(picked[p // 4], place[p % 4]).astype(BF16)
            for w in range(3):
                cam_out[2 * p, w] = block[w * 32 : (w + 1) * 32, 0:128]
                cam_out[2 * p + 1, w] = block[w * 32 : (w + 1) * 32, 128:256]

    parts = ((0, 1, 6, 7), (2, 3, 4, 5), tuple(range(8)))

    def keep(it, part_of):
        for i, g in enumerate(parts[part_of]):
            first = part_of * 64 + i * 16
            ext[it, first : first + 16, 1024:1280] = est[g * 16 : (g + 1) * 16, :].astype(BF16)

    fetch[1].wait()
    with jax.named_scope("layout in"):
        for y in range(16):
            flat[y * 16 : (y + 1) * 16, :] = init_ref[pl.ds(y, 16, stride=16), :]
        est[...] = flat[...].T
        for part_of in range(2):
            keep(0, part_of)

    with jax.named_scope("entry wait"):
        pl.semaphore_wait(barrier, greetings)

    slot = part_i * 4 + gz

    def cam_copy(a, s):
        return pltpu.make_async_remote_copy(
            src_ref=cam_out.at[a],
            dst_ref=cam_in.at[s],
            send_sem=cam_send.at[a],
            recv_sem=cam_recv.at[s],
            device_id=target(a),
            device_id_type=MESH,
        )

    def rim_copy(high, a, k):
        first = 0 if high else 16
        return pltpu.make_async_remote_copy(
            src_ref=cam_out.at[a, :, pl.ds(first, 16), :],
            dst_ref=rim_in.at[int(high), k],
            send_sem=rim_send.at[int(high), a],
            recv_sem=rim_recv.at[int(high), k],
            device_id=high_target(a) if high else low_target(a),
            device_id_type=MESH,
        )

    def e_copy(it, m, at):
        first, count, to = ((0, 32, 160), (0, 64 if it else 128, 0), (32, 32, 128))[m // 9]
        return pltpu.make_async_remote_copy(
            src_ref=ext.at[it, pl.ds(first, count), pl.ds(1024, 256)],
            dst_ref=ext.at[it, pl.ds(to, count), pl.ds(at % 9 * 256, 256)],
            send_sem=e_send.at[it, m],
            recv_sem=e_recv.at[it, at],
            device_id=place_of(m),
            device_id_type=MESH,
        )

    def middle_copy(m, at):
        return pltpu.make_async_remote_copy(
            src_ref=ext.at[1, pl.ds(64, 64), pl.ds(1024, 256)],
            dst_ref=ext.at[1, pl.ds(64, 64), pl.ds(at % 9 * 256, 256)],
            send_sem=g_send.at[m - 9],
            recv_sem=g_recv.at[at - 9],
            device_id=place_of(m),
            device_id_type=MESH,
        )

    def mate_rims(it, up):
        first, to = (32, 128) if up else (0, 160)
        return pltpu.make_async_remote_copy(
            src_ref=ext.at[it, pl.ds(first, 32), :],
            dst_ref=ext.at[it, pl.ds(to, 32), :],
            send_sem=r_send.at[it],
            recv_sem=r_recv.at[it],
            device_id=mate,
            device_id_type=MESH,
        )

    def with_mate(body):
        @pl.when(even)
        def _():
            body(True)

        @pl.when(jnp.logical_not(even))
        def _():
            body(False)

    def send_estimate(it, ms):
        around(ms, lambda m: e_copy(it, m, 26 - m).start())

    def wait_estimate(it, ms):
        around(ms, lambda m: e_copy(it, m, m).wait_recv())

    with jax.named_scope("send estimate"):
        send_estimate(0, everyone)

    with jax.named_scope("send camera"):
        @pl.when(part_z == gz)
        def _():
            cam_in[slot] = cam_out[gx]

        others(16, target, lambda a: cam_copy(a, slot).start())

        @pl.when(gives_low)
        def _():
            @pl.when(part_z + 1 == gz)
            def _():
                rim_in[0, gz] = cam_out[gx, :, 16:32, :]

            others(16, low_target, lambda a: rim_copy(False, a, gz).start())

        @pl.when(gives_high)
        def _():
            @pl.when(part_z - 1 == gz)
            def _():
                rim_in[1, gz] = cam_out[gx, :, 0:16, :]

            others(16, high_target, lambda a: rim_copy(True, a, gz).start())

    fetch[2].wait()
    with jax.named_scope("taps"):
        for v in range(VIEWS):
            for a in range(3):
                raw[a * 8 + v : a * 8 + v + 1, 0:TAPS] = taps_ref[v, a : a + 1, :]
        total = jnp.sum(raw[...], axis=1, keepdims=True)
        total = jnp.where((iota((24, 1), 0) & 7) < VIEWS, total, 1.0)
        back[...] = (raw[...] / total).astype(BF16).astype(F32)

    with jax.named_scope("tables"):
        def tables(i, carry):
            lane = iota((8, 128), 1)
            for k in range(6):
                j = i * 6 + k
                rows = pl.ds(pl.multiple_of(j * 8, 8), 8)
                x = lane & 15
                xf[rows, :] = pick(raw[0:8, :], inside(x + 31 - j))
                xb[rows, :] = pick(back[0:8, :], inside(j - 1 - x))
                for half in range(2):
                    y = (lane >> 4) + 8 * half
                    yf[half, rows, :] = pick(raw[8:16, :], inside(y + 31 - j))
                    yb[half, rows, :] = pick(back[8:16, :], inside(j - 1 - y))
            return carry

        lax.fori_loop(0, 8, tables, 0)

    def rows_of(table, j, v):
        return table[pl.ds(j * 128 + v, 16, stride=8), :]

    with jax.named_scope("products"):
        def products(i, carry):
            v, n = i // 9, i % 9
            dx, dy = n // 3, n % 3
            x = rows_of(xf, dx, v)
            for half in range(2):
                ys = rows_of(yf.at[half], dy, v)
                for y in range(16):
                    kf[v, pl.ds(pl.multiple_of(n * 256 + y * 16, 16), 16), half * 128 : (half + 1) * 128] = (
                        x * ys[y : y + 1, :]
                    ).astype(BF16)
            return carry

        lax.fori_loop(0, 9 * VIEWS, products, 0)

    with jax.named_scope("pass rims"):
        wait_estimate(0, sides)
        with_mate(lambda up: mate_rims(0, up).start())

    with jax.named_scope("bands"):
        def bands(block, carry):
            r = iota((8, 128), 0) + block * 8
            z_out = jnp.where(r < 128, r, jnp.where(r < 144, r - 144, r - 16))
            rows = pl.ds(pl.multiple_of(block * 8, 8), 8)
            lane = iota((8, 128), 1)
            near = jnp.where(lane < 32, lane, jnp.where(lane < 64, lane + 64, lane - 32))
            far = jnp.where(lane < 32, lane - 32, jnp.where(lane < 64, lane + 96, 4096))
            for half, z_in in enumerate((near, far)):
                index = inside(z_out - z_in + HALF)
                for v in range(VIEWS):
                    band_f = jnp.broadcast_to(raw[16 + v : 17 + v, :], (8, 128))
                    bzf[v, rows, half * 128 : (half + 1) * 128] = pick(band_f, index)
            return carry

        lax.fori_loop(0, 20, bands, 0)

        def back_bands(block, carry):
            z_out = iota((8, 128), 0) + block * 8
            rows = pl.ds(pl.multiple_of(block * 8, 8), 8)
            lane = iota((8, 128), 1)
            far = jnp.where(lane < 16, lane - 16, jnp.where(lane < 32, lane + 112, 1024))
            for half, z_in in enumerate((lane, far)):
                index = inside(z_in - z_out + HALF)
                for v in range(VIEWS):
                    band_b = jnp.broadcast_to(back[16 + v : 17 + v, :], (8, 128))
                    bzb[v, rows, half * 128 : (half + 1) * 128] = pick(band_b, index)
            return carry

        lax.fori_loop(0, 16, back_bands, 0)

    with jax.named_scope("scale"):
        fx, fy, fz = raw[0:8, :], raw[8:16, :], raw[16:24, :]
        bx, by = back[0:8, :], back[8:16, :]
        f_sum, b_sum = jnp.zeros((8, 128), F32), jnp.zeros((8, 128), F32)
        for t in range(TAPS):
            f_sum += (fx[:, t : t + 1] * fy).astype(BF16).astype(F32)
            b_sum += (bx[:, t : t + 1] * by).astype(BF16).astype(F32)

        def lanes_sum(a):
            return jnp.sum(a, axis=1, keepdims=True)

        f_scale = lanes_sum(f_sum) * lanes_sum(fz.astype(BF16).astype(F32))
        b_total = jnp.where(iota((8, 1), 0) < VIEWS, lanes_sum(b_sum), 1.0)
        b_scale = lanes_sum(bx) * lanes_sum(by) / b_total
        scale[0:8, :] = jnp.broadcast_to(f_scale, (8, 128))
        scale[8:16, :] = jnp.broadcast_to(b_scale, (8, 128))

    with jax.named_scope("back products"):
        def back_products(i, carry):
            v, n = i // 9, i % 9
            dx, dy = n // 3, n % 3
            x = rows_of(xb, 2 - dx, v)
            for half in range(2):
                ys = rows_of(yb.at[half], 2 - dy, v)
                for y in range(16):
                    kb[n, pl.ds(pl.multiple_of(v * 256 + y * 16, 16), 16), half * 128 : (half + 1) * 128] = (
                        x * ys[y : y + 1, :]
                    ).astype(BF16)
            return carry

        lax.fori_loop(0, 9 * VIEWS, back_products, 0)

    def factor(row):
        value = scale[row : row + 1, :]
        return jnp.concatenate([value, value], axis=1)

    def blur(it):
        for v in range(VIEWS):
            u = dot(ext[it], kf[v])
            high = u.astype(BF16)
            ubuf[v, 0:192, 0:256] = high
            ubuf[v, 0:192, 256:512] = (u - high.astype(F32)).astype(BF16)
        for v in range(VIEWS):
            halves = dot(bzf[v].astype(BF16), ubuf[v])
            inverse[v] = factor(v) / (halves[:, 0:256] + halves[:, 256:512])

    def quotients():
        row = iota((32, 256), 0)
        seen = jnp.where(row < 16, one(below), one(above)) > 0
        for v in range(VIEWS):
            quot[v, 0:128, :] = (cam[v, 0:128, :].astype(F32) * inverse[v, 0:128, :]).astype(BF16)
            rim = jnp.where(seen, cam[v, 128:160, :].astype(F32) * inverse[v, 128:160, :], 0.0)
            quot[v, 128:160, :] = rim.astype(BF16)

    with jax.named_scope("wait estimate"):
        wait_estimate(0, rims)
        with_mate(lambda up: mate_rims(0, not up).wait_recv())
    with jax.named_scope("blur"):
        blur(0)

    def mate_copy(first, to):
        return pltpu.make_async_remote_copy(
            src_ref=cam.at[:, pl.ds(first, 16), :],
            dst_ref=cam.at[:, pl.ds(to, 16), :],
            send_sem=m_send,
            recv_sem=m_recv,
            device_id=mate,
            device_id_type=MESH,
        )

    def pair(r, even, odd):
        low = iota(even.shape, 1) < 64
        even, odd = even.astype(F32), odd.astype(F32)
        if r == 0:
            return jnp.where(low, even, odd).astype(BF16)
        return pltpu.roll(jnp.where(low, odd, even), 64, 1).astype(BF16)

    def assemble(z):
        for k in range(4):
            @pl.when(jnp.logical_not(is_self(source(4 * z + k))))
            def _():
                cam_copy(0, 4 * z + k).wait_recv()
        for v in range(VIEWS):
            r, w = v // 3, v % 3
            for t in range(2):
                cam[v, z * 32 : (z + 1) * 32, t * 128 : (t + 1) * 128] = pair(
                    r, cam_in[z * 4 + 2 * t, w], cam_in[z * 4 + 2 * t + 1, w]
                )

    def assemble_rim(high):
        place = high_source if high else low_source
        others(4, place, lambda k: rim_copy(high, 0, k).wait_recv())
        for v in range(VIEWS):
            r, w = v // 3, v % 3
            for t in range(2):
                cam[v, 128 + high * 16 : 144 + high * 16, t * 128 : (t + 1) * 128] = pair(
                    r, rim_in[high, 2 * t, w], rim_in[high, 2 * t + 1, w]
                )

    with jax.named_scope("camera in"):
        @pl.when(even)
        def _():
            assemble(3)
            mate_copy(112, 128).start()
            assemble(0)

        @pl.when(jnp.logical_not(even))
        def _():
            assemble(0)
            mate_copy(0, 144).start()
            assemble(3)

        assemble(1)
        assemble(2)

        @pl.when(takes_low)
        def _():
            assemble_rim(0)

        @pl.when(takes_high)
        def _():
            assemble_rim(1)

        @pl.when(even)
        def _():
            mate_copy(0, 144).wait_recv()

        @pl.when(jnp.logical_not(even))
        def _():
            mate_copy(112, 128).wait_recv()

    def c_copy(part_of, n, at):
        return pltpu.make_async_remote_copy(
            src_ref=code_out[part_of].at[n],
            dst_ref=code_in[part_of].at[at],
            send_sem=c_send.at[part_of, n],
            recv_sem=c_recv.at[part_of, at],
            device_id=place_of(9 + n),
            device_id_type=MESH,
        )

    def encode(work, part_of, n):
        groups, out = parts[part_of], code_out[part_of]
        if part_of != 1:
            base = jnp.concatenate(
                [work[g * 16 + 8 : g * 16 + 9, :] for g in range(8)] + [jnp.zeros((8, 256), F32)], axis=0
            ).astype(BF16)
            out[n, len(groups) * 16 : len(groups) * 16 + 16, :] = base
            bases[...] = base.astype(F32)
        for i, g in enumerate(groups):
            out[n, i * 16 : (i + 1) * 16, :] = (work[g * 16 : (g + 1) * 16, :] - bases[g : g + 1, :]).astype(BF16)

    def collect(part_of):
        groups, code = parts[part_of], code_in[part_of]
        for n in reversed(ORDER):
            @pl.when(there(9 + n))
            def _():
                c_copy(part_of, n, n).wait_recv()
                with jax.named_scope("add"):
                    if part_of == 2:
                        base = code[n, 128:144, :].astype(F32)
                    else:
                        base = code_in[0][n, 64:80, :].astype(F32)
                    for i, g in enumerate(groups):
                        rows = slice(g * 16, (g + 1) * 16)
                        acc[rows, :] += code[n, i * 16 : (i + 1) * 16, :].astype(F32) + base[g : g + 1, :]

    def update(part_of):
        for g in parts[part_of]:
            rows = slice(g * 16, (g + 1) * 16)
            est[rows, :] = est[rows, :] * acc[rows, :] / VIEWS

    def sent():
        around(everyone, lambda m: e_copy(0, m, 26 - m).wait_send())
        for it in range(ITERS):
            with_mate(lambda up: mate_rims(it, up).wait_send())
        for it in range(1, ITERS):
            around(everyone, lambda m: e_copy(it, m, 26 - m).wait_send())
            around(sides, lambda m: middle_copy(m, 26 - m).wait_send())
        for part_of in range(2):
            around(sides, lambda m: c_copy(part_of, m - 9, 17 - m).wait_send())

        @pl.when(even)
        def _():
            mate_copy(112, 128).wait_send()

        @pl.when(jnp.logical_not(even))
        def _():
            mate_copy(0, 144).wait_send()
        others(16, target, lambda a: cam_copy(a, slot).wait_send())

        @pl.when(gives_low)
        def _():
            others(16, low_target, lambda a: rim_copy(False, a, gz).wait_send())

        @pl.when(gives_high)
        def _():
            others(16, high_target, lambda a: rim_copy(True, a, gz).wait_send())

    for it in range(ITERS):
        if it > 0:
            with jax.named_scope("wait estimate 2"):
                wait_estimate(it, sides)
                with_mate(lambda up: mate_rims(it, up).start())
                wait_estimate(it, rims)
                around(sides, lambda m: middle_copy(m, m).wait_recv())
                with_mate(lambda up: mate_rims(it, not up).wait_recv())
            with jax.named_scope("blur 2"):
                blur(it)
        with jax.named_scope("quotients"):
            quotients()
        with jax.named_scope("third"):
            for v in range(VIEWS):
                value = dot(bzb[v].astype(BF16), quot[v]) * factor(8 + v)
                third[:, v * 256 : (v + 1) * 256] = value.astype(BF16)

        last = it == ITERS - 1
        with jax.named_scope("partial sums"):
            for count, n in enumerate(ORDER):
                @pl.when(there(9 + n))
                def _():
                    work = part.at[count % 2]
                    work[...] = dot(third[...], kb[n])
                    if last:
                        encode(work, 2, n)
                        c_copy(2, n, 8 - n).start()
                    else:
                        encode(work, 0, n)
                        c_copy(0, n, 8 - n).start()
                        encode(work, 1, n)
            if not last:
                for n in ORDER:
                    @pl.when(there(9 + n))
                    def _():
                        c_copy(1, n, 8 - n).start()

        with jax.named_scope("own sum"):
            acc[...] = dot(third[...], kb[4])
        if last:
            with jax.named_scope("sent"):
                sent()
            collect(2)
            update(2)
        else:
            collect(0)
            update(0)
            keep(it + 1, 0)
            send_estimate(it + 1, everyone)
            collect(1)
            update(1)
            keep(it + 1, 1)
            around(sides, lambda m: middle_copy(m, 26 - m).start())

    with jax.named_scope("layout out"):
        flat[...] = est[...].T
        for y in range(16):
            out_ref[pl.ds(y, 16, stride=16), :] = flat[y * 16 : (y + 1) * 16, :]

    for n in ORDER:
        @pl.when(there(9 + n))
        def _():
            c_copy(2, n, 8 - n).wait_send()


def per_device(sizes, camera, initial, psf_taps):
    held = pl.BlockSpec(memory_space=pl.ANY)
    dma = pltpu.SemaphoreType.DMA
    rows = initial.reshape(256, 128)
    result = pl.pallas_call(
        functools.partial(kernel, sizes),
        out_shape=jax.ShapeDtypeStruct((256, 128), F32),
        in_specs=[held, held, held],
        out_specs=pl.BlockSpec(memory_space=pltpu.VMEM),
        scratch_shapes=[
            pltpu.VMEM((VIEWS, 32, 4, 256), BF16),
            pltpu.VMEM((256, 128), F32),
            pltpu.VMEM((VIEWS, 3, TAPS), F32),
            dma((3,)),
            pltpu.VMEM((128, 256), F32),
            pltpu.VMEM((ITERS, 192, 9 * 256), BF16),
            pltpu.VMEM((VIEWS, 256, 256), BF16),
            pltpu.VMEM((VIEWS, 160, 256), F32),
            pltpu.VMEM((VIEWS, 256, 512), BF16),
            pltpu.VMEM((VIEWS, 9 * 256, 256), BF16),
            pltpu.VMEM((9, VIEWS * 256, 256), BF16),
            pltpu.VMEM((VIEWS, 160, 256), F32),
            pltpu.VMEM((VIEWS, 128, 256), F32),
            pltpu.VMEM((24, 128), F32),
            pltpu.VMEM((24, 128), F32),
            pltpu.VMEM((48 * 8, 128), F32),
            pltpu.VMEM((2, 48 * 8, 128), F32),
            pltpu.VMEM((48 * 8, 128), F32),
            pltpu.VMEM((2, 48 * 8, 128), F32),
            pltpu.VMEM((16, 128), F32),
            pltpu.VMEM((2, 96, 1024), BF16),
            pltpu.VMEM((4, 1024, 256), BF16),
            pltpu.VMEM((16, 3, 32, 128), BF16),
            pltpu.VMEM((16, 3, 32, 128), BF16),
            pltpu.VMEM((2, 4, 3, 16, 128), BF16),
            pltpu.VMEM((VIEWS, 160, 256), BF16),
            pltpu.VMEM((128, VIEWS * 256), BF16),
            pltpu.VMEM((2, 128, 256), F32),
            pltpu.VMEM((256, 128), F32),
            pltpu.VMEM((128, 256), F32),
            pltpu.VMEM((16, 256), F32),
            *[pltpu.VMEM((9, rows, 256), BF16) for rows in (80, 64, 144) * 2],
            dma((16,)), dma((16,)),
            dma((2, 16)), dma((2, 4)),
            dma((ITERS, 27)), dma((ITERS, 27)),
            dma((9,)), dma((9,)),
            dma((3, 9)), dma((3, 9)),
            dma(()), dma(()), dma((ITERS,)), dma((ITERS,)),
        ],
        compiler_params=pltpu.CompilerParams(
            collective_id=0, has_side_effects=True, vmem_limit_bytes=55040 * 1024
        ),
    )(camera, rows, psf_taps)
    return result.reshape(initial.shape)


def solution(mesh):
    in_specs = (P(None, "gx", ("gy", "gz"), None), P("gx", "gy", "gz"), P())
    out_specs = P("gx", "gy", "gz")
    sizes = tuple(mesh.shape[a] for a in ("gx", "gy", "gz"))
    return jax.shard_map(
        functools.partial(per_device, sizes),
        mesh=mesh, in_specs=in_specs, out_specs=out_specs, check_vma=False,
    )
```

```python
import functools

import jax
import jax.numpy as jnp
from jax import lax
from jax.experimental import pallas as pl
from jax.experimental.pallas import tpu as pltpu
from jax.sharding import PartitionSpec as P

VIEWS = 6
TAPS = 31
HALF = TAPS // 2
ITERS = 2
F32 = jnp.float32
BF16 = jnp.bfloat16
MESH = pl.DeviceIdType.MESH
ORDER = (0, 2, 6, 8, 1, 3, 5, 7)


def dot(a, b):
    return jnp.dot(a, b, preferred_element_type=F32)


def iota(shape, dim):
    return lax.broadcasted_iota(jnp.int32, shape, dim)


def inside(index):
    return jnp.where((index >= 0) & (index < TAPS), index, 127)


def pick(table, index):
    return jnp.take_along_axis(table, index, axis=1)


def kernel(
    sizes, cam_hbm, init_hbm, taps_hbm, out_ref,
    cam_raw, init_ref, taps_ref, in_sem,
    est, ext, quot, inverse, ubuf, kf, kb, bzf, bzb, raw, back, xf, yf, xb, yb, scale,
    picked, place, cam_out, cam_in, rim_in, cam, third, part, flat, acc, bases, code_out0, code_out1, code_out2, code_in0, code_in1, code_in2,
    cam_send, cam_recv, rim_send, rim_recv, e_send, e_recv, g_send, g_recv, c_send, c_recv, m_send, m_recv, r_send, r_recv,
):
    code_out, code_in = (code_out0, code_out1, code_out2), (code_in0, code_in1, code_in2)
    nx, ny, nz = sizes
    gx, gy, gz = lax.axis_index("gx"), lax.axis_index("gy"), lax.axis_index("gz")
    below, above = gz > 0, gz < nz - 1

    fetch = [
        pltpu.make_async_copy(cam_hbm, cam_raw, in_sem.at[0]),
        pltpu.make_async_copy(init_hbm, init_ref, in_sem.at[1]),
        pltpu.make_async_copy(taps_hbm, taps_ref, in_sem.at[2]),
    ]
    for copy in fetch:
        copy.start()

    has_x = (gx > 0, True, gx < nx - 1)
    has_y = (gy > 0, True, gy < ny - 1)
    has_z = (gz == 2, True, gz == 1)
    even = (gz & 1) == 0
    mate = (gx, gy, gz ^ 1)

    def steps(m):
        return m % 9 // 3 - 1, m % 3 - 1, m // 9 - 1

    def place_of(m):
        dx, dy, dz = steps(m)
        return gx + dx, gy + dy, gz + dz

    def there(m):
        flags = [has[d + 1] for has, d in zip((has_x, has_y, has_z), steps(m)) if d]
        return functools.reduce(jnp.logical_and, flags)

    def around(ms, body):
        for m in ms:
            @pl.when(there(m))
            def _():
                body(m)

    everyone = sorted((m for m in range(27) if m != 13), key=lambda m: -sum(map(abs, steps(m))))
    rims = [m for m in everyone if m // 9 != 1]
    sides = [m for m in everyone if m // 9 == 1]

    part_z, part_i = gx >> 2, gx & 3

    def is_self(place):
        return (place[0] == gx) & (place[2] == gz)

    def source(s):
        return 4 * gz + s // 4, gy, s % 4

    def low_source(k):
        return 4 * gz - 1, gy, k

    def high_source(k):
        return 4 * gz + 4, gy, k

    def target(a):
        return a, gy, part_z

    gives_low = (part_i == 3) & (part_z == 1)
    gives_high = (part_i == 0) & (part_z == 2)
    takes_low, takes_high = gz == 2, gz == 1

    def low_target(a):
        return a, gy, part_z + 1

    def high_target(a):
        return a, gy, part_z - 1

    def others(count, place, body):
        for s in range(count):
            @pl.when(jnp.logical_not(is_self(place(s))))
            def _():
                body(s)

    barrier = pltpu.get_barrier_semaphore()

    def greet(place):
        pl.semaphore_signal(barrier, inc=1, device_id=place, device_id_type=MESH)

    others(16, source, lambda s: greet(source(s)))

    @pl.when(takes_low)
    def _():
        others(4, low_source, lambda k: greet(low_source(k)))

    @pl.when(takes_high)
    def _():
        others(4, high_source, lambda k: greet(high_source(k)))

    around(everyone, lambda m: greet(place_of(m)))
    greet(mate)

    def one(flag):
        return flag.astype(jnp.int32)

    wide = 1 + one(gx > 0) + one(gx < nx - 1)
    tall = 1 + one(gy > 0) + one(gy < ny - 1)
    deep = 1 + one(gz == 1) + one(gz == 2)
    greetings = wide * tall * deep + 16 - one(part_z == gz)
    greetings += one(gives_low) * (16 - one(part_z + 1 == gz))
    greetings += one(gives_high) * (16 - one(part_z - 1 == gz))

    with jax.named_scope("zeros"):
        for m in everyone:
            step, lanes = m // 9, slice(m % 9 * 256, m % 9 * 256 + 256)
            rows = (slice(128, 160), slice(0, 128), slice(160, 192))[step]

            none = jnp.logical_not(there(m))
            if step == 0:
                none = none & even
            elif step == 2:
                none = none & jnp.logical_not(even)
            for it in range(ITERS):
                @pl.when(none)
                def _():
                    ext[it, rows, lanes] = jnp.zeros((rows.stop - rows.start, 256), BF16)

        quot[:, 160:256, :] = jnp.zeros((VIEWS, 96, 256), BF16)
        place[...] = jnp.zeros(place.shape, BF16)
        raw[...] = jnp.zeros((24, 128), F32)
        ubuf[:, 192:256, :] = jnp.zeros((VIEWS, 64, 512), BF16)

    with jax.named_scope("sort camera"):
        row, col = iota((32, 256), 0), iota((32, 256), 1)
        same_x = row == (col >> 7) * 16 + (col & 15)
        for r in range(2):
            turned = ((col >> 6) & 1) == (r + gz) % 2
            for y in range(4):
                ones = (same_x & turned & (((col >> 4) & 3) == y)).astype(F32).astype(BF16)
                for q in range(4):
                    first = (r * 4 + y) * 128 + q * 32
                    place[q, first : first + 32, :] = ones
    fetch[0].wait()
    with jax.named_scope("sort camera 2"):
        for v in range(VIEWS):
            r, w = v // 3, v % 3
            for y in range(4):
                plane = cam_raw[v, :, y, :]
                lanes = slice((r * 4 + y) * 128, (r * 4 + y + 1) * 128)
                for h in range(2):
                    picked[h, w * 32 : (w + 1) * 32, lanes] = plane[:, h * 128 : (h + 1) * 128]
        for p in range(8):
            block = dot(picked[p // 4], place[p % 4]).astype(BF16)
            for w in range(3):
                cam_out[2 * p, w] = block[w * 32 : (w + 1) * 32, 0:128]
                cam_out[2 * p + 1, w] = block[w * 32 : (w + 1) * 32, 128:256]

    parts = ((0, 1, 6, 7), (2, 3, 4, 5), tuple(range(8)))

    def keep(it, part_of):
        for i, g in enumerate(parts[part_of]):
            first = part_of * 64 + i * 16
            ext[it, first : first + 16, 1024:1280] = est[g * 16 : (g + 1) * 16, :].astype(BF16)

    fetch[1].wait()
    with jax.named_scope("layout in"):
        for y in range(16):
            flat[y * 16 : (y + 1) * 16, :] = init_ref[pl.ds(y, 16, stride=16), :]
        est[...] = flat[...].T
        for part_of in range(2):
            keep(0, part_of)

    with jax.named_scope("entry wait"):
        pl.semaphore_wait(barrier, greetings)

    slot = part_i * 4 + gz

    def cam_copy(a, s):
        return pltpu.make_async_remote_copy(
            src_ref=cam_out.at[a],
            dst_ref=cam_in.at[s],
            send_sem=cam_send.at[a],
            recv_sem=cam_recv.at[s],
            device_id=target(a),
            device_id_type=MESH,
        )

    def rim_copy(high, a, k):
        first = 0 if high else 16
        return pltpu.make_async_remote_copy(
            src_ref=cam_out.at[a, :, pl.ds(first, 16), :],
            dst_ref=rim_in.at[int(high), k],
            send_sem=rim_send.at[int(high), a],
            recv_sem=rim_recv.at[int(high), k],
            device_id=high_target(a) if high else low_target(a),
            device_id_type=MESH,
        )

    def e_copy(it, m, at):
        first, count, to = ((0, 32, 160), (0, 64 if it else 128, 0), (32, 32, 128))[m // 9]
        return pltpu.make_async_remote_copy(
            src_ref=ext.at[it, pl.ds(first, count), pl.ds(1024, 256)],
            dst_ref=ext.at[it, pl.ds(to, count), pl.ds(at % 9 * 256, 256)],
            send_sem=e_send.at[it, m],
            recv_sem=e_recv.at[it, at],
            device_id=place_of(m),
            device_id_type=MESH,
        )

    def middle_copy(m, at):
        return pltpu.make_async_remote_copy(
            src_ref=ext.at[1, pl.ds(64, 64), pl.ds(1024, 256)],
            dst_ref=ext.at[1, pl.ds(64, 64), pl.ds(at % 9 * 256, 256)],
            send_sem=g_send.at[m - 9],
            recv_sem=g_recv.at[at - 9],
            device_id=place_of(m),
            device_id_type=MESH,
        )

    def mate_rims(it, up):
        first, to = (32, 128) if up else (0, 160)
        return pltpu.make_async_remote_copy(
            src_ref=ext.at[it, pl.ds(first, 32), :],
            dst_ref=ext.at[it, pl.ds(to, 32), :],
            send_sem=r_send.at[it],
            recv_sem=r_recv.at[it],
            device_id=mate,
            device_id_type=MESH,
        )

    def with_mate(body):
        @pl.when(even)
        def _():
            body(True)

        @pl.when(jnp.logical_not(even))
        def _():
            body(False)

    def send_estimate(it, ms):
        around(ms, lambda m: e_copy(it, m, 26 - m).start())

    def wait_estimate(it, ms):
        around(ms, lambda m: e_copy(it, m, m).wait_recv())

    with jax.named_scope("send estimate"):
        send_estimate(0, everyone)

    def turn(s):
        return (gx + 8 + s) & 15

    with jax.named_scope("send camera"):
        @pl.when(gives_low)
        def _():
            others(16, lambda s: low_target(turn(s)), lambda s: rim_copy(False, turn(s), gz).start())

            @pl.when(part_z + 1 == gz)
            def _():
                rim_in[0, gz] = cam_out[gx, :, 16:32, :]

        @pl.when(gives_high)
        def _():
            others(16, lambda s: high_target(turn(s)), lambda s: rim_copy(True, turn(s), gz).start())

            @pl.when(part_z - 1 == gz)
            def _():
                rim_in[1, gz] = cam_out[gx, :, 0:16, :]

        others(16, lambda s: target(turn(s)), lambda s: cam_copy(turn(s), slot).start())

        @pl.when(part_z == gz)
        def _():
            cam_in[slot] = cam_out[gx]

    fetch[2].wait()
    with jax.named_scope("taps"):
        for v in range(VIEWS):
            for a in range(3):
                raw[a * 8 + v : a * 8 + v + 1, 0:TAPS] = taps_ref[v, a : a + 1, :]
        total = jnp.sum(raw[...], axis=1, keepdims=True)
        total = jnp.where((iota((24, 1), 0) & 7) < VIEWS, total, 1.0)
        back[...] = (raw[...] / total).astype(BF16).astype(F32)

    with jax.named_scope("tables"):
        def tables(i, carry):
            lane = iota((8, 128), 1)
            for k in range(6):
                j = i * 6 + k
                rows = pl.ds(pl.multiple_of(j * 8, 8), 8)
                x = lane & 15
                xf[rows, :] = pick(raw[0:8, :], inside(x + 31 - j))
                xb[rows, :] = pick(back[0:8, :], inside(j - 1 - x))
                for half in range(2):
                    y = (lane >> 4) + 8 * half
                    yf[half, rows, :] = pick(raw[8:16, :], inside(y + 31 - j))
                    yb[half, rows, :] = pick(back[8:16, :], inside(j - 1 - y))
            return carry

        lax.fori_loop(0, 8, tables, 0)

    def rows_of(table, j, v):
        return table[pl.ds(j * 128 + v, 16, stride=8), :]

    with jax.named_scope("products"):
        def products(i, carry):
            v, n = i // 9, i % 9
            dx, dy = n // 3, n % 3
            x = rows_of(xf, dx, v)
            for half in range(2):
                ys = rows_of(yf.at[half], dy, v)
                for y in range(16):
                    kf[v, pl.ds(pl.multiple_of(n * 256 + y * 16, 16), 16), half * 128 : (half + 1) * 128] = (
                        x * ys[y : y + 1, :]
                    ).astype(BF16)
            return carry

        lax.fori_loop(0, 9 * VIEWS, products, 0)

    with jax.named_scope("pass rims"):
        wait_estimate(0, sides)
        with_mate(lambda up: mate_rims(0, up).start())

    with jax.named_scope("bands"):
        def bands(block, carry):
            r = iota((8, 128), 0) + block * 8
            z_out = jnp.where(r < 128, r, jnp.where(r < 144, r - 144, r - 16))
            rows = pl.ds(pl.multiple_of(block * 8, 8), 8)
            lane = iota((8, 128), 1)
            near = jnp.where(lane < 32, lane, jnp.where(lane < 64, lane + 64, lane - 32))
            far = jnp.where(lane < 32, lane - 32, jnp.where(lane < 64, lane + 96, 4096))
            for half, z_in in enumerate((near, far)):
                index = inside(z_out - z_in + HALF)
                for v in range(VIEWS):
                    band_f = jnp.broadcast_to(raw[16 + v : 17 + v, :], (8, 128))
                    bzf[v, rows, half * 128 : (half + 1) * 128] = pick(band_f, index)
            return carry

        lax.fori_loop(0, 20, bands, 0)

        def back_bands(block, carry):
            z_out = iota((8, 128), 0) + block * 8
            rows = pl.ds(pl.multiple_of(block * 8, 8), 8)
            lane = iota((8, 128), 1)
            far = jnp.where(lane < 16, lane - 16, jnp.where(lane < 32, lane + 112, 1024))
            for half, z_in in enumerate((lane, far)):
                index = inside(z_in - z_out + HALF)
                for v in range(VIEWS):
                    band_b = jnp.broadcast_to(back[16 + v : 17 + v, :], (8, 128))
                    bzb[v, rows, half * 128 : (half + 1) * 128] = pick(band_b, index)
            return carry

        lax.fori_loop(0, 16, back_bands, 0)

    with jax.named_scope("scale"):
        fx, fy, fz = raw[0:8, :], raw[8:16, :], raw[16:24, :]
        bx, by = back[0:8, :], back[8:16, :]
        f_sum, b_sum = jnp.zeros((8, 128), F32), jnp.zeros((8, 128), F32)
        for t in range(TAPS):
            f_sum += (fx[:, t : t + 1] * fy).astype(BF16).astype(F32)
            b_sum += (bx[:, t : t + 1] * by).astype(BF16).astype(F32)

        def lanes_sum(a):
            return jnp.sum(a, axis=1, keepdims=True)

        f_scale = lanes_sum(f_sum) * lanes_sum(fz.astype(BF16).astype(F32))
        b_total = jnp.where(iota((8, 1), 0) < VIEWS, lanes_sum(b_sum), 1.0)
        b_scale = lanes_sum(bx) * lanes_sum(by) / b_total
        scale[0:8, :] = jnp.broadcast_to(f_scale, (8, 128))
        scale[8:16, :] = jnp.broadcast_to(b_scale, (8, 128))

    with jax.named_scope("back products"):
        def back_products(i, carry):
            v, n = i // 9, i % 9
            dx, dy = n // 3, n % 3
            x = rows_of(xb, 2 - dx, v)
            for half in range(2):
                ys = rows_of(yb.at[half], 2 - dy, v)
                for y in range(16):
                    kb[n, pl.ds(pl.multiple_of(v * 256 + y * 16, 16), 16), half * 128 : (half + 1) * 128] = (
                        x * ys[y : y + 1, :]
                    ).astype(BF16)
            return carry

        lax.fori_loop(0, 9 * VIEWS, back_products, 0)

    def factor(row):
        value = scale[row : row + 1, :]
        return jnp.concatenate([value, value], axis=1)

    def blur(it):
        for v in range(VIEWS):
            u = dot(ext[it], kf[v])
            high = u.astype(BF16)
            ubuf[v, 0:192, 0:256] = high
            ubuf[v, 0:192, 256:512] = (u - high.astype(F32)).astype(BF16)
        for v in range(VIEWS):
            halves = dot(bzf[v].astype(BF16), ubuf[v])
            inverse[v] = factor(v) / (halves[:, 0:256] + halves[:, 256:512])

    def quotients():
        row = iota((32, 256), 0)
        seen = jnp.where(row < 16, one(below), one(above)) > 0
        for v in range(VIEWS):
            quot[v, 0:128, :] = (cam[v, 0:128, :].astype(F32) * inverse[v, 0:128, :]).astype(BF16)
            rim = jnp.where(seen, cam[v, 128:160, :].astype(F32) * inverse[v, 128:160, :], 0.0)
            quot[v, 128:160, :] = rim.astype(BF16)

    with jax.named_scope("wait estimate"):
        wait_estimate(0, rims)
        with_mate(lambda up: mate_rims(0, not up).wait_recv())
    with jax.named_scope("blur"):
        blur(0)

    def mate_copy(first, to):
        return pltpu.make_async_remote_copy(
            src_ref=cam.at[:, pl.ds(first, 16), :],
            dst_ref=cam.at[:, pl.ds(to, 16), :],
            send_sem=m_send,
            recv_sem=m_recv,
            device_id=mate,
            device_id_type=MESH,
        )

    def pair(r, even, odd):
        low = iota(even.shape, 1) < 64
        even, odd = even.astype(F32), odd.astype(F32)
        if r == 0:
            return jnp.where(low, even, odd).astype(BF16)
        return pltpu.roll(jnp.where(low, odd, even), 64, 1).astype(BF16)

    def assemble(z):
        for k in range(4):
            @pl.when(jnp.logical_not(is_self(source(4 * z + k))))
            def _():
                cam_copy(0, 4 * z + k).wait_recv()
        for v in range(VIEWS):
            r, w = v // 3, v % 3
            for t in range(2):
                cam[v, z * 32 : (z + 1) * 32, t * 128 : (t + 1) * 128] = pair(
                    r, cam_in[z * 4 + 2 * t, w], cam_in[z * 4 + 2 * t + 1, w]
                )

    def assemble_rim(high):
        place = high_source if high else low_source
        others(4, place, lambda k: rim_copy(high, 0, k).wait_recv())
        for v in range(VIEWS):
            r, w = v // 3, v % 3
            for t in range(2):
                cam[v, 128 + high * 16 : 144 + high * 16, t * 128 : (t + 1) * 128] = pair(
                    r, rim_in[high, 2 * t, w], rim_in[high, 2 * t + 1, w]
                )

    with jax.named_scope("camera in"):
        @pl.when(even)
        def _():
            assemble(3)
            mate_copy(112, 128).start()
            assemble(0)

        @pl.when(jnp.logical_not(even))
        def _():
            assemble(0)
            mate_copy(0, 144).start()
            assemble(3)

        assemble(1)
        assemble(2)

        @pl.when(takes_low)
        def _():
            assemble_rim(0)

        @pl.when(takes_high)
        def _():
            assemble_rim(1)

        @pl.when(even)
        def _():
            mate_copy(0, 144).wait_recv()

        @pl.when(jnp.logical_not(even))
        def _():
            mate_copy(112, 128).wait_recv()

    def c_copy(part_of, n, at):
        return pltpu.make_async_remote_copy(
            src_ref=code_out[part_of].at[n],
            dst_ref=code_in[part_of].at[at],
            send_sem=c_send.at[part_of, n],
            recv_sem=c_recv.at[part_of, at],
            device_id=place_of(9 + n),
            device_id_type=MESH,
        )

    def encode(work, part_of, n):
        groups, out = parts[part_of], code_out[part_of]
        if part_of != 1:
            base = jnp.concatenate(
                [work[g * 16 + 8 : g * 16 + 9, :] for g in range(8)] + [jnp.zeros((8, 256), F32)], axis=0
            ).astype(BF16)
            out[n, len(groups) * 16 : len(groups) * 16 + 16, :] = base
            bases[...] = base.astype(F32)
        for i, g in enumerate(groups):
            out[n, i * 16 : (i + 1) * 16, :] = (work[g * 16 : (g + 1) * 16, :] - bases[g : g + 1, :]).astype(BF16)

    def collect(part_of):
        groups, code = parts[part_of], code_in[part_of]
        for n in reversed(ORDER):
            @pl.when(there(9 + n))
            def _():
                c_copy(part_of, n, n).wait_recv()
                with jax.named_scope("add"):
                    if part_of == 2:
                        base = code[n, 128:144, :].astype(F32)
                    else:
                        base = code_in[0][n, 64:80, :].astype(F32)
                    for i, g in enumerate(groups):
                        rows = slice(g * 16, (g + 1) * 16)
                        acc[rows, :] += code[n, i * 16 : (i + 1) * 16, :].astype(F32) + base[g : g + 1, :]

    def update(part_of):
        for g in parts[part_of]:
            rows = slice(g * 16, (g + 1) * 16)
            est[rows, :] = est[rows, :] * acc[rows, :] / VIEWS

    def sent():
        around(everyone, lambda m: e_copy(0, m, 26 - m).wait_send())
        for it in range(ITERS):
            with_mate(lambda up: mate_rims(it, up).wait_send())
        for it in range(1, ITERS):
            around(everyone, lambda m: e_copy(it, m, 26 - m).wait_send())
            around(sides, lambda m: middle_copy(m, 26 - m).wait_send())
        for part_of in range(2):
            around(sides, lambda m: c_copy(part_of, m - 9, 17 - m).wait_send())

        @pl.when(even)
        def _():
            mate_copy(112, 128).wait_send()

        @pl.when(jnp.logical_not(even))
        def _():
            mate_copy(0, 144).wait_send()
        others(16, target, lambda a: cam_copy(a, slot).wait_send())

        @pl.when(gives_low)
        def _():
            others(16, low_target, lambda a: rim_copy(False, a, gz).wait_send())

        @pl.when(gives_high)
        def _():
            others(16, high_target, lambda a: rim_copy(True, a, gz).wait_send())

    for it in range(ITERS):
        if it > 0:
            with jax.named_scope("wait estimate 2"):
                wait_estimate(it, sides)
                with_mate(lambda up: mate_rims(it, up).start())
                wait_estimate(it, rims)
                around(sides, lambda m: middle_copy(m, m).wait_recv())
                with_mate(lambda up: mate_rims(it, not up).wait_recv())
            with jax.named_scope("blur 2"):
                blur(it)
        with jax.named_scope("quotients"):
            quotients()
        with jax.named_scope("third"):
            for v in range(VIEWS):
                value = dot(bzb[v].astype(BF16), quot[v]) * factor(8 + v)
                third[:, v * 256 : (v + 1) * 256] = value.astype(BF16)

        last = it == ITERS - 1
        with jax.named_scope("partial sums"):
            for count, n in enumerate(ORDER):
                @pl.when(there(9 + n))
                def _():
                    work = part.at[count % 2]
                    work[...] = dot(third[...], kb[n])
                    if last:
                        encode(work, 2, n)
                        c_copy(2, n, 8 - n).start()
                    else:
                        encode(work, 0, n)
                        c_copy(0, n, 8 - n).start()
                        encode(work, 1, n)
            if not last:
                for n in ORDER:
                    @pl.when(there(9 + n))
                    def _():
                        c_copy(1, n, 8 - n).start()

        with jax.named_scope("own sum"):
            acc[...] = dot(third[...], kb[4])
        if last:
            with jax.named_scope("sent"):
                sent()
            collect(2)
            update(2)
        else:
            collect(0)
            update(0)
            keep(it + 1, 0)
            send_estimate(it + 1, everyone)
            collect(1)
            update(1)
            keep(it + 1, 1)
            around(sides, lambda m: middle_copy(m, 26 - m).start())

    with jax.named_scope("layout out"):
        flat[...] = est[...].T
        for y in range(16):
            out_ref[pl.ds(y, 16, stride=16), :] = flat[y * 16 : (y + 1) * 16, :]

    for n in ORDER:
        @pl.when(there(9 + n))
        def _():
            c_copy(2, n, 8 - n).wait_send()


def per_device(sizes, camera, initial, psf_taps):
    held = pl.BlockSpec(memory_space=pl.ANY)
    dma = pltpu.SemaphoreType.DMA
    rows = initial.reshape(256, 128)
    result = pl.pallas_call(
        functools.partial(kernel, sizes),
        out_shape=jax.ShapeDtypeStruct((256, 128), F32),
        in_specs=[held, held, held],
        out_specs=pl.BlockSpec(memory_space=pltpu.VMEM),
        scratch_shapes=[
            pltpu.VMEM((VIEWS, 32, 4, 256), BF16),
            pltpu.VMEM((256, 128), F32),
            pltpu.VMEM((VIEWS, 3, TAPS), F32),
            dma((3,)),
            pltpu.VMEM((128, 256), F32),
            pltpu.VMEM((ITERS, 192, 9 * 256), BF16),
            pltpu.VMEM((VIEWS, 256, 256), BF16),
            pltpu.VMEM((VIEWS, 160, 256), F32),
            pltpu.VMEM((VIEWS, 256, 512), BF16),
            pltpu.VMEM((VIEWS, 9 * 256, 256), BF16),
            pltpu.VMEM((9, VIEWS * 256, 256), BF16),
            pltpu.VMEM((VIEWS, 160, 256), F32),
            pltpu.VMEM((VIEWS, 128, 256), F32),
            pltpu.VMEM((24, 128), F32),
            pltpu.VMEM((24, 128), F32),
            pltpu.VMEM((48 * 8, 128), F32),
            pltpu.VMEM((2, 48 * 8, 128), F32),
            pltpu.VMEM((48 * 8, 128), F32),
            pltpu.VMEM((2, 48 * 8, 128), F32),
            pltpu.VMEM((16, 128), F32),
            pltpu.VMEM((2, 96, 1024), BF16),
            pltpu.VMEM((4, 1024, 256), BF16),
            pltpu.VMEM((16, 3, 32, 128), BF16),
            pltpu.VMEM((16, 3, 32, 128), BF16),
            pltpu.VMEM((2, 4, 3, 16, 128), BF16),
            pltpu.VMEM((VIEWS, 160, 256), BF16),
            pltpu.VMEM((128, VIEWS * 256), BF16),
            pltpu.VMEM((2, 128, 256), F32),
            pltpu.VMEM((256, 128), F32),
            pltpu.VMEM((128, 256), F32),
            pltpu.VMEM((16, 256), F32),
            *[pltpu.VMEM((9, rows, 256), BF16) for rows in (80, 64, 144) * 2],
            dma((16,)), dma((16,)),
            dma((2, 16)), dma((2, 4)),
            dma((ITERS, 27)), dma((ITERS, 27)),
            dma((9,)), dma((9,)),
            dma((3, 9)), dma((3, 9)),
            dma(()), dma(()), dma((ITERS,)), dma((ITERS,)),
        ],
        compiler_params=pltpu.CompilerParams(
            collective_id=0, has_side_effects=True, vmem_limit_bytes=55040 * 1024
        ),
    )(camera, rows, psf_taps)
    return result.reshape(initial.shape)


def solution(mesh):
    in_specs = (P(None, "gx", ("gy", "gz"), None), P("gx", "gy", "gz"), P())
    out_specs = P("gx", "gy", "gz")
    sizes = tuple(mesh.shape[a] for a in ("gx", "gy", "gz"))
    return jax.shard_map(
        functools.partial(per_device, sizes),
        mesh=mesh, in_specs=in_specs, out_specs=out_specs, check_vma=False,
    )
```

```python
import functools

import jax
import jax.numpy as jnp
from jax import lax
from jax.experimental import pallas as pl
from jax.experimental.pallas import tpu as pltpu
from jax.sharding import PartitionSpec as P

VIEWS = 6
TAPS = 31
HALF = TAPS // 2
ITERS = 2
F32 = jnp.float32
BF16 = jnp.bfloat16
MESH = pl.DeviceIdType.MESH
ORDER = (0, 2, 6, 8, 1, 3, 5, 7)


def dot(a, b):
    return jnp.dot(a, b, preferred_element_type=F32)


def iota(shape, dim):
    return lax.broadcasted_iota(jnp.int32, shape, dim)


def inside(index):
    return jnp.where((index >= 0) & (index < TAPS), index, 127)


def pick(table, index):
    return jnp.take_along_axis(table, index, axis=1)


def kernel(
    sizes, cam_hbm, init_hbm, taps_hbm, out_ref,
    cam_raw, init_ref, taps_ref, in_sem,
    est, ext, quot, inverse, ubuf, kf, kb, bzf, bzb, raw, back, xf, yf, xb, yb, scale,
    picked, place, cam_out, cam_in, rim_in, cam, third, part, flat, acc, code_out0, code_out1, code_out2, code_in0, code_in1, code_in2,
    cam_send, cam_recv, rim_send, rim_recv, e_send, e_recv, g_send, g_recv, c_send, c_recv, m_send, m_recv,
):
    code_out, code_in = (code_out0, code_out1, code_out2), (code_in0, code_in1, code_in2)
    nx, ny, nz = sizes
    gx, gy, gz = lax.axis_index("gx"), lax.axis_index("gy"), lax.axis_index("gz")
    below, above = gz > 0, gz < nz - 1

    fetch = [
        pltpu.make_async_copy(cam_hbm, cam_raw, in_sem.at[0]),
        pltpu.make_async_copy(init_hbm, init_ref, in_sem.at[1]),
        pltpu.make_async_copy(taps_hbm, taps_ref, in_sem.at[2]),
    ]
    for copy in fetch:
        copy.start()

    has_x = (gx > 0, True, gx < nx - 1)
    has_y = (gy > 0, True, gy < ny - 1)
    has_z = (below, True, above)

    def steps(m):
        return m % 9 // 3 - 1, m % 3 - 1, m // 9 - 1

    def place_of(m):
        dx, dy, dz = steps(m)
        return gx + dx, gy + dy, gz + dz

    def there(m):
        flags = [has[d + 1] for has, d in zip((has_x, has_y, has_z), steps(m)) if d]
        return functools.reduce(jnp.logical_and, flags)

    def around(ms, body):
        for m in ms:
            @pl.when(there(m))
            def _():
                body(m)

    everyone = sorted((m for m in range(27) if m != 13), key=lambda m: -sum(map(abs, steps(m))))
    rims = [m for m in everyone if m // 9 != 1]
    sides = [m for m in everyone if m // 9 == 1]

    part_z, part_i = gx >> 2, gx & 3

    def is_self(place):
        return (place[0] == gx) & (place[2] == gz)

    def source(s):
        return 4 * gz + s // 4, gy, s % 4

    def low_source(k):
        return 4 * gz - 1, gy, k

    def high_source(k):
        return 4 * gz + 4, gy, k

    def target(a):
        return a, gy, part_z

    gives_low = (part_i == 3) & (part_z == 1)
    gives_high = (part_i == 0) & (part_z == 2)
    takes_low, takes_high = gz == 2, gz == 1

    def low_target(a):
        return a, gy, part_z + 1

    def high_target(a):
        return a, gy, part_z - 1

    def others(count, place, body):
        for s in range(count):
            @pl.when(jnp.logical_not(is_self(place(s))))
            def _():
                body(s)

    barrier = pltpu.get_barrier_semaphore()

    def greet(place):
        pl.semaphore_signal(barrier, inc=1, device_id=place, device_id_type=MESH)

    others(16, source, lambda s: greet(source(s)))

    @pl.when(takes_low)
    def _():
        others(4, low_source, lambda k: greet(low_source(k)))

    @pl.when(takes_high)
    def _():
        others(4, high_source, lambda k: greet(high_source(k)))

    around(everyone, lambda m: greet(place_of(m)))

    def one(flag):
        return flag.astype(jnp.int32)

    wide = 1 + one(gx > 0) + one(gx < nx - 1)
    tall = 1 + one(gy > 0) + one(gy < ny - 1)
    deep = 1 + one(below) + one(above)
    greetings = wide * tall * deep - 1 + 16 - one(part_z == gz)
    greetings += one(gives_low) * (16 - one(part_z + 1 == gz))
    greetings += one(gives_high) * (16 - one(part_z - 1 == gz))

    with jax.named_scope("zeros"):
        for m in everyone:
            step, lanes = m // 9, slice(m % 9 * 256, m % 9 * 256 + 256)
            rows = (slice(128, 160), slice(0, 128), slice(160, 192))[step]

            for it in range(ITERS):
                @pl.when(jnp.logical_not(there(m)))
                def _():
                    ext[it, rows, lanes] = jnp.zeros((rows.stop - rows.start, 256), BF16)

        quot[:, 160:256, :] = jnp.zeros((VIEWS, 96, 256), BF16)
        place[...] = jnp.zeros(place.shape, BF16)
        raw[...] = jnp.zeros((24, 128), F32)
        ubuf[:, 192:256, :] = jnp.zeros((VIEWS, 64, 512), BF16)

    with jax.named_scope("sort camera"):
        row, col = iota((32, 256), 0), iota((32, 256), 1)
        same_x = row == (col >> 7) * 16 + (col & 15)
        for r in range(2):
            turned = ((col >> 6) & 1) == (r + gz) % 2
            for y in range(4):
                ones = (same_x & turned & (((col >> 4) & 3) == y)).astype(F32).astype(BF16)
                for q in range(4):
                    first = (r * 4 + y) * 128 + q * 32
                    place[q, first : first + 32, :] = ones
    fetch[0].wait()
    with jax.named_scope("sort camera 2"):
        for v in range(VIEWS):
            r, w = v // 3, v % 3
            for y in range(4):
                plane = cam_raw[v, :, y, :]
                lanes = slice((r * 4 + y) * 128, (r * 4 + y + 1) * 128)
                for h in range(2):
                    picked[h, w * 32 : (w + 1) * 32, lanes] = plane[:, h * 128 : (h + 1) * 128]
        for p in range(8):
            block = dot(picked[p // 4], place[p % 4]).astype(BF16)
            for w in range(3):
                cam_out[2 * p, w] = block[w * 32 : (w + 1) * 32, 0:128]
                cam_out[2 * p + 1, w] = block[w * 32 : (w + 1) * 32, 128:256]

    parts = ((0, 1, 6, 7), (2, 3, 4, 5), tuple(range(8)))

    def keep(it, part_of):
        for i, g in enumerate(parts[part_of]):
            first = part_of * 64 + i * 16
            ext[it, first : first + 16, 1024:1280] = est[g * 16 : (g + 1) * 16, :].astype(BF16)

    fetch[1].wait()
    with jax.named_scope("layout in"):
        for y in range(16):
            flat[y * 16 : (y + 1) * 16, :] = init_ref[pl.ds(y, 16, stride=16), :]
        est[...] = flat[...].T
        for part_of in range(2):
            keep(0, part_of)

    with jax.named_scope("entry wait"):
        pl.semaphore_wait(barrier, greetings)

    slot = part_i * 4 + gz

    def cam_copy(a, s):
        return pltpu.make_async_remote_copy(
            src_ref=cam_out.at[a],
            dst_ref=cam_in.at[s],
            send_sem=cam_send.at[a],
            recv_sem=cam_recv.at[s],
            device_id=target(a),
            device_id_type=MESH,
        )

    def rim_copy(high, a, k):
        first = 0 if high else 16
        return pltpu.make_async_remote_copy(
            src_ref=cam_out.at[a, :, pl.ds(first, 16), :],
            dst_ref=rim_in.at[int(high), k],
            send_sem=rim_send.at[int(high), a],
            recv_sem=rim_recv.at[int(high), k],
            device_id=high_target(a) if high else low_target(a),
            device_id_type=MESH,
        )

    def e_copy(it, m, at):
        first, count, to = ((0, 32, 160), (0, 64 if it else 128, 0), (32, 32, 128))[m // 9]
        return pltpu.make_async_remote_copy(
            src_ref=ext.at[it, pl.ds(first, count), pl.ds(1024, 256)],
            dst_ref=ext.at[it, pl.ds(to, count), pl.ds(at % 9 * 256, 256)],
            send_sem=e_send.at[it, m],
            recv_sem=e_recv.at[it, at],
            device_id=place_of(m),
            device_id_type=MESH,
        )

    def middle_copy(m, at):
        return pltpu.make_async_remote_copy(
            src_ref=ext.at[1, pl.ds(64, 64), pl.ds(1024, 256)],
            dst_ref=ext.at[1, pl.ds(64, 64), pl.ds(at % 9 * 256, 256)],
            send_sem=g_send.at[m - 9],
            recv_sem=g_recv.at[at - 9],
            device_id=place_of(m),
            device_id_type=MESH,
        )

    def send_estimate(it, ms):
        around(ms, lambda m: e_copy(it, m, 26 - m).start())

    def wait_estimate(it, ms):
        around(ms, lambda m: e_copy(it, m, m).wait_recv())

    with jax.named_scope("send estimate"):
        send_estimate(0, everyone)

    with jax.named_scope("send camera"):
        @pl.when(part_z == gz)
        def _():
            cam_in[slot] = cam_out[gx]

        others(16, target, lambda a: cam_copy(a, slot).start())

        @pl.when(gives_low)
        def _():
            @pl.when(part_z + 1 == gz)
            def _():
                rim_in[0, gz] = cam_out[gx, :, 16:32, :]

            others(16, low_target, lambda a: rim_copy(False, a, gz).start())

        @pl.when(gives_high)
        def _():
            @pl.when(part_z - 1 == gz)
            def _():
                rim_in[1, gz] = cam_out[gx, :, 0:16, :]

            others(16, high_target, lambda a: rim_copy(True, a, gz).start())

    fetch[2].wait()
    with jax.named_scope("taps"):
        for v in range(VIEWS):
            for a in range(3):
                raw[a * 8 + v : a * 8 + v + 1, 0:TAPS] = taps_ref[v, a : a + 1, :]
        total = jnp.sum(raw[...], axis=1, keepdims=True)
        total = jnp.where((iota((24, 1), 0) & 7) < VIEWS, total, 1.0)
        back[...] = (raw[...] / total).astype(BF16).astype(F32)

    with jax.named_scope("tables"):
        def tables(i, carry):
            lane = iota((8, 128), 1)
            for k in range(6):
                j = i * 6 + k
                rows = pl.ds(pl.multiple_of(j * 8, 8), 8)
                x = lane & 15
                xf[rows, :] = pick(raw[0:8, :], inside(x + 31 - j))
                xb[rows, :] = pick(back[0:8, :], inside(j - 1 - x))
                for half in range(2):
                    y = (lane >> 4) + 8 * half
                    yf[half, rows, :] = pick(raw[8:16, :], inside(y + 31 - j))
                    yb[half, rows, :] = pick(back[8:16, :], inside(j - 1 - y))
            return carry

        lax.fori_loop(0, 8, tables, 0)

    def rows_of(table, j, v):
        return table[pl.ds(j * 128 + v, 16, stride=8), :]

    with jax.named_scope("products"):
        def products(i, carry):
            v, n = i // 9, i % 9
            dx, dy = n // 3, n % 3
            x = rows_of(xf, dx, v)
            for half in range(2):
                ys = rows_of(yf.at[half], dy, v)
                for y in range(16):
                    kf[v, pl.ds(pl.multiple_of(n * 256 + y * 16, 16), 16), half * 128 : (half + 1) * 128] = (
                        x * ys[y : y + 1, :]
                    ).astype(BF16)
            return carry

        lax.fori_loop(0, 9 * VIEWS, products, 0)

    with jax.named_scope("bands"):
        def bands(block, carry):
            r = iota((8, 128), 0) + block * 8
            z_out = jnp.where(r < 128, r, jnp.where(r < 144, r - 144, r - 16))
            rows = pl.ds(pl.multiple_of(block * 8, 8), 8)
            lane = iota((8, 128), 1)
            near = jnp.where(lane < 32, lane, jnp.where(lane < 64, lane + 64, lane - 32))
            far = jnp.where(lane < 32, lane - 32, jnp.where(lane < 64, lane + 96, 4096))
            for half, z_in in enumerate((near, far)):
                index = inside(z_out - z_in + HALF)
                for v in range(VIEWS):
                    band_f = jnp.broadcast_to(raw[16 + v : 17 + v, :], (8, 128))
                    bzf[v, rows, half * 128 : (half + 1) * 128] = pick(band_f, index)
            return carry

        lax.fori_loop(0, 20, bands, 0)

        def back_bands(block, carry):
            z_out = iota((8, 128), 0) + block * 8
            rows = pl.ds(pl.multiple_of(block * 8, 8), 8)
            lane = iota((8, 128), 1)
            far = jnp.where(lane < 16, lane - 16, jnp.where(lane < 32, lane + 112, 1024))
            for half, z_in in enumerate((lane, far)):
                index = inside(z_in - z_out + HALF)
                for v in range(VIEWS):
                    band_b = jnp.broadcast_to(back[16 + v : 17 + v, :], (8, 128))
                    bzb[v, rows, half * 128 : (half + 1) * 128] = pick(band_b, index)
            return carry

        lax.fori_loop(0, 16, back_bands, 0)

    with jax.named_scope("scale"):
        fx, fy, fz = raw[0:8, :], raw[8:16, :], raw[16:24, :]
        bx, by = back[0:8, :], back[8:16, :]
        f_sum, b_sum = jnp.zeros((8, 128), F32), jnp.zeros((8, 128), F32)
        for t in range(TAPS):
            f_sum += (fx[:, t : t + 1] * fy).astype(BF16).astype(F32)
            b_sum += (bx[:, t : t + 1] * by).astype(BF16).astype(F32)

        def lanes_sum(a):
            return jnp.sum(a, axis=1, keepdims=True)

        f_scale = lanes_sum(f_sum) * lanes_sum(fz.astype(BF16).astype(F32))
        b_total = jnp.where(iota((8, 1), 0) < VIEWS, lanes_sum(b_sum), 1.0)
        b_scale = lanes_sum(bx) * lanes_sum(by) / b_total
        scale[0:8, :] = jnp.broadcast_to(f_scale, (8, 128))
        scale[8:16, :] = jnp.broadcast_to(b_scale, (8, 128))

    with jax.named_scope("back products"):
        def back_products(i, carry):
            v, n = i // 9, i % 9
            dx, dy = n // 3, n % 3
            x = rows_of(xb, 2 - dx, v)
            for half in range(2):
                ys = rows_of(yb.at[half], 2 - dy, v)
                for y in range(16):
                    kb[n, pl.ds(pl.multiple_of(v * 256 + y * 16, 16), 16), half * 128 : (half + 1) * 128] = (
                        x * ys[y : y + 1, :]
                    ).astype(BF16)
            return carry

        lax.fori_loop(0, 9 * VIEWS, back_products, 0)

    def factor(row):
        value = scale[row : row + 1, :]
        return jnp.concatenate([value, value], axis=1)

    def spread(it, first, last):
        for v in range(VIEWS):
            u = dot(ext[it, first:last, :], kf[v])
            high = u.astype(BF16)
            ubuf[v, first:last, 0:256] = high
            ubuf[v, first:last, 256:512] = (u - high.astype(F32)).astype(BF16)

    def blur(it):
        for v in range(VIEWS):
            halves = dot(bzf[v].astype(BF16), ubuf[v])
            inverse[v] = factor(v) / (halves[:, 0:256] + halves[:, 256:512])

    def quotients():
        row = iota((32, 256), 0)
        seen = jnp.where(row < 16, one(below), one(above)) > 0
        for v in range(VIEWS):
            quot[v, 0:128, :] = (cam[v, 0:128, :].astype(F32) * inverse[v, 0:128, :]).astype(BF16)
            rim = jnp.where(seen, cam[v, 128:160, :].astype(F32) * inverse[v, 128:160, :], 0.0)
            quot[v, 128:160, :] = rim.astype(BF16)

    with jax.named_scope("wait estimate"):
        wait_estimate(0, everyone)
    with jax.named_scope("blur"):
        spread(0, 0, 192)
        blur(0)

    def mate_copy(first, to):
        return pltpu.make_async_remote_copy(
            src_ref=cam.at[:, pl.ds(first, 16), :],
            dst_ref=cam.at[:, pl.ds(to, 16), :],
            send_sem=m_send,
            recv_sem=m_recv,
            device_id=(gx, gy, gz ^ 1),
            device_id_type=MESH,
        )

    def pair(r, even, odd):
        low = iota(even.shape, 1) < 64
        even, odd = even.astype(F32), odd.astype(F32)
        if r == 0:
            return jnp.where(low, even, odd).astype(BF16)
        return pltpu.roll(jnp.where(low, odd, even), 64, 1).astype(BF16)

    def assemble(z):
        for k in range(4):
            @pl.when(jnp.logical_not(is_self(source(4 * z + k))))
            def _():
                cam_copy(0, 4 * z + k).wait_recv()
        for v in range(VIEWS):
            r, w = v // 3, v % 3
            for t in range(2):
                cam[v, z * 32 : (z + 1) * 32, t * 128 : (t + 1) * 128] = pair(
                    r, cam_in[z * 4 + 2 * t, w], cam_in[z * 4 + 2 * t + 1, w]
                )

    def assemble_rim(high):
        place = high_source if high else low_source
        others(4, place, lambda k: rim_copy(high, 0, k).wait_recv())
        for v in range(VIEWS):
            r, w = v // 3, v % 3
            for t in range(2):
                cam[v, 128 + high * 16 : 144 + high * 16, t * 128 : (t + 1) * 128] = pair(
                    r, rim_in[high, 2 * t, w], rim_in[high, 2 * t + 1, w]
                )

    even = (gz & 1) == 0
    with jax.named_scope("camera in"):
        @pl.when(even)
        def _():
            assemble(3)
            mate_copy(112, 128).start()
            assemble(0)

        @pl.when(jnp.logical_not(even))
        def _():
            assemble(0)
            mate_copy(0, 144).start()
            assemble(3)

        assemble(1)
        assemble(2)

        @pl.when(takes_low)
        def _():
            assemble_rim(0)

        @pl.when(takes_high)
        def _():
            assemble_rim(1)

        @pl.when(even)
        def _():
            mate_copy(0, 144).wait_recv()

        @pl.when(jnp.logical_not(even))
        def _():
            mate_copy(112, 128).wait_recv()

    def c_copy(part_of, n, at):
        return pltpu.make_async_remote_copy(
            src_ref=code_out[part_of].at[n],
            dst_ref=code_in[part_of].at[at],
            send_sem=c_send.at[part_of, n],
            recv_sem=c_recv.at[part_of, at],
            device_id=place_of(9 + n),
            device_id_type=MESH,
        )

    def encode(work, part_of, n):
        groups, out = parts[part_of], code_out[part_of]
        base = [work[g * 16 + 8 : g * 16 + 9, :] for g in groups]
        base = jnp.concatenate(base + [jnp.zeros((16 - len(groups), 256), F32)], axis=0).astype(BF16)
        out[n, len(groups) * 16 : len(groups) * 16 + 16, :] = base
        base = base.astype(F32)
        for i, g in enumerate(groups):
            out[n, i * 16 : (i + 1) * 16, :] = (work[g * 16 : (g + 1) * 16, :] - base[i : i + 1, :]).astype(BF16)

    def collect(part_of):
        groups, code = parts[part_of], code_in[part_of]
        for n in reversed(ORDER):
            @pl.when(there(9 + n))
            def _():
                c_copy(part_of, n, n).wait_recv()
                with jax.named_scope("add"):
                    base = code[n, len(groups) * 16 : len(groups) * 16 + 16, :].astype(F32)
                    for i, g in enumerate(groups):
                        rows = slice(g * 16, (g + 1) * 16)
                        acc[rows, :] += code[n, i * 16 : (i + 1) * 16, :].astype(F32) + base[i : i + 1, :]

    def update(part_of):
        for g in parts[part_of]:
            rows = slice(g * 16, (g + 1) * 16)
            est[rows, :] = est[rows, :] * acc[rows, :] / VIEWS

    def sent():
        around(everyone, lambda m: e_copy(0, m, 26 - m).wait_send())
        for it in range(1, ITERS):
            around(everyone, lambda m: e_copy(it, m, 26 - m).wait_send())
            around(sides, lambda m: middle_copy(m, 26 - m).wait_send())
        for part_of in range(2):
            around(sides, lambda m: c_copy(part_of, m - 9, 17 - m).wait_send())

        @pl.when(even)
        def _():
            mate_copy(112, 128).wait_send()

        @pl.when(jnp.logical_not(even))
        def _():
            mate_copy(0, 144).wait_send()
        others(16, target, lambda a: cam_copy(a, slot).wait_send())

        @pl.when(gives_low)
        def _():
            others(16, low_target, lambda a: rim_copy(False, a, gz).wait_send())

        @pl.when(gives_high)
        def _():
            others(16, high_target, lambda a: rim_copy(True, a, gz).wait_send())

    for it in range(ITERS):
        if it > 0:
            with jax.named_scope("wait estimate 2"):
                wait_estimate(it, sides)
                around(sides, lambda m: middle_copy(m, m).wait_recv())
                spread(it, 0, 128)
                wait_estimate(it, rims)
                spread(it, 128, 192)
            with jax.named_scope("blur 2"):
                blur(it)
        with jax.named_scope("quotients"):
            quotients()
        with jax.named_scope("third"):
            for v in range(VIEWS):
                value = dot(bzb[v].astype(BF16), quot[v]) * factor(8 + v)
                third[:, v * 256 : (v + 1) * 256] = value.astype(BF16)

        last = it == ITERS - 1
        with jax.named_scope("partial sums"):
            for count, n in enumerate(ORDER):
                @pl.when(there(9 + n))
                def _():
                    work = part.at[count % 2]
                    work[...] = dot(third[...], kb[n])
                    if last:
                        encode(work, 2, n)
                        c_copy(2, n, 8 - n).start()
                    else:
                        encode(work, 0, n)
                        c_copy(0, n, 8 - n).start()
                        encode(work, 1, n)
            if not last:
                for n in ORDER:
                    @pl.when(there(9 + n))
                    def _():
                        c_copy(1, n, 8 - n).start()

        with jax.named_scope("own sum"):
            acc[...] = dot(third[...], kb[4])
        if last:
            with jax.named_scope("sent"):
                sent()
            collect(2)
            update(2)
        else:
            collect(0)
            update(0)
            keep(it + 1, 0)
            send_estimate(it + 1, everyone)
            collect(1)
            update(1)
            keep(it + 1, 1)
            around(sides, lambda m: middle_copy(m, 26 - m).start())

    with jax.named_scope("layout out"):
        flat[...] = est[...].T
        for y in range(16):
            out_ref[pl.ds(y, 16, stride=16), :] = flat[y * 16 : (y + 1) * 16, :]

    for n in ORDER:
        @pl.when(there(9 + n))
        def _():
            c_copy(2, n, 8 - n).wait_send()


def per_device(sizes, camera, initial, psf_taps):
    held = pl.BlockSpec(memory_space=pl.ANY)
    dma = pltpu.SemaphoreType.DMA
    rows = initial.reshape(256, 128)
    result = pl.pallas_call(
        functools.partial(kernel, sizes),
        out_shape=jax.ShapeDtypeStruct((256, 128), F32),
        in_specs=[held, held, held],
        out_specs=pl.BlockSpec(memory_space=pltpu.VMEM),
        scratch_shapes=[
            pltpu.VMEM((VIEWS, 32, 4, 256), BF16),
            pltpu.VMEM((256, 128), F32),
            pltpu.VMEM((VIEWS, 3, TAPS), F32),
            dma((3,)),
            pltpu.VMEM((128, 256), F32),
            pltpu.VMEM((ITERS, 192, 9 * 256), BF16),
            pltpu.VMEM((VIEWS, 256, 256), BF16),
            pltpu.VMEM((VIEWS, 160, 256), F32),
            pltpu.VMEM((VIEWS, 256, 512), BF16),
            pltpu.VMEM((VIEWS, 9 * 256, 256), BF16),
            pltpu.VMEM((9, VIEWS * 256, 256), BF16),
            pltpu.VMEM((VIEWS, 160, 256), F32),
            pltpu.VMEM((VIEWS, 128, 256), F32),
            pltpu.VMEM((24, 128), F32),
            pltpu.VMEM((24, 128), F32),
            pltpu.VMEM((48 * 8, 128), F32),
            pltpu.VMEM((2, 48 * 8, 128), F32),
            pltpu.VMEM((48 * 8, 128), F32),
            pltpu.VMEM((2, 48 * 8, 128), F32),
            pltpu.VMEM((16, 128), F32),
            pltpu.VMEM((2, 96, 1024), BF16),
            pltpu.VMEM((4, 1024, 256), BF16),
            pltpu.VMEM((16, 3, 32, 128), BF16),
            pltpu.VMEM((16, 3, 32, 128), BF16),
            pltpu.VMEM((2, 4, 3, 16, 128), BF16),
            pltpu.VMEM((VIEWS, 160, 256), BF16),
            pltpu.VMEM((128, VIEWS * 256), BF16),
            pltpu.VMEM((2, 128, 256), F32),
            pltpu.VMEM((256, 128), F32),
            pltpu.VMEM((128, 256), F32),
            *[pltpu.VMEM((9, rows, 256), BF16) for rows in (80, 80, 144) * 2],
            dma((16,)), dma((16,)),
            dma((2, 16)), dma((2, 4)),
            dma((ITERS, 27)), dma((ITERS, 27)),
            dma((9,)), dma((9,)),
            dma((3, 9)), dma((3, 9)),
            dma(()), dma(()),
        ],
        compiler_params=pltpu.CompilerParams(
            collective_id=0, has_side_effects=True, vmem_limit_bytes=55040 * 1024
        ),
    )(camera, rows, psf_taps)
    return result.reshape(initial.shape)


def solution(mesh):
    in_specs = (P(None, "gx", ("gy", "gz"), None), P("gx", "gy", "gz"), P())
    out_specs = P("gx", "gy", "gz")
    sizes = tuple(mesh.shape[a] for a in ("gx", "gy", "gz"))
    return jax.shard_map(
        functools.partial(per_device, sizes),
        mesh=mesh, in_specs=in_specs, out_specs=out_specs, check_vma=False,
    )
```
